32 devices in a mesh: comp: 2 (over core), gx: 4 (over z), gy: 4 (over y, x).
Axes of the slice: x: 2, y: 2, z: 4, core: 2. Of those that a mesh axis runs over, the one named last changes fastest.
Arguments:
- atmos_state: float32 [10, 20, 128, 512], P(None, None, ('comp', 'gx'), 'gy'), may hold values from -6 to 6
- atmos_diffusion: float32 [10], replicated, may hold values from 0.03 to 0.12
- remap_atmos: float32 [512, 128, 128], P(('comp', 'gx', 'gy')), may hold values from -0.1237436867076458 to 1.5237436867076457
- exchange_owner: int32 [512, 1], P(('comp', 'gx', 'gy')), may hold values from 0 to 15; in each aligned block of 16 rows (0 to 15, 16 to 31, ...) at most 2 rows name the same one
- exchange_slot: int32 [512], P(('comp', 'gx', 'gy')), may hold values from 0 to 15
- remap_ocean: float32 [512, 128, 128], P(('comp', 'gx', 'gy')), may hold values from -0.1237436867076458 to 1.5237436867076457
- ocean_owner: int32 [512, 1], P(('comp', 'gx', 'gy')), may hold values from 0 to 15; in each aligned block of 16 rows (0 to 15, 16 to 31, ...) at most 2 rows name the same one
- ocean_slot: int32 [512], P(('comp', 'gx', 'gy')), may hold values from 0 to 63
- ocean_state: float32 [4, 8, 256, 512], P(None, None, 'gx', 'gy'), may hold values from -6 to 6
- ocean_mixing: float32 [4], replicated, may hold values from 0.03 to 0.12
- wet_mask: int32 [256, 512], P('gx', 'gy'), may hold values 0 or 1
Outputs:
- atmos_next: float32 [10, 20, 128, 512], P(None, None, ('comp', 'gx'), 'gy')
- ocean_next: float32 [4, 8, 256, 512], P(None, None, 'gx', 'gy')
- ocean_surface: float32 [4, 128, 512], P(None, ('comp', 'gx'), 'gy')
The draws below stay inside these ranges and needn't reach their ends.
Inputs may be any that keep to these rules, and one draw needn't show every extreme that they name: `exchange_owner`: among the rows of one device, no owner appears more than 2 times, and one appears exactly 2 times. `ocean_owner`: among the rows of one device, no owner appears more than 2 times, and one appears exactly 2 times.
All inputs are finite; a program needn't handle non-finite values. No bound on the sum of `wet_mask` on one device may be relied on, other than what follows from the above.
Results may differ from the reference program's by a relative error of at most 0.000088.
Values sent between devices are 32-bit elements; how exact they have to be, the bound alone decides.
No kernel may reach another device: no remote copies, remote signals or barrier semaphores. Data moves between devices by JAX's collectives and lax.ppermute only.
A program may use at most 128 MiB of HBM per device.

```python
import math
import jax
import jax.numpy as jnp
import numpy as np
from jax import lax

NF = 10
NO = 4
LEV = 20
OLEV = 8
TILE = 128
AX_DEV = 16
OX_DEV = 64
CAP = 2
NAX = 128
NAY = 512
NOX = 256
NOY = 512
NA_TILES = 512
NO_TILES = 1024
N_GX = 4
N_GY = 4


def remap_tiles(key, count):
    diagonal_key, spread_key = jax.random.split(key)
    diagonal = jax.random.uniform(diagonal_key, (count, TILE), jnp.float32, 0.6, 1.4)
    spread = jax.random.truncated_normal(spread_key, -4.0, 4.0, (count, TILE, TILE), jnp.float32) * (0.35 / math.sqrt(TILE))
    return spread + diagonal[:, :, None] * jnp.eye(TILE, dtype=jnp.float32)[None]


def draw_remap_atmos(key, part):
    return remap_tiles(jax.random.fold_in(key, 11), NA_TILES)


def draw_remap_ocean(key, part):
    return remap_tiles(jax.random.fold_in(key, 23), NA_TILES)


def plant(drawn, stream_key, least, high):
    longest = drawn.shape.index(max(drawn.shape))
    spots = []
    for shift in (0, 1):
        where = [jax.random.randint(jax.random.fold_in(stream_key, axis), (), 0, length) for axis, length in enumerate(drawn.shape)]
        where[longest] = (where[longest] + shift) % drawn.shape[longest]
        spots.append(tuple(where))
    return drawn.at[spots[0]].set(least).at[spots[1]].set(high)


def block_levels(rng, shape, cuts, low, largest):
    level, own = 1.0, jax.random.fold_in(rng, 6)
    for axis_at, parts in cuts:
        steps = jnp.exp(jax.random.uniform(jax.random.fold_in(own, axis_at), (parts,), jnp.float32, low / len(cuts), largest / len(cuts)))
        level = level * jnp.repeat(steps, shape[axis_at] // parts).reshape([-1 if axis == axis_at else 1 for axis in range(len(shape))])
    return level


def deal_out(stream_key, own, number, rows, number_of, top, most, skew):
    ranking = jax.random.permutation(stream_key, number_of)
    crowded, ordinary = shares(number_of, rows * top, most, skew, True), shares(number_of, rows * top, most, skew, False)
    places = jnp.arange(number_of)

    def named(tallies, offset_by):
        used = int((tallies > 0).sum())
        fixed = max(1, used // 4)
        shifted = fixed + (places - fixed + offset_by * (used - fixed)) % max(1, number_of - fixed)
        return jnp.zeros((number_of,), jnp.int32).at[ranking[jnp.where(places < fixed, places, shifted)]].set(jnp.asarray(tallies, jnp.int32))

    tallies = jnp.where(number % 4 == 0, named(crowded, number // 4), named(ordinary, number - number // 4 - 1))
    mixed = jax.random.permutation(jax.random.fold_in(own, 3), number_of)
    giver, taker = mixed[0:number_of // 2 * 2:2], mixed[1:number_of // 2 * 2:2]
    slack = jnp.minimum(tallies[giver] - 1, most - tallies[taker]) // 2
    slack = jnp.where((giver == ranking[0]) | (taker == ranking[0]) | (tallies[taker] == 0), 0, jnp.maximum(slack, 0))
    shifted = jax.random.randint(jax.random.fold_in(own, 4), (number_of // 2,), 0, 1 << 20) % (slack + 1)
    tallies = tallies.at[giver].add(-shifted).at[taker].add(shifted)
    members = jnp.searchsorted(jnp.cumsum(tallies), jnp.arange(rows * top), side="right").astype(jnp.int32)
    table = members.reshape(top, rows).T
    table = table[jax.random.permutation(jax.random.fold_in(own, 1), rows)]
    offset_by = jax.random.randint(jax.random.fold_in(own, 2), (rows, 1), 0, top)
    return jnp.take_along_axis(table, (jnp.arange(top)[None, :] + offset_by) % top, axis=1)


def shares(amount, total, limit, lean, full):
    portions = [(1 << 20) // math.isqrt(standing ** lean) + 1 for standing in range(1, amount + 1)]
    largest = limit if full else min(limit, max(-(-total // amount), total * portions[0] // sum(portions)))
    least = 1 if total - largest >= amount - 1 else 0
    holding, rest = [largest] + [least] * (amount - 1), total - largest - least * (amount - 1)
    while rest > 0:
        candidates = [i for i in range(1, amount) if holding[i] < largest] or [i for i in range(1, amount) if holding[i] < limit]
        whole, left = sum([portions[i] for i in candidates]), rest
        for i in candidates:
            addition = min(limit - holding[i], max(1, left * portions[i] // whole), rest)
            holding[i] = holding[i] + addition
            rest = rest - addition
    return np.array(holding)


def centred(own_key, extent, deviation, reach, cuts=(), held_as=jnp.bfloat16):
    values = deviation * jax.random.normal(own_key, extent, jnp.float32)
    if cuts:
        values = values * block_levels(own_key, extent, cuts, -0.22, 0.18)
    return jnp.clip(values, -reach, reach).astype(held_as)


def setup_inputs(seed: int = 0) -> dict:
    seeds = jax.random.split(jax.random.key(seed), 12)
    atmos_state = centred(seeds[0], (NF, LEV, NAX, NAY), 1.0, 6.0, ((2, 8), (3, 4)), jnp.float32)
    atmos_diffusion = jnp.clip(jnp.exp(jax.random.uniform(seeds[1], (NF,), jnp.float32, math.log(0.03), math.log(0.12))), 0.03, 0.12)
    remap_atmos = draw_remap_atmos(jax.random.fold_in(seeds[11], 71), 0)
    exchange_owner_keys = jax.random.split(jax.random.fold_in(seeds[3], 1), NA_TILES // AX_DEV)
    exchange_owner_turns = jax.random.permutation(jax.random.fold_in(seeds[3], 3), NA_TILES // AX_DEV)
    exchange_owner = jax.vmap(lambda own, number: deal_out(jax.random.fold_in(seeds[3], 2), own, number, AX_DEV, N_GX * N_GY, 1, CAP, 2))(exchange_owner_keys, exchange_owner_turns).reshape((NA_TILES, 1))
    exchange_slot = plant(jax.random.randint(seeds[4], (NA_TILES,), 0, AX_DEV), jax.random.fold_in(seeds[4], 1), 0, AX_DEV - 1).astype(jnp.int32)
    remap_ocean = draw_remap_ocean(jax.random.fold_in(seeds[11], 71), 0)
    ocean_owner_keys = jax.random.split(jax.random.fold_in(seeds[6], 1), NA_TILES // AX_DEV)
    ocean_owner_turns = jax.random.permutation(jax.random.fold_in(seeds[6], 3), NA_TILES // AX_DEV)
    ocean_owner = jax.vmap(lambda own, number: deal_out(jax.random.fold_in(seeds[6], 2), own, number, AX_DEV, N_GX * N_GY, 1, CAP, 2))(ocean_owner_keys, ocean_owner_turns).reshape((NA_TILES, 1))
    ocean_slot = plant(jax.random.randint(seeds[7], (NA_TILES,), 0, OX_DEV), jax.random.fold_in(seeds[7], 1), 0, OX_DEV - 1).astype(jnp.int32)
    ocean_state = centred(seeds[8], (NO, OLEV, NOX, NOY), 1.0, 6.0, ((2, 4), (3, 4)), jnp.float32)
    ocean_mixing = jnp.clip(jnp.exp(jax.random.uniform(seeds[9], (NO,), jnp.float32, math.log(0.03), math.log(0.12))), 0.03, 0.12)
    wet_mask = plant((jax.random.randint(seeds[10], (NOX, NOY), 0, 4) < 3).astype(jnp.int32), jax.random.fold_in(seeds[10], 1), 0, 1)
    return dict(atmos_state=atmos_state, atmos_diffusion=atmos_diffusion, remap_atmos=remap_atmos, exchange_owner=exchange_owner, exchange_slot=exchange_slot, remap_ocean=remap_ocean, ocean_owner=ocean_owner, ocean_slot=ocean_slot, ocean_state=ocean_state, ocean_mixing=ocean_mixing, wet_mask=wet_mask)


HIGHEST = lax.Precision.HIGHEST
FORCING_SCALE = (0.1, -0.1, 0.1, 0.1)

def vertical_mix(state):
    upper = jnp.concatenate([state[:, :1], state[:, :-1]], axis=1)
    lower = jnp.concatenate([state[:, 1:], state[:, -1:]], axis=1)
    return upper + lower - 2.0 * state

def atmos_step(state, diffusion):
    beside = jnp.roll(state, 1, 2) + jnp.roll(state, -1, 2) + jnp.roll(state, 1, 3) + jnp.roll(state, -1, 3) - 4.0 * state
    return state + diffusion[:, None, None, None] * beside + 0.1 * vertical_mix(state)

def ocean_step(state, wet_cells, forcing, mixing):
    total = jnp.zeros_like(state)
    for axis_number, offset in ((2, 1), (2, -1), (3, 1), (3, -1)):
        nearby = jnp.roll(state, offset, axis_number)
        nearby_wet = jnp.roll(wet_cells, offset, axis_number - 2)
        total = total + nearby_wet * (nearby - state)
    tendency = mixing[:, None, None, None] * wet_cells * total + 0.1 * vertical_mix(state)
    scales = jnp.array(FORCING_SCALE, dtype=jnp.float32)
    top_level = tendency[:, :1] + scales[:, None, None, None] * forcing[:, None]
    tendency = jnp.concatenate([top_level, tendency[:, 1:]], axis=1)
    return state + wet_cells * tendency

def grid_to_tiles(grid, rows_each):
    channels, grid_rows, grid_cols = grid.shape
    blocks = grid.reshape(channels, grid_rows // rows_each, rows_each, grid_cols // TILE, TILE)
    return blocks.transpose(1, 3, 2, 0, 4).reshape(-1, channels, TILE)

def tiles_to_grid(tiles, rows_each, grid_rows, grid_cols):
    channels = tiles.shape[1]
    blocks = tiles.reshape(grid_rows // rows_each, grid_cols // TILE, rows_each, channels, TILE)
    return blocks.transpose(3, 0, 2, 1, 4).reshape(channels, grid_rows, grid_cols)

def surface_fluxes(fields):
    speed = jnp.sqrt(fields[:, 2] * fields[:, 2] + fields[:, 3] * fields[:, 3] + 0.5)
    heat_flux = speed * (fields[:, 0] - fields[:, 4]) + fields[:, 6] + fields[:, 7]
    fresh_flux = speed * fields[:, 1] + fields[:, 5] + fields[:, 8]
    east_stress = speed * fields[:, 2] * (1.0 + 0.2 * jnp.tanh(fields[:, 9]))
    north_stress = speed * fields[:, 3]
    return jnp.stack([heat_flux, fresh_flux, east_stress, north_stress], axis=1)

def reference(atmos_state, atmos_diffusion, remap_atmos, exchange_owner, exchange_slot, remap_ocean, ocean_owner, ocean_slot, ocean_state, ocean_mixing, wet_mask):
    after_first = atmos_step(atmos_state, atmos_diffusion)
    atmos_next = atmos_step(after_first, atmos_diffusion)
    surface_tiles = grid_to_tiles(after_first[:, LEV - 1], AX_DEV)
    pieces = jnp.einsum('tfc,tcd->tfd', surface_tiles, remap_atmos, precision=HIGHEST)
    section = jnp.arange(NA_TILES, dtype=jnp.int32) // (AX_DEV * N_GX * N_GY)
    exchange_index = ((section * (N_GX * N_GY) + exchange_owner[:, 0]) * AX_DEV + exchange_slot).astype(jnp.int32)
    exchange_fields = jax.ops.segment_sum(pieces, exchange_index, num_segments=NA_TILES)
    fluxes = surface_fluxes(exchange_fields)
    mapped = jnp.einsum('jgc,jcd->jgd', fluxes, remap_ocean, precision=HIGHEST)
    ocean_index = (ocean_owner[:, 0] * OX_DEV + ocean_slot).astype(jnp.int32)
    forcing_tiles = jax.ops.segment_sum(mapped, ocean_index, num_segments=NO_TILES)
    forcing = tiles_to_grid(forcing_tiles, OX_DEV, NOX, NOY)
    wet_cells = wet_mask.astype(jnp.float32)
    ocean_next = ocean_step(ocean_state, wet_cells, forcing, ocean_mixing)
    ocean_top = grid_to_tiles(ocean_next[:, 0], OX_DEV)
    on_exchange = jnp.einsum('jgc,jdc->jgd', ocean_top[ocean_index], remap_ocean, precision=HIGHEST)
    on_atmos = jnp.einsum('tgc,tdc->tgd', on_exchange[exchange_index], remap_atmos, precision=HIGHEST)
    ocean_surface = tiles_to_grid(on_atmos, AX_DEV, NAX, NAY)
    return (atmos_next, ocean_next, ocean_surface)
```

```python
import functools

import jax
import jax.numpy as jnp
from jax import lax
from jax.experimental import pallas as pl
from jax.experimental.pallas import tpu as pltpu
from jax.sharding import PartitionSpec as P

F32 = jnp.float32
BF16 = jnp.bfloat16
FORCING_SCALE = (0.1, -0.1, 0.1, 0.1)
SECTION = ("gx", "gy")
EVERY = ("comp", "gx", "gy")
CAPACITY = 2
PIECE_ROWS = 12
FLUX_ROWS = 16
VMEM_LIMIT = 40 * 1024 * 1024


def shifted(block, axis, distance):
    devices = range(lax.axis_size(axis))
    route = [((i - distance) % len(devices), i) for i in devices]
    return lax.ppermute(block, axis, route)


def dot(left, right, transposed=False):
    dims = (((1,), (1 if transposed else 0,)), ((), ()))
    return lax.dot_general(left, right, dims, preferred_element_type=F32)


def halves(values):
    high = values.astype(BF16)
    return high, (values - high.astype(F32)).astype(BF16)


def remapped(rows, block, transposed=False):
    rows_high, rows_low = halves(rows)
    block_high, block_low = halves(block)
    return (
        dot(rows_high, block_high, transposed)
        + dot(rows_low, block_high, transposed)
        + dot(rows_high, block_low, transposed)
    )


def picked(selection, values):
    chosen = selection.astype(BF16)
    high = values.astype(BF16)
    rest = values - high.astype(F32)
    middle = rest.astype(BF16)
    low = (rest - middle.astype(F32)).astype(BF16)
    return dot(chosen, high) + dot(chosen, middle) + dot(chosen, low)


def one_hot(labels):
    lanes = lax.broadcasted_iota(jnp.int32, labels.shape, 1).astype(F32)
    return (labels == lanes).astype(F32)


def grid_index(shape):
    return lax.broadcasted_iota(jnp.int32, shape, 0), lax.broadcasted_iota(jnp.int32, shape, 1)


def around(cells, north, south, west, east):
    rows, lanes = grid_index(cells.shape)
    row_count, width = cells.shape
    return (
        jnp.where(rows == 0, north, pltpu.roll(cells, 1, 0)),
        jnp.where(rows == row_count - 1, south, pltpu.roll(cells, row_count - 1, 0)),
        jnp.where(lanes == 0, west, pltpu.roll(cells, 1, 1)),
        jnp.where(lanes == width - 1, east, pltpu.roll(cells, width - 1, 1)),
    )


def diffused(cells, upper, lower, sides, diffusion):
    beside = sides[0] + sides[1] + sides[2] + sides[3] - 4.0 * cells
    return cells + diffusion * beside + 0.1 * (upper + lower - 2.0 * cells)


def edges_kernel(sizes, state, ocean, wet, first_rows, last_rows, first_cols, last_cols):
    fields, levels, rows, ocean_blocks, sea_rows = sizes
    blocks = fields * levels
    wet_row = blocks + ocean_blocks
    half = fields // 2
    tail = first_rows.shape[0] - wet_row
    width = state.shape[1]
    for out, at, sea_at in ((first_rows, 0, 0), (last_rows, rows - 1, sea_rows - 1)):
        out[pl.ds(wet_row, tail), :] = jnp.zeros((tail, width), F32)
        out[pl.ds(0, blocks), :] = state[pl.ds(at, blocks, stride=rows), :]
        out[pl.ds(blocks, ocean_blocks), :] = ocean[pl.ds(sea_at, ocean_blocks, stride=sea_rows), :]
        out[pl.ds(wet_row, 1), :] = wet[pl.ds(sea_at, 1), :].astype(F32)
    lanes = lax.broadcasted_iota(jnp.int32, (rows, width), 1)
    for part in range(2):
        first = jnp.zeros((rows, width), F32)
        last = jnp.zeros((rows, width), F32)
        for lane in range(half * levels):
            at = (part * half * levels + lane) * rows
            cells = state[pl.ds(at, rows), :]
            first = jnp.where(lanes == lane, cells[:, 0:1], first)
            last = jnp.where(lanes == lane, cells[:, width - 1 : width], last)
        first_cols[pl.ds(part * rows, rows), :] = first
        last_cols[pl.ds(part * rows, rows), :] = last
    lanes = lax.broadcasted_iota(jnp.int32, (sea_rows, width), 1)
    cells = wet[...].astype(F32)
    first = jnp.where(lanes == ocean_blocks, cells[:, 0:1], 0.0)
    last = jnp.where(lanes == ocean_blocks, cells[:, width - 1 : width], 0.0)
    for lane in range(ocean_blocks):
        cells = ocean[pl.ds(lane * sea_rows, sea_rows), :]
        first = jnp.where(lanes == lane, cells[:, 0:1], first)
        last = jnp.where(lanes == lane, cells[:, width - 1 : width], last)
    first_cols[pl.ds(2 * rows, sea_rows), :] = first
    last_cols[pl.ds(2 * rows, sea_rows), :] = last


def atmos_kernel(sizes, with_edges, state, north, south, west, east, diffusion, out, *edges):
    fields, levels, rows = sizes
    half = fields // 2
    width = state.shape[1]
    lanes = lax.broadcasted_iota(jnp.int32, (rows, width), 1)
    if with_edges:
        for cols in edges[2:]:
            cols[...] = jnp.zeros(cols.shape, F32)

    def field_step(field, carry):
        part = field // half
        within = (field - part * half) * levels
        held = pl.ds(pl.multiple_of(part * rows, rows), rows)
        back = lax.rem(width - within, width)
        west_cols = pltpu.roll(west[held, :], back, 1)
        east_cols = pltpu.roll(east[held, :], back, 1)
        number = diffusion[field]
        first = jnp.zeros((rows, width), F32)
        last = jnp.zeros((rows, width), F32)
        for level in range(levels):
            block = field * levels + level
            start = pl.multiple_of(block * rows, rows)
            cells = state[pl.ds(start, rows), :]
            upper = cells if level == 0 else state[pl.ds(start - rows, rows), :]
            lower = cells if level == levels - 1 else state[pl.ds(start + rows, rows), :]
            sides = around(
                cells,
                north[pl.ds(block, 1), :],
                south[pl.ds(block, 1), :],
                west_cols[:, level : level + 1],
                east_cols[:, level : level + 1],
            )
            after = diffused(cells, upper, lower, sides, number)
            out[pl.ds(start, rows), :] = after
            if with_edges:
                first = jnp.where(lanes == level, after[:, 0:1], first)
                last = jnp.where(lanes == level, after[:, width - 1 : width], last)
        if with_edges:
            edges[2][held, :] += pltpu.roll(first, within, 1)
            edges[3][held, :] += pltpu.roll(last, within, 1)
        return carry

    lax.fori_loop(0, fields, field_step, 0)
    if with_edges:
        blocks = fields * levels
        edges[0][...] = out[pl.ds(0, blocks, stride=rows), :]
        edges[1][...] = out[pl.ds(rows - 1, blocks, stride=rows), :]


def ocean_kernel(sizes, ocean, wet, north, south, west, east, mixing, out):
    fields, levels, rows, skipped, skipped_cols = sizes
    width = ocean.shape[1]
    cols = pl.ds(skipped_cols, rows)
    wet_cells = wet[...].astype(F32)
    wet_block = fields * levels
    wet_sides = around(
        wet_cells,
        north[pl.ds(skipped + wet_block, 1), :],
        south[pl.ds(skipped + wet_block, 1), :],
        west[cols, :][:, wet_block : wet_block + 1],
        east[cols, :][:, wet_block : wet_block + 1],
    )

    def field_step(field, carry):
        back = lax.rem(width - field * levels, width)
        west_cols = pltpu.roll(west[cols, :], back, 1)
        east_cols = pltpu.roll(east[cols, :], back, 1)
        number = mixing[field] * wet_cells
        for level in range(levels):
            block = field * levels + level
            start = pl.multiple_of(block * rows, rows)
            cells = ocean[pl.ds(start, rows), :]
            upper = cells if level == 0 else ocean[pl.ds(start - rows, rows), :]
            lower = cells if level == levels - 1 else ocean[pl.ds(start + rows, rows), :]
            sides = around(
                cells,
                north[pl.ds(skipped + block, 1), :],
                south[pl.ds(skipped + block, 1), :],
                west_cols[:, level : level + 1],
                east_cols[:, level : level + 1],
            )
            total = wet_sides[0] * (sides[0] - cells)
            for side in range(1, 4):
                total = total + wet_sides[side] * (sides[side] - cells)
            tendency = number * total + 0.1 * (upper + lower - 2.0 * cells)
            out[pl.ds(start, rows), :] = cells + wet_cells * tendency
        return carry

    lax.fori_loop(0, fields, field_step, 0)


def ranks_of(index, row, count, tally):
    def clear(at, carry):
        tally[at] = 0
        return carry

    lax.fori_loop(0, tally.shape[0], clear, 0)
    places = []
    for entry in range(count):
        owner = index[row, entry]
        rank = tally[owner]
        tally[owner] = rank + 1
        places.append((owner, rank))
    return places


def pieces_kernel(
    sizes, state, north, south, west, east, remap, index, diffusion, out, surface, tally
):
    fields, levels, rows, targets = sizes
    half = fields // 2
    width = out.shape[1]
    for field in range(fields):
        block = field * levels + levels - 1
        lane = (field % half) * levels + levels - 1
        held = pl.ds((field // half) * rows, rows)
        cells = state[field, 1]
        sides = around(
            cells,
            north[pl.ds(block, 1), :],
            south[pl.ds(block, 1), :],
            west[held, :][:, lane : lane + 1],
            east[held, :][:, lane : lane + 1],
        )
        surface[pl.ds(field * rows, rows), :] = diffused(
            cells, state[field, 0], cells, sides, diffusion[field]
        )
    out[...] = jnp.zeros(out.shape, F32)
    slots = targets * CAPACITY
    out[pl.ds(fields, slots, stride=PIECE_ROWS), :] = jnp.full((slots, width), -1.0, F32)
    places = ranks_of(index, 0, rows, tally)
    for tile in range(rows):
        owner, rank = places[tile]
        start = (owner * CAPACITY + rank) * PIECE_ROWS
        piece = remapped(surface[pl.ds(tile, fields, stride=rows), :], remap[tile])
        label = jnp.full((1, width), index[1, tile].astype(F32))
        out[pl.ds(start, fields), :] = piece
        out[pl.ds(start + fields, 1), :] = label


def flux_kernel(sizes, arrived, remap, index, out, gather, fluxes, tally):
    fields, flux_count, rows, targets, sections = sizes
    width = out.shape[1]
    slots = targets * CAPACITY
    select = one_hot(arrived[pl.ds(fields, slots, stride=PIECE_ROWS), :])
    gather[...] = select
    values = jnp.concatenate(
        [arrived[pl.ds(field, slots, stride=PIECE_ROWS), :] for field in range(fields)], axis=1
    )
    exchange = picked(jnp.transpose(select)[:rows, :], values)
    a = [exchange[:, field * width : (field + 1) * width] for field in range(fields)]
    speed = jnp.sqrt(a[2] * a[2] + a[3] * a[3] + 0.5)
    fluxes[pl.ds(0, rows), :] = speed * (a[0] - a[4]) + a[6] + a[7]
    fluxes[pl.ds(rows, rows), :] = speed * a[1] + a[5] + a[8]
    fluxes[pl.ds(2 * rows, rows), :] = speed * a[2] * (1.0 + 0.2 * jnp.tanh(a[9]))
    fluxes[pl.ds(3 * rows, rows), :] = speed * a[3]
    out[...] = jnp.zeros(out.shape, F32)
    devices = targets * sections
    label_row = CAPACITY * flux_count
    for entry in range(CAPACITY):
        out[pl.ds(label_row + entry, devices, stride=FLUX_ROWS), :] = jnp.full(
            (devices, width), -1.0, F32
        )
    places = ranks_of(index, 2, rows, tally)
    for tile in range(rows):
        owner, rank = places[tile]
        mapped = remapped(fluxes[pl.ds(tile, flux_count, stride=rows), :], remap[tile])
        label = jnp.full((1, width), index[3, tile].astype(F32))
        for section in range(sections):
            start = (section * targets + owner) * FLUX_ROWS
            out[pl.ds(start + rank * flux_count, flux_count), :] = mapped
            out[pl.ds(start + label_row + rank, 1), :] = label


def sea_kernel(sizes, landed, base, wet, own, out, answers):
    flux_count, sea_rows, targets, sections = sizes
    width = landed.shape[1]
    devices = targets * sections
    label_row = CAPACITY * flux_count
    select = jnp.concatenate(
        [
            one_hot(landed[pl.ds(label_row + entry, devices, stride=FLUX_ROWS), :])
            for entry in range(CAPACITY)
        ],
        axis=0,
    )
    values = jnp.concatenate(
        [
            jnp.concatenate(
                [
                    landed[pl.ds(entry * flux_count + flux, devices, stride=FLUX_ROWS), :]
                    for flux in range(flux_count)
                ],
                axis=1,
            )
            for entry in range(CAPACITY)
        ],
        axis=0,
    )
    forcing = picked(jnp.transpose(select)[:sea_rows, :], values)
    wet_cells = wet[...].astype(F32)
    tops = []
    for flux in range(flux_count):
        top = base[flux, 0] + wet_cells * (
            FORCING_SCALE[flux] * forcing[:, flux * width : (flux + 1) * width]
        )
        out[flux, 0] = top
        tops.append(top)
    all_tops = jnp.concatenate(tops, axis=1)
    first = own[0] * (targets * FLUX_ROWS)
    for entry in range(CAPACITY):
        mine = one_hot(landed[pl.ds(first + label_row + entry, targets, stride=FLUX_ROWS), :])
        reply = picked(mine[:, :sea_rows], all_tops)
        for flux in range(flux_count):
            answers[
                pl.ds(entry * flux_count + flux, targets, stride=CAPACITY * flux_count), :
            ] = reply[:, flux * width : (flux + 1) * width]


def reply_kernel(sizes, answered, remap, index, gather, out, on_exchange, tally):
    flux_count, rows, targets = sizes
    width = out.shape[1]
    slots = targets * CAPACITY
    places = ranks_of(index, 2, rows, tally)
    for tile in range(rows):
        owner, rank = places[tile]
        start = (owner * CAPACITY + rank) * flux_count
        on_exchange[pl.ds(tile * flux_count, flux_count), :] = remapped(
            answered[pl.ds(start, flux_count), :], remap[tile], True
        )
    values = jnp.concatenate(
        [on_exchange[pl.ds(flux, rows, stride=flux_count), :] for flux in range(flux_count)], axis=1
    )
    replies = picked(gather[...][:, :rows], values)
    for flux in range(flux_count):
        out[pl.ds(flux, slots, stride=flux_count), :] = replies[
            :, flux * width : (flux + 1) * width
        ]


def surface_kernel(sizes, returned, remap, index, out, tally):
    flux_count, rows, targets = sizes
    places = ranks_of(index, 0, rows, tally)
    for tile in range(rows):
        owner, rank = places[tile]
        start = (owner * CAPACITY + rank) * flux_count
        out[pl.ds(tile, flux_count, stride=rows), :] = remapped(
            returned[pl.ds(start, flux_count), :], remap[tile], True
        )


VMEM = pl.BlockSpec(memory_space=pltpu.VMEM)
SMEM = pl.BlockSpec(memory_space=pltpu.SMEM)


def array(*shape):
    return jax.ShapeDtypeStruct(shape, F32)


def call(kernel, name, outs, in_specs, scratch=(), flops=0, moved=0, **more):
    return pl.pallas_call(
        kernel,
        name=name,
        out_shape=outs,
        in_specs=in_specs,
        scratch_shapes=list(scratch),
        compiler_params=pltpu.CompilerParams(vmem_limit_bytes=VMEM_LIMIT),
        cost_estimate=pl.CostEstimate(flops=flops, bytes_accessed=moved, transcendentals=0),
        **more,
    )


def on_device(
    atmos_state,
    atmos_diffusion,
    remap_atmos,
    exchange_owner,
    exchange_slot,
    remap_ocean,
    ocean_owner,
    ocean_slot,
    ocean_state,
    ocean_mixing,
    wet_mask,
):
    targets = lax.axis_size(SECTION)
    sections = lax.axis_size("comp")
    devices = targets * sections
    fields, levels, rows, width = atmos_state.shape
    sea_fields, sea_levels, sea_rows, _ = ocean_state.shape
    blocks = fields * levels
    sea_blocks = sea_fields * sea_levels
    edge_rows = -(-(blocks + sea_blocks + 1) // 8) * 8
    edge_cols = 2 * rows + sea_rows
    slots = targets * CAPACITY
    ring = ("comp", "gx")

    index = jnp.stack([exchange_owner[:, 0], exchange_slot, ocean_owner[:, 0], ocean_slot])
    section = lax.axis_index("comp").astype(jnp.int32).reshape(1)
    state = atmos_state.reshape(blocks * rows, width)
    ocean = ocean_state.reshape(sea_blocks * sea_rows, width)

    first_rows, last_rows, first_cols, last_cols = call(
        functools.partial(edges_kernel, (fields, levels, rows, sea_blocks, sea_rows)),
        "edges",
        (
            array(edge_rows, width),
            array(edge_rows, width),
            array(edge_cols, width),
            array(edge_cols, width),
        ),
        [VMEM] * 3,
        moved=state.size * 4 + ocean.size * 4,
    )(state, ocean, wet_mask)
    west = shifted(last_cols, "gy", 1)
    east = shifted(first_cols, "gy", -1)
    north = shifted(last_rows, ring, 1)
    south = shifted(first_rows, ring, -1)

    pieces = pl.pallas_call(
        functools.partial(pieces_kernel, (fields, levels, rows, targets)),
        name="pieces",
        grid=(1,),
        out_shape=array(slots * PIECE_ROWS, width),
        in_specs=[
            pl.BlockSpec((fields, 2, rows, width), lambda i: (0, levels // 2 - 1, 0, 0)),
            VMEM,
            VMEM,
            VMEM,
            VMEM,
            VMEM,
            SMEM,
            SMEM,
        ],
        out_specs=VMEM,
        scratch_shapes=[pltpu.VMEM((fields * rows, width), F32), pltpu.SMEM((targets,), jnp.int32)],
        compiler_params=pltpu.CompilerParams(vmem_limit_bytes=VMEM_LIMIT),
        cost_estimate=pl.CostEstimate(
            flops=6 * fields * rows * width * width,
            bytes_accessed=remap_atmos.size * 4,
            transcendentals=0,
        ),
    )(atmos_state, north, south, west, east, remap_atmos, index, atmos_diffusion)
    arrived = lax.all_to_all(
        pieces.reshape(targets, CAPACITY * PIECE_ROWS, width), SECTION, 0, 0, tiled=True
    )

    after_first, up_rows, down_rows, left_cols, right_cols = call(
        functools.partial(atmos_kernel, (fields, levels, rows), True),
        "first_step",
        (
            array(blocks * rows, width),
            array(blocks, width),
            array(blocks, width),
            array(2 * rows, width),
            array(2 * rows, width),
        ),
        [VMEM] * 5 + [SMEM],
        flops=20 * state.size,
        moved=state.size * 8,
    )(state, north, south, west, east, atmos_diffusion)
    west_next = shifted(right_cols, "gy", 1)
    east_next = shifted(left_cols, "gy", -1)
    north_next = shifted(down_rows, ring, 1)
    south_next = shifted(up_rows, ring, -1)
    sea_base = call(
        functools.partial(ocean_kernel, (sea_fields, sea_levels, sea_rows, blocks, 2 * rows)),
        "sea_base",
        array(sea_blocks * sea_rows, width),
        [VMEM] * 6 + [SMEM],
        flops=30 * ocean.size,
        moved=ocean.size * 8,
    )(ocean, wet_mask, north, south, west, east, ocean_mixing)

    outgoing, gather = call(
        functools.partial(flux_kernel, (fields, sea_fields, rows, targets, sections)),
        "fluxes",
        (array(devices * FLUX_ROWS, width), array(slots, width)),
        [VMEM, VMEM, SMEM],
        [
            pltpu.VMEM((sea_fields * rows, width), F32),
            pltpu.SMEM((targets,), jnp.int32),
        ],
        flops=6 * sea_fields * rows * width * width,
        moved=remap_ocean.size * 4,
    )(arrived.reshape(slots * PIECE_ROWS, width), remap_ocean, index)
    landed = lax.all_to_all(
        outgoing.reshape(devices, FLUX_ROWS, width), EVERY, 0, 0, tiled=True
    )

    top_block = pl.BlockSpec((sea_fields, 1, sea_rows, width), lambda i: (0, 0, 0, 0))
    ocean_next, answers = pl.pallas_call(
        functools.partial(sea_kernel, (sea_fields, sea_rows, targets, sections)),
        name="sea_top",
        grid=(1,),
        out_shape=(
            array(sea_fields, sea_levels, sea_rows, width),
            array(slots * sea_fields, width),
        ),
        in_specs=[VMEM, top_block, VMEM, SMEM],
        out_specs=(top_block, VMEM),
        input_output_aliases={1: 0},
        compiler_params=pltpu.CompilerParams(vmem_limit_bytes=VMEM_LIMIT),
        cost_estimate=pl.CostEstimate(flops=0, bytes_accessed=landed.size * 4, transcendentals=0),
    )(
        landed.reshape(devices * FLUX_ROWS, width),
        sea_base.reshape(sea_fields, sea_levels, sea_rows, width),
        wet_mask,
        section,
    )
    answered = lax.all_to_all(
        answers.reshape(targets, CAPACITY * sea_fields, width), SECTION, 0, 0, tiled=True
    )

    atmos_next = call(
        functools.partial(atmos_kernel, (fields, levels, rows), False),
        "second_step",
        array(blocks * rows, width),
        [VMEM] * 5 + [SMEM],
        flops=20 * state.size,
        moved=state.size * 8,
    )(after_first, north_next, south_next, west_next, east_next, atmos_diffusion)

    replies = call(
        functools.partial(reply_kernel, (sea_fields, rows, targets)),
        "replies",
        array(slots * sea_fields, width),
        [VMEM, VMEM, SMEM, VMEM],
        [
            pltpu.VMEM((sea_fields * rows, width), F32),
            pltpu.SMEM((targets,), jnp.int32),
        ],
        flops=6 * sea_fields * rows * width * width,
        moved=remap_ocean.size * 4,
    )(answered.reshape(slots * sea_fields, width), remap_ocean, index, gather)
    returned = lax.all_to_all(
        replies.reshape(targets, CAPACITY * sea_fields, width), SECTION, 0, 0, tiled=True
    )
    ocean_surface = call(
        functools.partial(surface_kernel, (sea_fields, rows, targets)),
        "surface",
        array(sea_fields * rows, width),
        [VMEM, VMEM, SMEM],
        [pltpu.SMEM((targets,), jnp.int32)],
        flops=6 * sea_fields * rows * width * width,
        moved=remap_atmos.size * 4,
    )(returned.reshape(slots * sea_fields, width), remap_atmos, index)
    return (
        atmos_next.reshape(atmos_state.shape),
        ocean_next,
        ocean_surface.reshape(sea_fields, rows, width),
    )


def solution(mesh):
    in_specs = (
        P(None, None, ("comp", "gx"), "gy"),
        P(),
        P(("comp", "gx", "gy"), None, None),
        P(("comp", "gx", "gy"), None),
        P(("comp", "gx", "gy")),
        P(("comp", "gx", "gy"), None, None),
        P(("comp", "gx", "gy"), None),
        P(("comp", "gx", "gy")),
        P(None, None, "gx", "gy"),
        P(),
        P("gx", "gy"),
    )
    out_specs = (
        P(None, None, ("comp", "gx"), "gy"),
        P(None, None, "gx", "gy"),
        P(None, ("comp", "gx"), "gy"),
    )
    return jax.shard_map(
        on_device, mesh=mesh, in_specs=in_specs, out_specs=out_specs, check_vma=False
    )
```

```python
import functools

import jax
import jax.numpy as jnp
from jax import lax
from jax.experimental import pallas as pl
from jax.experimental.pallas import tpu as pltpu
from jax.sharding import PartitionSpec as P

F32 = jnp.float32
BF16 = jnp.bfloat16
FORCING_SCALE = (0.1, -0.1, 0.1, 0.1)
SECTION = ("gx", "gy")
EVERY = ("comp", "gx", "gy")
CAPACITY = 2
PIECE_ROWS = 12
VMEM_LIMIT = 8 * 1024 * 1024
STREAM_LIMIT = 60 * 1024 * 1024


def shifted(block, axis, distance):
    devices = range(lax.axis_size(axis))
    route = [((i - distance) % len(devices), i) for i in devices]
    return lax.ppermute(block, axis, route)


def dot(left, right, transposed=False):
    dims = (((1,), (1 if transposed else 0,)), ((), ()))
    return lax.dot_general(left, right, dims, preferred_element_type=F32)


def halves(values):
    high = values.astype(BF16)
    return high, (values - high.astype(F32)).astype(BF16)


def remapped(rows, weights):
    count, width = rows.shape
    high, low = halves(rows)
    if count < 16:
        filler = jnp.zeros((16 - count, width), F32)
        high, low = halves(jnp.concatenate([rows, filler], axis=0))
    left = jnp.concatenate(
        [
            jnp.concatenate([high, high], axis=1),
            jnp.concatenate([low, jnp.zeros(low.shape, BF16)], axis=1),
        ],
        axis=0,
    )
    product = dot(left, weights)
    return product[:count, :] + product[16 : 16 + count, :]


def both_halves(block):
    return jnp.concatenate(halves(block), axis=0)


def weights_kernel(transposed, remap, weights):
    for tile in range(remap.shape[0]):
        block = remap[tile]
        weights[tile] = both_halves(jnp.transpose(block) if transposed else block)


def picked(selection, values):
    chosen = selection.astype(BF16)
    high = values.astype(BF16)
    rest = values - high.astype(F32)
    middle = rest.astype(BF16)
    low = (rest - middle.astype(F32)).astype(BF16)
    return dot(chosen, high) + dot(chosen, middle) + dot(chosen, low)


def one_hot(labels):
    lanes = lax.broadcasted_iota(jnp.int32, labels.shape, 1).astype(F32)
    return (labels == lanes).astype(F32)


def grid_index(shape):
    return lax.broadcasted_iota(jnp.int32, shape, 0), lax.broadcasted_iota(jnp.int32, shape, 1)


def around(cells, north, south, west, east):
    rows, lanes = grid_index(cells.shape)
    row_count, width = cells.shape
    return (
        jnp.where(rows == 0, north, pltpu.roll(cells, 1, 0)),
        jnp.where(rows == row_count - 1, south, pltpu.roll(cells, row_count - 1, 0)),
        jnp.where(lanes == 0, west, pltpu.roll(cells, 1, 1)),
        jnp.where(lanes == width - 1, east, pltpu.roll(cells, width - 1, 1)),
    )


def diffused(cells, upper, lower, sides, diffusion):
    beside = sides[0] + sides[1] + sides[2] + sides[3] - 4.0 * cells
    return cells + diffusion * beside + 0.1 * (upper + lower - 2.0 * cells)


class Edges:
    def __init__(self, fields, levels, rows, sea_blocks, sea_rows, width):
        self.fields, self.levels, self.rows, self.width = fields, levels, rows, width
        self.sea_blocks, self.sea_rows = sea_blocks, sea_rows
        self.half = fields // 2
        self.part = self.half * levels
        self.part_rows = -(-self.part // 8) * 8
        self.atmos_rows = 2 * self.part_rows
        self.wet_row = self.atmos_rows + sea_blocks
        self.near_rows = -(-(self.wet_row + 1) // 8) * 8
        self.corner_row = self.atmos_rows
        self.far_rows = self.atmos_rows + 8
        self.sea_tiles = sea_blocks * sea_rows // width
        self.sea_cols = 4 * rows
        self.sea_col_rows = -(-(self.sea_tiles + 1) // 8) * 8
        self.col_rows = self.sea_cols + self.sea_col_rows


def squared(values):
    rows, width = values.shape
    if rows == width:
        return values
    return jnp.concatenate([values, jnp.zeros((width - rows, width), F32)], axis=0)


def chunk(source, target, at, rows, arrival):
    part = pl.ds(pl.multiple_of(at * rows, 8), rows)
    return pltpu.make_async_copy(source.at[part], target.at[part], arrival)


def edges_kernel(
    at,
    state_far,
    ocean_far,
    wet_far,
    near_first,
    near_last,
    far_first,
    far_last,
    first,
    last,
    state,
    ocean,
    wet,
    arrivals,
):
    rows, part, width = at.rows, at.part, at.width
    field_rows = at.levels * rows
    sea_parts = 4
    copies = [
        chunk(state_far, state, field, field_rows, arrivals.at[field])
        for field in range(at.fields)
    ]
    copies += [
        chunk(ocean_far, ocean, field, ocean.shape[0] // sea_parts, arrivals.at[at.fields + field])
        for field in range(sea_parts)
    ]
    copies.append(pltpu.make_async_copy(wet_far, wet, arrivals.at[at.fields + sea_parts]))
    for copy in copies:
        copy.start()
    for out in (near_first, near_last, far_first, far_last):
        out[...] = jnp.zeros(out.shape, F32)
    for cols in (first, last):
        cols[pl.ds(at.sea_cols, at.sea_col_rows), :] = jnp.zeros((at.sea_col_rows, width), F32)
    for half in range(2):
        for field in range(half * at.half, (half + 1) * at.half):
            copies[field].wait()
        for row in range(rows):
            lines = state[pl.ds(half * part * rows + row, part, stride=rows), :]
            held = pl.ds(half * at.part_rows, part)
            if row < 2:
                (near_first, far_first)[row][held, :] = lines
            if row >= rows - 2:
                (near_last, far_last)[rows - 1 - row][held, :] = lines
            turned = jnp.transpose(squared(lines))
            near, far = half * rows + row, (2 + half) * rows + row
            first[pl.ds(near, 1), :] = turned[0:1, :]
            first[pl.ds(far, 1), :] = turned[1:2, :]
            last[pl.ds(near, 1), :] = turned[width - 1 : width, :]
            last[pl.ds(far, 1), :] = turned[width - 2 : width - 1, :]
    for copy in copies[at.fields :]:
        copy.wait()
    for out, sea_row in ((near_first, 0), (near_last, at.sea_rows - 1)):
        out[pl.ds(at.atmos_rows, at.sea_blocks), :] = ocean[
            pl.ds(sea_row, at.sea_blocks, stride=at.sea_rows), :
        ]
        out[pl.ds(at.wet_row, 1), :] = wet[pl.ds(sea_row, 1), :].astype(F32)
    for tile in range(at.sea_tiles + 1):
        if tile < at.sea_tiles:
            lines = ocean[pl.ds(tile * width, width), :]
        else:
            lines = squared(wet[...].astype(F32))
        turned = jnp.transpose(lines)
        first[pl.ds(at.sea_cols + tile, 1), :] = turned[0:1, :]
        last[pl.ds(at.sea_cols + tile, 1), :] = turned[width - 1 : width, :]


def corners_kernel(at, far_first, far_last, west, east, to_north, to_south):
    for out, lines, row in ((to_north, far_first, 0), (to_south, far_last, at.rows - 1)):
        out[...] = lines[...]
        for place, (cols, half) in enumerate(((west, 0), (west, 1), (east, 0), (east, 1))):
            out[pl.ds(at.corner_row + place, 1), :] = cols[pl.ds(half * at.rows + row, 1), :]


def spread(at, diffusion, part, places):
    numbers = jnp.zeros(places.shape, F32)
    is_first = places < 0
    is_last = places < 0
    for field in range(at.half):
        start = field * at.levels
        numbers = jnp.where(places >= start, diffusion[part * at.half + field], numbers)
        is_first = is_first | (places == start)
        is_last = is_last | (places == start + at.levels - 1)
    return numbers, is_first, is_last


def ring_step(at, part, halos, edges, diffusion, outs):
    north, south, west, east, far_north, far_south = halos
    near_first, near_last, first, last = edges
    rows, width = at.rows, at.width
    shape = (at.part_rows, width)
    held = pl.ds(part * at.part_rows, shape[0])
    lines, lanes = grid_index(shape)
    numbers, is_first, is_last = spread(at, diffusion, part, lines)
    for out, outside, further, own, is_north in (
        (outs[0], north, far_north, near_first, True),
        (outs[1], south, far_south, near_last, False),
    ):
        turned = jnp.transpose(squared(further[pl.ds(at.corner_row, 8), :]))[: shape[0], :]
        cells, beyond, inside = outside[held, :], further[held, :], own[held, :]
        west_col = jnp.where(lanes == 0, turned[:, part : part + 1], pltpu.roll(cells, 1, 1))
        east_col = jnp.where(
            lanes == width - 1, turned[:, 2 + part : 3 + part], pltpu.roll(cells, width - 1, 1)
        )
        sides = (
            beyond if is_north else inside,
            inside if is_north else beyond,
            west_col,
            east_col,
        )
        upper = jnp.where(is_first, cells, pltpu.roll(cells, 1, 0))
        lower = jnp.where(is_last, cells, pltpu.roll(cells, shape[0] - 1, 0))
        out[...] = diffused(cells, upper, lower, sides, numbers)

    shape = (rows, width)
    near, far = pl.ds(part * rows, rows), pl.ds((2 + part) * rows, rows)
    lines, lanes = grid_index(shape)
    numbers, is_first, is_last = spread(at, diffusion, part, lanes)
    for out, outside, own, corner, is_west in (
        (outs[2], west, first, 0, True),
        (outs[3], east, last, 2, False),
    ):
        cells, beyond, inside = outside[near, :], outside[far, :], own[near, :]
        place = pl.ds(at.corner_row + corner + part, 1)
        sides = (
            jnp.where(lines == 0, far_north[place, :], pltpu.roll(cells, 1, 0)),
            jnp.where(lines == rows - 1, far_south[place, :], pltpu.roll(cells, rows - 1, 0)),
            beyond if is_west else inside,
            inside if is_west else beyond,
        )
        upper = jnp.where(is_first, cells, pltpu.roll(cells, 1, 1))
        lower = jnp.where(is_last, cells, pltpu.roll(cells, width - 1, 1))
        out[...] = diffused(cells, upper, lower, sides, numbers)


def field_step(at, field, state, out, north, south, first_line, west_cols, east_cols, number):
    levels, rows, width = at.levels, at.rows, at.width
    lines, lanes = grid_index((rows, width))
    for level in range(levels):
        line = first_line + field * levels + level
        start = pl.multiple_of((field * levels + level) * rows, rows)
        cells = state[pl.ds(start, rows), :]
        first_level, last_level = level == 0, level == levels - 1
        upper = cells if first_level else state[pl.ds(start - rows, rows), :]
        lower = cells if last_level else state[pl.ds(start + rows, rows), :]
        sides = (
            jnp.where(lines == 0, north[pl.ds(line, 1), :], pltpu.roll(cells, 1, 0)),
            jnp.where(
                lines == rows - 1, south[pl.ds(line, 1), :], pltpu.roll(cells, rows - 1, 0)
            ),
            jnp.where(lanes == 0, pltpu.roll(west_cols, (width - level) % width, 1), pltpu.roll(cells, 1, 1)),
            jnp.where(
                lanes == width - 1,
                pltpu.roll(east_cols, width - 1 - level, 1),
                pltpu.roll(cells, width - 1, 1),
            ),
        )
        out[pl.ds(start, rows), :] = diffused(cells, upper, lower, sides, number)


def steps_kernel(
    at,
    part,
    state_far,
    north,
    south,
    west,
    east,
    far_north,
    far_south,
    near_first,
    near_last,
    first,
    last,
    diffusion,
    *rest,
):
    if part:
        rest = rest[1:]
    out_far, state, middle, out, *ring, arrivals, departures = rest
    rows, width, levels = at.rows, at.width, at.levels
    field_rows = levels * rows
    whole = part * at.half

    def coming(field):
        return pltpu.make_async_copy(
            state_far.at[pl.ds(pl.multiple_of((whole + field) * field_rows, 8), field_rows)],
            state.at[pl.ds(pl.multiple_of(field * field_rows, 8), field_rows)],
            arrivals.at[field],
        )

    def going(field):
        return pltpu.make_async_copy(
            out.at[pl.ds(pl.multiple_of(field * field_rows, 8), field_rows)],
            out_far.at[pl.ds(pl.multiple_of((whole + field) * field_rows, 8), field_rows)],
            departures.at[field],
        )

    for field in range(at.half):
        coming(field).start()
    halos = (north, south, west, east, far_north, far_south)
    ring_step(at, part, halos, (near_first, near_last, first, last), diffusion, ring)
    held = pl.ds(part * rows, rows)

    def both_steps(field, carry):
        back = lax.rem(width - field * levels, width)
        number = diffusion[whole + field]
        west_cols = pltpu.roll(west[held, :], back, 1)
        east_cols = pltpu.roll(east[held, :], back, 1)
        coming(field).wait()
        line = part * at.part_rows
        field_step(at, field, state, middle, north, south, line, west_cols, east_cols, number)
        west_cols = pltpu.roll(ring[2][...], back, 1)
        east_cols = pltpu.roll(ring[3][...], back, 1)
        field_step(at, field, middle, out, ring[0], ring[1], 0, west_cols, east_cols, number)
        going(field).start()
        return carry

    lax.fori_loop(0, at.half, both_steps, 0)
    for field in range(at.half):
        going(field).wait()


def ocean_kernel(
    at,
    levels,
    ocean_far,
    wet,
    north,
    south,
    west,
    east,
    mixing,
    out_far,
    ocean,
    out,
    wests,
    easts,
    arrivals,
    departures,
):
    fields, field_rows = at.sea_blocks // levels, levels * at.sea_rows
    for field in range(fields):
        chunk(ocean_far, ocean, field, field_rows, arrivals.at[field]).start()
    rows, width = at.sea_rows, at.width
    lines, lanes = grid_index((rows, width))
    per_tile = width // rows
    held = pl.ds(at.sea_cols, at.sea_col_rows)
    wests[...] = jnp.transpose(squared(west[held, :]))
    easts[...] = jnp.transpose(squared(east[held, :]))
    wet_cells = wet[...].astype(F32)
    wet_lane = at.sea_tiles
    wet_sides = around(
        wet_cells,
        north[pl.ds(at.wet_row, 1), :],
        south[pl.ds(at.wet_row, 1), :],
        wests[pl.ds(0, rows), :][:, wet_lane : wet_lane + 1],
        easts[pl.ds(0, rows), :][:, wet_lane : wet_lane + 1],
    )

    def field_step(field, carry):
        chunk(ocean_far, ocean, field, field_rows, arrivals.at[field]).wait()
        back = lax.rem(width - field * (levels // per_tile), width)
        west_cols = pltpu.roll(wests[...], back, 1)
        east_cols = pltpu.roll(easts[...], back, 1)
        number = mixing[field] * wet_cells
        for level in range(levels):
            block = field * levels + level
            start = pl.multiple_of(block * rows, rows)
            first_level, last_level = level == 0, level == levels - 1
            cells = ocean[pl.ds(start, rows), :]
            upper = cells if first_level else ocean[pl.ds(start - rows, rows), :]
            lower = cells if last_level else ocean[pl.ds(start + rows, rows), :]
            above = pltpu.roll(cells, 1, 0)
            below = pltpu.roll(cells, rows - 1, 0)
            line = at.atmos_rows + block
            tile, within = level // per_tile, (level % per_tile) * rows
            west_col = pltpu.roll(west_cols[within : within + rows, :], (width - tile) % width, 1)
            east_col = pltpu.roll(east_cols[within : within + rows, :], width - 1 - tile, 1)
            sides = (
                jnp.where(lines == 0, north[pl.ds(line, 1), :], above),
                jnp.where(lines == rows - 1, south[pl.ds(line, 1), :], below),
                jnp.where(lanes == 0, west_col, pltpu.roll(cells, 1, 1)),
                jnp.where(lanes == width - 1, east_col, pltpu.roll(cells, width - 1, 1)),
            )
            total = wet_sides[0] * (sides[0] - cells)
            for side in range(1, 4):
                total = total + wet_sides[side] * (sides[side] - cells)
            tendency = number * total + 0.1 * (upper + lower - 2.0 * cells)
            out[pl.ds(start, rows), :] = cells + wet_cells * tendency
        chunk(out, out_far, field, field_rows, departures.at[field]).start()
        return carry

    lax.fori_loop(0, fields, field_step, 0)
    for field in range(fields):
        chunk(out, out_far, field, field_rows, departures.at[field]).wait()


def ranks_of(index, row, count, tally):
    def clear(at, carry):
        tally[at] = 0
        return carry

    lax.fori_loop(0, tally.shape[0], clear, 0)
    places = []
    for entry in range(count):
        owner = index[row, entry]
        rank = tally[owner]
        tally[owner] = rank + 1
        places.append((owner, rank))
    return places


def inner_kernel(at, state_far, diffusion, out, top, arrival):
    fields, rows, width = at.fields, at.rows, at.width
    copy = pltpu.make_async_copy(state_far.at[:, pl.ds(at.levels - 2, 2)], top, arrival)
    copy.start()
    lines, lanes = grid_index((rows, width))
    copy.wait()
    for field in range(fields):
        cells = top[field, 1]
        sides = (
            jnp.where(lines == 0, 0.0, pltpu.roll(cells, 1, 0)),
            jnp.where(lines == rows - 1, 0.0, pltpu.roll(cells, rows - 1, 0)),
            jnp.where(lanes == 0, 0.0, pltpu.roll(cells, 1, 1)),
            jnp.where(lanes == width - 1, 0.0, pltpu.roll(cells, width - 1, 1)),
        )
        out[pl.ds(field * rows, rows), :] = diffused(
            cells, top[field, 0], cells, sides, diffusion[field]
        )


def pieces_kernel(
    at, targets, inner, north, south, west, east, weights, index, diffusion, out, surface, tally
):
    fields, levels, rows, width = at.fields, at.levels, at.rows, at.width
    lines, lanes = grid_index((rows, width))
    for field in range(fields):
        part = field // at.half
        held = pl.ds(part * rows, rows)
        lane = (field % at.half) * levels + levels - 1
        line = pl.ds(part * at.part_rows + lane, 1)
        outside = (
            jnp.where(lines == 0, north[line, :], 0.0)
            + jnp.where(lines == rows - 1, south[line, :], 0.0)
            + jnp.where(lanes == 0, pltpu.roll(west[held, :], (width - lane) % width, 1), 0.0)
            + jnp.where(lanes == width - 1, pltpu.roll(east[held, :], width - 1 - lane, 1), 0.0)
        )
        here = pl.ds(field * rows, rows)
        surface[here, :] = inner[here, :] + diffusion[field] * outside
    surface[pl.ds(fields * rows, (16 - fields) * rows), :] = jnp.zeros(
        ((16 - fields) * rows, width), F32
    )
    out[...] = jnp.zeros(out.shape, F32)
    slots = targets * CAPACITY
    for row in (fields, fields + 1):
        out[pl.ds(row, slots, stride=PIECE_ROWS), :] = jnp.full((slots, width), -1.0, F32)
    places = ranks_of(index, 2, rows, tally)
    for tile in range(rows):
        owner, rank = places[tile]
        start = (owner * CAPACITY + rank) * PIECE_ROWS
        label = jnp.full((1, width), index[3, tile].astype(F32))
        out[pl.ds(start + fields + 1, 1), :] = label
    places = ranks_of(index, 0, rows, tally)
    for tile in range(rows):
        owner, rank = places[tile]
        start = (owner * CAPACITY + rank) * PIECE_ROWS
        piece = remapped(surface[pl.ds(tile, 16, stride=rows), :], weights[tile])[:fields, :]
        label = jnp.full((1, width), index[1, tile].astype(F32))
        out[pl.ds(start, fields), :] = piece
        out[pl.ds(start + fields, 1), :] = label


def flux_kernel(sizes, arrived, remap, index, out, gather, sea_labels, fluxes, tally):
    fields, flux_count, rows, targets, sections = sizes
    width = out.shape[1]
    slots = targets * CAPACITY
    select = one_hot(arrived[pl.ds(fields, slots, stride=PIECE_ROWS), :])
    gather[...] = select
    sea_labels[...] = arrived[pl.ds(fields + 1, slots, stride=PIECE_ROWS), :]
    values = jnp.concatenate(
        [arrived[pl.ds(field, slots, stride=PIECE_ROWS), :] for field in range(fields)], axis=1
    )
    exchange = picked(jnp.transpose(select)[:rows, :], values)
    a = [exchange[:, field * width : (field + 1) * width] for field in range(fields)]
    speed = jnp.sqrt(a[2] * a[2] + a[3] * a[3] + 0.5)
    fluxes[pl.ds(0, rows), :] = speed * (a[0] - a[4]) + a[6] + a[7]
    fluxes[pl.ds(rows, rows), :] = speed * a[1] + a[5] + a[8]
    fluxes[pl.ds(2 * rows, rows), :] = speed * a[2] * (1.0 + 0.2 * jnp.tanh(a[9]))
    fluxes[pl.ds(3 * rows, rows), :] = speed * a[3]
    out[...] = jnp.zeros(out.shape, F32)
    places = ranks_of(index, 2, rows, tally)
    for tile in range(rows):
        owner, rank = places[tile]
        mapped = remapped(fluxes[pl.ds(tile, flux_count, stride=rows), :], both_halves(remap[tile]))
        for section in range(sections):
            start = ((section * targets + owner) * CAPACITY + rank) * flux_count
            out[pl.ds(start, flux_count), :] = mapped


def sea_kernel(
    sizes,
    landed,
    wet,
    own_labels,
    other_labels,
    own,
    base,
    out,
    answers,
    tops,
    before,
    wet_here,
    arrivals,
    departures,
):
    flux_count, sea_rows, targets = sizes
    fetched = [
        pltpu.make_async_copy(
            out.at[flux, 0], before.at[pl.ds(flux * sea_rows, sea_rows)], arrivals.at[flux]
        )
        for flux in range(flux_count)
    ]
    fetched.append(pltpu.make_async_copy(wet, wet_here, arrivals.at[flux_count]))
    for copy in fetched:
        copy.start()
    width = landed.shape[1]
    slots = targets * CAPACITY
    mine = one_hot(own_labels[...])
    others = one_hot(other_labels[...])
    is_first = own[0] == 0
    select = jnp.concatenate(
        [jnp.where(is_first, mine, others), jnp.where(is_first, others, mine)], axis=0
    )
    values = jnp.concatenate(
        [landed[pl.ds(flux, 2 * slots, stride=flux_count), :] for flux in range(flux_count)], axis=1
    )
    forcing = picked(jnp.transpose(select)[:sea_rows, :], values)
    for copy in fetched:
        copy.wait()
    wet_cells = wet_here[...].astype(F32)
    copies = []
    for flux in range(flux_count):
        held = pl.ds(flux * sea_rows, sea_rows)
        tops[held, :] = before[held, :] + wet_cells * (
            FORCING_SCALE[flux] * forcing[:, flux * width : (flux + 1) * width]
        )
        copies.append(
            pltpu.make_async_copy(tops.at[held], out.at[flux, 0], departures.at[flux])
        )
        copies[flux].start()
    all_tops = jnp.concatenate(
        [tops[pl.ds(flux * sea_rows, sea_rows), :] for flux in range(flux_count)], axis=1
    )
    reply = picked(mine[:, :sea_rows], all_tops)
    for flux in range(flux_count):
        answers[pl.ds(flux, slots, stride=flux_count), :] = reply[
            :, flux * width : (flux + 1) * width
        ]
    for copy in copies:
        copy.wait()


def reply_kernel(sizes, answered, remap, index, gather, out, on_exchange, tally):
    flux_count, rows, targets = sizes
    width = out.shape[1]
    slots = targets * CAPACITY
    places = ranks_of(index, 2, rows, tally)
    for tile in range(rows):
        owner, rank = places[tile]
        start = (owner * CAPACITY + rank) * flux_count
        on_exchange[pl.ds(tile * flux_count, flux_count), :] = remapped(
            answered[pl.ds(start, flux_count), :], both_halves(jnp.transpose(remap[tile]))
        )
    values = jnp.concatenate(
        [on_exchange[pl.ds(flux, rows, stride=flux_count), :] for flux in range(flux_count)], axis=1
    )
    replies = picked(gather[...][:, :rows], values)
    for flux in range(flux_count):
        out[pl.ds(flux, slots, stride=flux_count), :] = replies[
            :, flux * width : (flux + 1) * width
        ]


def surface_kernel(sizes, returned, weights, index, out, tally):
    flux_count, rows, targets = sizes
    places = ranks_of(index, 0, rows, tally)
    for tile in range(rows):
        owner, rank = places[tile]
        start = (owner * CAPACITY + rank) * flux_count
        out[pl.ds(tile, flux_count, stride=rows), :] = remapped(
            returned[pl.ds(start, flux_count), :], weights[tile]
        )


VMEM = pl.BlockSpec(memory_space=pltpu.VMEM)
SMEM = pl.BlockSpec(memory_space=pltpu.SMEM)
ANY = pl.BlockSpec(memory_space=pl.ANY)


def array(*shape):
    return jax.ShapeDtypeStruct(shape, F32)


def call(kernel, name, outs, in_specs, scratch=(), after=(), limit=VMEM_LIMIT, work=1_000_000, **more):
    def body(*refs):
        kernel(*refs[: len(in_specs)], *refs[len(in_specs) + len(after) :])

    run = pl.pallas_call(
        body,
        name=name,
        out_shape=outs,
        in_specs=list(in_specs) + [ANY] * len(after),
        scratch_shapes=list(scratch),
        compiler_params=pltpu.CompilerParams(vmem_limit_bytes=limit),
        cost_estimate=pl.CostEstimate(flops=0, bytes_accessed=work, transcendentals=0),
        **more,
    )
    return lambda *arguments: run(*arguments, *after)


def on_device(
    atmos_state,
    atmos_diffusion,
    remap_atmos,
    exchange_owner,
    exchange_slot,
    remap_ocean,
    ocean_owner,
    ocean_slot,
    ocean_state,
    ocean_mixing,
    wet_mask,
):
    targets = lax.axis_size(SECTION)
    sections = lax.axis_size("comp")
    devices = targets * sections
    fields, levels, rows, width = atmos_state.shape
    sea_fields, sea_levels, sea_rows, _ = ocean_state.shape
    blocks = fields * levels
    sea_blocks = sea_fields * sea_levels
    at = Edges(fields, levels, rows, sea_blocks, sea_rows, width)
    slots = targets * CAPACITY
    ring = ("comp", "gx")
    tally = pltpu.SMEM((targets,), jnp.int32)

    index = jnp.stack([exchange_owner[:, 0], exchange_slot, ocean_owner[:, 0], ocean_slot])
    section = lax.axis_index("comp").astype(jnp.int32).reshape(1)
    state = atmos_state.reshape(blocks * rows, width)
    ocean = ocean_state.reshape(sea_blocks * sea_rows, width)

    state_copy = pltpu.VMEM((blocks * rows, width), F32)
    ocean_copy = pltpu.VMEM((sea_blocks * sea_rows, width), F32)
    wet_copy = pltpu.VMEM((sea_rows, width), jnp.int32)
    ocean_flags = pltpu.SemaphoreType.DMA((sea_fields,))
    near_first, near_last, far_first, far_last, first_cols, last_cols = call(
        functools.partial(edges_kernel, at),
        "edges",
        (array(at.near_rows, width),) * 2
        + (array(at.far_rows, width),) * 2
        + (array(at.col_rows, width),) * 2,
        [ANY] * 3,
        [state_copy, ocean_copy, wet_copy, pltpu.SemaphoreType.DMA((fields + 5,))],
        limit=STREAM_LIMIT,
    )(state, ocean, wet_mask)
    north = shifted(near_last, ring, 1)
    south = shifted(near_first, ring, -1)
    west = shifted(last_cols, "gy", 1)
    east = shifted(first_cols, "gy", -1)

    def weights_of(remap, transposed, name, before):
        return call(
            functools.partial(weights_kernel, transposed),
            name,
            jax.ShapeDtypeStruct((rows, 2 * width, width), BF16),
            [VMEM],
            after=(before,),
        )(remap)

    inner = call(
        functools.partial(inner_kernel, at),
        "inner",
        array(fields * rows, width),
        [ANY, SMEM],
        [pltpu.VMEM((fields, 2, rows, width), F32), pltpu.SemaphoreType.DMA],
        after=(first_cols,),
    )(atmos_state, atmos_diffusion)
    pieces = call(
        functools.partial(pieces_kernel, at, targets),
        "pieces",
        array(slots * PIECE_ROWS, width),
        [VMEM] * 6 + [SMEM] * 2,
        [pltpu.VMEM((16 * rows, width), F32), tally],
    )(
        inner,
        north,
        south,
        west,
        east,
        weights_of(remap_atmos, False, "piece_weights", first_cols),
        index,
        atmos_diffusion,
    )
    arrived = lax.all_to_all(
        pieces.reshape(targets, CAPACITY * PIECE_ROWS, width), SECTION, 0, 0, tiled=True
    )
    outgoing, gather, own_labels = call(
        functools.partial(flux_kernel, (fields, sea_fields, rows, targets, sections)),
        "fluxes",
        (
            array(devices * CAPACITY * sea_fields, width),
            array(slots, width),
            array(slots, width),
        ),
        [VMEM, VMEM, SMEM],
        [pltpu.VMEM((sea_fields * rows, width), F32), tally],
    )(
        arrived.reshape(slots * PIECE_ROWS, width),
        remap_ocean,
        index,
    )
    landed = lax.all_to_all(
        outgoing.reshape(devices, CAPACITY * sea_fields, width), EVERY, 0, 0, tiled=True
    )
    other_labels = shifted(own_labels, "comp", 1)
    to_north, to_south = call(
        functools.partial(corners_kernel, at),
        "corners",
        (array(at.far_rows, width),) * 2,
        [VMEM] * 4,
        after=(outgoing,),
    )(far_first, far_last, west, east)
    far_north = shifted(to_south, ring, 1)
    far_south = shifted(to_north, ring, -1)

    sea_base = call(
        functools.partial(ocean_kernel, at, sea_levels),
        "sea_base",
        array(sea_blocks * sea_rows, width),
        [ANY] + [VMEM] * 5 + [SMEM],
        [ocean_copy] * 2 + [pltpu.VMEM((width, width), F32)] * 2 + [ocean_flags] * 2,
        after=(outgoing,),
        limit=STREAM_LIMIT,
        work=1_000_000_000,
        out_specs=ANY,
    )(ocean, wet_mask, north, south, west, east, ocean_mixing)

    ocean_next, answers = call(
        functools.partial(sea_kernel, (sea_fields, sea_rows, targets)),
        "sea_top",
        (
            array(sea_fields, sea_levels, sea_rows, width),
            array(slots * sea_fields, width),
        ),
        [VMEM, ANY, VMEM, VMEM, SMEM, ANY],
        [pltpu.VMEM((sea_fields * sea_rows, width), F32)] * 2
        + [wet_copy, pltpu.SemaphoreType.DMA((sea_fields + 1,)), ocean_flags],
        after=(far_north, far_south),
        out_specs=(ANY, VMEM),
        input_output_aliases={5: 0},
    )(
        landed.reshape(devices * CAPACITY * sea_fields, width),
        wet_mask,
        own_labels,
        other_labels,
        section,
        sea_base.reshape(sea_fields, sea_levels, sea_rows, width),
    )
    answered = lax.all_to_all(
        answers.reshape(targets, CAPACITY * sea_fields, width), SECTION, 0, 0, tiled=True
    )
    def both_steps(part, before, **more):
        return call(
            functools.partial(steps_kernel, at, part),
            "steps_" + "ab"[part],
            array(blocks * rows, width),
            [ANY] + [VMEM] * 10 + [SMEM] + [ANY] * part,
            [pltpu.VMEM((at.part * rows, width), F32)] * 3
            + [pltpu.VMEM((at.part_rows, width), F32)] * 2
            + [pltpu.VMEM((rows, width), F32)] * 2
            + [pltpu.SemaphoreType.DMA((at.half,))] * 2,
            after=(before,),
            limit=STREAM_LIMIT,
            work=1_000_000_000,
            out_specs=ANY,
            **more,
        )

    halos = (north, south, west, east, far_north, far_south)
    halos += (near_first, near_last, first_cols, last_cols)
    atmos_next = both_steps(0, answers)(state, *halos, atmos_diffusion)
    answered, atmos_next = lax.optimization_barrier((answered, atmos_next))

    replies = call(
        functools.partial(reply_kernel, (sea_fields, rows, targets)),
        "replies",
        array(slots * sea_fields, width),
        [VMEM, VMEM, SMEM, VMEM],
        [pltpu.VMEM((sea_fields * rows, width), F32), tally],
    )(
        answered.reshape(slots * sea_fields, width),
        remap_ocean,
        index,
        gather,
    )
    returned = lax.all_to_all(
        replies.reshape(targets, CAPACITY * sea_fields, width), SECTION, 0, 0, tiled=True
    )
    atmos_next = both_steps(1, replies, input_output_aliases={12: 0})(
        state, *halos, atmos_diffusion, atmos_next
    )
    ocean_surface = call(
        functools.partial(surface_kernel, (sea_fields, rows, targets)),
        "surface",
        array(sea_fields * rows, width),
        [VMEM, VMEM, SMEM],
        [tally],
    )(
        returned.reshape(slots * sea_fields, width),
        weights_of(remap_atmos, True, "surface_weights", replies),
        index,
    )
    return (
        atmos_next.reshape(atmos_state.shape),
        ocean_next,
        ocean_surface.reshape(sea_fields, rows, width),
    )


def solution(mesh):
    in_specs = (
        P(None, None, ("comp", "gx"), "gy"),
        P(),
        P(("comp", "gx", "gy"), None, None),
        P(("comp", "gx", "gy"), None),
        P(("comp", "gx", "gy")),
        P(("comp", "gx", "gy"), None, None),
        P(("comp", "gx", "gy"), None),
        P(("comp", "gx", "gy")),
        P(None, None, "gx", "gy"),
        P(),
        P("gx", "gy"),
    )
    out_specs = (
        P(None, None, ("comp", "gx"), "gy"),
        P(None, None, "gx", "gy"),
        P(None, ("comp", "gx"), "gy"),
    )
    return jax.shard_map(
        on_device, mesh=mesh, in_specs=in_specs, out_specs=out_specs, check_vma=False
    )
```

```python
import functools

import jax
import jax.numpy as jnp
from jax import lax
from jax.experimental import pallas as pl
from jax.experimental.pallas import tpu as pltpu
from jax.sharding import PartitionSpec as P

F32 = jnp.float32
BF16 = jnp.bfloat16
FORCING_SCALE = (0.1, -0.1, 0.1, 0.1)
SECTION = ("gx", "gy")
EVERY = ("comp", "gx", "gy")
CAPACITY = 2
PIECE_ROWS = 12
VMEM_LIMIT = 8 * 1024 * 1024
EDGES_LIMIT = 60 * 1024 * 1024
SEA_LIMIT = 53 * 1024 * 1024
STEPS_LIMIT = 53 * 1024 * 1024


def shifted(block, axis, distance):
    devices = range(lax.axis_size(axis))
    route = [((i - distance) % len(devices), i) for i in devices]
    return lax.ppermute(block, axis, route)


def dot(left, right, transposed=False):
    dims = (((1,), (1 if transposed else 0,)), ((), ()))
    return lax.dot_general(left, right, dims, preferred_element_type=F32)


def halves(values):
    high = values.astype(BF16)
    return high, (values - high.astype(F32)).astype(BF16)


def remapped(rows, weights):
    count, width = rows.shape
    high, low = halves(rows)
    if count < 16:
        filler = jnp.zeros((16 - count, width), F32)
        high, low = halves(jnp.concatenate([rows, filler], axis=0))
    left = jnp.concatenate(
        [
            jnp.concatenate([high, high], axis=1),
            jnp.concatenate([low, jnp.zeros(low.shape, BF16)], axis=1),
        ],
        axis=0,
    )
    product = dot(left, weights)
    return product[:count, :] + product[16 : 16 + count, :]


def both_halves(block):
    return jnp.concatenate(halves(block), axis=0)


def weights_kernel(transposed, remap, weights):
    for tile in range(remap.shape[0]):
        block = remap[tile]
        weights[tile] = both_halves(jnp.transpose(block) if transposed else block)


def picked(selection, values):
    chosen = selection.astype(BF16)
    high = values.astype(BF16)
    rest = values - high.astype(F32)
    middle = rest.astype(BF16)
    low = (rest - middle.astype(F32)).astype(BF16)
    return dot(chosen, high) + dot(chosen, middle) + dot(chosen, low)


def one_hot(labels):
    lanes = lax.broadcasted_iota(jnp.int32, labels.shape, 1).astype(F32)
    return (labels == lanes).astype(F32)


def grid_index(shape):
    return lax.broadcasted_iota(jnp.int32, shape, 0), lax.broadcasted_iota(jnp.int32, shape, 1)


def around(cells, north, south, west, east):
    rows, lanes = grid_index(cells.shape)
    row_count, width = cells.shape
    return (
        jnp.where(rows == 0, north, pltpu.roll(cells, 1, 0)),
        jnp.where(rows == row_count - 1, south, pltpu.roll(cells, row_count - 1, 0)),
        jnp.where(lanes == 0, west, pltpu.roll(cells, 1, 1)),
        jnp.where(lanes == width - 1, east, pltpu.roll(cells, width - 1, 1)),
    )


def diffused(cells, upper, lower, sides, diffusion):
    beside = sides[0] + sides[1] + sides[2] + sides[3] - 4.0 * cells
    return cells + diffusion * beside + 0.1 * (upper + lower - 2.0 * cells)


class Edges:
    def __init__(self, fields, levels, rows, sea_blocks, sea_rows, width):
        self.fields, self.levels, self.rows, self.width = fields, levels, rows, width
        self.sea_blocks, self.sea_rows = sea_blocks, sea_rows
        self.half = fields // 2
        self.part = self.half * levels
        self.part_rows = -(-self.part // 8) * 8
        self.atmos_rows = 2 * self.part_rows
        self.wet_row = self.atmos_rows + sea_blocks
        self.near_rows = -(-(self.wet_row + 1) // 8) * 8
        self.corner_row = self.atmos_rows
        self.far_rows = self.atmos_rows + 8
        self.sea_tiles = sea_blocks * sea_rows // width
        self.sea_cols = 4 * rows
        self.sea_col_rows = -(-(self.sea_tiles + 1) // 8) * 8
        self.col_rows = self.sea_cols + self.sea_col_rows


def squared(values):
    rows, width = values.shape
    if rows == width:
        return values
    return jnp.concatenate([values, jnp.zeros((width - rows, width), F32)], axis=0)


def chunk(source, target, at, rows, arrival):
    part = pl.ds(pl.multiple_of(at * rows, 8), rows)
    return pltpu.make_async_copy(source.at[part], target.at[part], arrival)


def edges_kernel(
    at,
    state_far,
    ocean_far,
    wet_far,
    near_first,
    near_last,
    far_first,
    far_last,
    first,
    last,
    state,
    ocean,
    wet,
    arrivals,
):
    rows, part, width = at.rows, at.part, at.width
    field_rows = at.levels * rows
    sea_parts = 4
    copies = [
        chunk(state_far, state, field, field_rows, arrivals.at[field])
        for field in range(at.fields)
    ]
    copies += [
        chunk(ocean_far, ocean, field, ocean.shape[0] // sea_parts, arrivals.at[at.fields + field])
        for field in range(sea_parts)
    ]
    copies.append(pltpu.make_async_copy(wet_far, wet, arrivals.at[at.fields + sea_parts]))
    for copy in copies:
        copy.start()
    for out in (near_first, near_last, far_first, far_last):
        out[...] = jnp.zeros(out.shape, F32)
    for cols in (first, last):
        cols[pl.ds(at.sea_cols, at.sea_col_rows), :] = jnp.zeros((at.sea_col_rows, width), F32)
    for half in range(2):
        for field in range(half * at.half, (half + 1) * at.half):
            copies[field].wait()
        for row in range(rows):
            lines = state[pl.ds(half * part * rows + row, part, stride=rows), :]
            held = pl.ds(half * at.part_rows, part)
            if row < 2:
                (near_first, far_first)[row][held, :] = lines
            if row >= rows - 2:
                (near_last, far_last)[rows - 1 - row][held, :] = lines
            turned = jnp.transpose(squared(lines))
            near, far = half * rows + row, (2 + half) * rows + row
            first[pl.ds(near, 1), :] = turned[0:1, :]
            first[pl.ds(far, 1), :] = turned[1:2, :]
            last[pl.ds(near, 1), :] = turned[width - 1 : width, :]
            last[pl.ds(far, 1), :] = turned[width - 2 : width - 1, :]
    for copy in copies[at.fields :]:
        copy.wait()
    for out, sea_row in ((near_first, 0), (near_last, at.sea_rows - 1)):
        out[pl.ds(at.atmos_rows, at.sea_blocks), :] = ocean[
            pl.ds(sea_row, at.sea_blocks, stride=at.sea_rows), :
        ]
        out[pl.ds(at.wet_row, 1), :] = wet[pl.ds(sea_row, 1), :].astype(F32)
    for tile in range(at.sea_tiles + 1):
        if tile < at.sea_tiles:
            lines = ocean[pl.ds(tile * width, width), :]
        else:
            lines = squared(wet[...].astype(F32))
        turned = jnp.transpose(lines)
        first[pl.ds(at.sea_cols + tile, 1), :] = turned[0:1, :]
        last[pl.ds(at.sea_cols + tile, 1), :] = turned[width - 1 : width, :]


def corners_kernel(at, far_first, far_last, west, east, to_north, to_south):
    for out, lines, row in ((to_north, far_first, 0), (to_south, far_last, at.rows - 1)):
        out[...] = lines[...]
        for place, (cols, half) in enumerate(((west, 0), (west, 1), (east, 0), (east, 1))):
            out[pl.ds(at.corner_row + place, 1), :] = cols[pl.ds(half * at.rows + row, 1), :]


def spread(at, diffusion, part, places):
    numbers = jnp.zeros(places.shape, F32)
    is_first = places < 0
    is_last = places < 0
    for field in range(at.half):
        start = field * at.levels
        numbers = jnp.where(places >= start, diffusion[part * at.half + field], numbers)
        is_first = is_first | (places == start)
        is_last = is_last | (places == start + at.levels - 1)
    return numbers, is_first, is_last


def ring_step(at, part, halos, edges, diffusion, outs):
    north, south, west, east, far_north, far_south = halos
    near_first, near_last, first, last = edges
    rows, width = at.rows, at.width
    shape = (at.part_rows, width)
    held = pl.ds(part * at.part_rows, shape[0])
    lines, lanes = grid_index(shape)
    numbers, is_first, is_last = spread(at, diffusion, part, lines)
    for out, outside, further, own, is_north in (
        (outs[0], north, far_north, near_first, True),
        (outs[1], south, far_south, near_last, False),
    ):
        turned = jnp.transpose(squared(further[pl.ds(at.corner_row, 8), :]))[: shape[0], :]
        cells, beyond, inside = outside[held, :], further[held, :], own[held, :]
        west_col = jnp.where(lanes == 0, turned[:, part : part + 1], pltpu.roll(cells, 1, 1))
        east_col = jnp.where(
            lanes == width - 1, turned[:, 2 + part : 3 + part], pltpu.roll(cells, width - 1, 1)
        )
        sides = (
            beyond if is_north else inside,
            inside if is_north else beyond,
            west_col,
            east_col,
        )
        upper = jnp.where(is_first, cells, pltpu.roll(cells, 1, 0))
        lower = jnp.where(is_last, cells, pltpu.roll(cells, shape[0] - 1, 0))
        out[...] = diffused(cells, upper, lower, sides, numbers)

    shape = (rows, width)
    near, far = pl.ds(part * rows, rows), pl.ds((2 + part) * rows, rows)
    lines, lanes = grid_index(shape)
    numbers, is_first, is_last = spread(at, diffusion, part, lanes)
    for out, outside, own, corner, is_west in (
        (outs[2], west, first, 0, True),
        (outs[3], east, last, 2, False),
    ):
        cells, beyond, inside = outside[near, :], outside[far, :], own[near, :]
        place = pl.ds(at.corner_row + corner + part, 1)
        sides = (
            jnp.where(lines == 0, far_north[place, :], pltpu.roll(cells, 1, 0)),
            jnp.where(lines == rows - 1, far_south[place, :], pltpu.roll(cells, rows - 1, 0)),
            beyond if is_west else inside,
            inside if is_west else beyond,
        )
        upper = jnp.where(is_first, cells, pltpu.roll(cells, 1, 1))
        lower = jnp.where(is_last, cells, pltpu.roll(cells, width - 1, 1))
        out[...] = diffused(cells, upper, lower, sides, numbers)


def field_step(at, field, state, out, north, south, first_line, west_cols, east_cols, number):
    levels, rows, width = at.levels, at.rows, at.width
    lines, lanes = grid_index((rows, width))
    for level in range(levels):
        line = first_line + field * levels + level
        start = pl.multiple_of((field * levels + level) * rows, rows)
        cells = state[pl.ds(start, rows), :]
        first_level, last_level = level == 0, level == levels - 1
        upper = cells if first_level else state[pl.ds(start - rows, rows), :]
        lower = cells if last_level else state[pl.ds(start + rows, rows), :]
        sides = (
            jnp.where(lines == 0, north[pl.ds(line, 1), :], pltpu.roll(cells, 1, 0)),
            jnp.where(
                lines == rows - 1, south[pl.ds(line, 1), :], pltpu.roll(cells, rows - 1, 0)
            ),
            jnp.where(lanes == 0, pltpu.roll(west_cols, (width - level) % width, 1), pltpu.roll(cells, 1, 1)),
            jnp.where(
                lanes == width - 1,
                pltpu.roll(east_cols, width - 1 - level, 1),
                pltpu.roll(cells, width - 1, 1),
            ),
        )
        out[pl.ds(start, rows), :] = diffused(cells, upper, lower, sides, number)


def steps_kernel(
    at,
    part,
    state_far,
    north,
    south,
    west,
    east,
    far_north,
    far_south,
    near_first,
    near_last,
    first,
    last,
    diffusion,
    *rest,
):
    if part:
        rest = rest[1:]
    out_far, state, middle, out, *ring, arrivals, departures = rest
    rows, width, levels = at.rows, at.width, at.levels
    field_rows = levels * rows
    whole = part * at.half

    def coming(field):
        return pltpu.make_async_copy(
            state_far.at[pl.ds(pl.multiple_of((whole + field) * field_rows, 8), field_rows)],
            state.at[pl.ds(pl.multiple_of(field * field_rows, 8), field_rows)],
            arrivals.at[field],
        )

    def going(field):
        return pltpu.make_async_copy(
            out.at[pl.ds(pl.multiple_of(field * field_rows, 8), field_rows)],
            out_far.at[pl.ds(pl.multiple_of((whole + field) * field_rows, 8), field_rows)],
            departures.at[field],
        )

    for field in range(at.half):
        coming(field).start()
    halos = (north, south, west, east, far_north, far_south)
    ring_step(at, part, halos, (near_first, near_last, first, last), diffusion, ring)
    held = pl.ds(part * rows, rows)

    def both_steps(field, carry):
        back = lax.rem(width - field * levels, width)
        number = diffusion[whole + field]
        west_cols = pltpu.roll(west[held, :], back, 1)
        east_cols = pltpu.roll(east[held, :], back, 1)
        coming(field).wait()
        line = part * at.part_rows
        field_step(at, field, state, middle, north, south, line, west_cols, east_cols, number)
        west_cols = pltpu.roll(ring[2][...], back, 1)
        east_cols = pltpu.roll(ring[3][...], back, 1)
        field_step(at, field, middle, out, ring[0], ring[1], 0, west_cols, east_cols, number)
        going(field).start()
        return carry

    lax.fori_loop(0, at.half, both_steps, 0)
    for field in range(at.half):
        going(field).wait()


def ocean_kernel(
    at,
    levels,
    ocean_far,
    wet,
    north,
    south,
    west,
    east,
    mixing,
    out_far,
    tops,
    ocean,
    out,
    wests,
    easts,
    arrivals,
    departures,
):
    fields, field_rows = at.sea_blocks // levels, levels * at.sea_rows
    for field in range(fields):
        chunk(ocean_far, ocean, field, field_rows, arrivals.at[field]).start()
    rows, width = at.sea_rows, at.width
    lines, lanes = grid_index((rows, width))
    per_tile = width // rows
    held = pl.ds(at.sea_cols, at.sea_col_rows)
    wests[...] = jnp.transpose(squared(west[held, :]))
    easts[...] = jnp.transpose(squared(east[held, :]))
    wet_cells = wet[...].astype(F32)
    wet_lane = at.sea_tiles
    wet_sides = around(
        wet_cells,
        north[pl.ds(at.wet_row, 1), :],
        south[pl.ds(at.wet_row, 1), :],
        wests[pl.ds(0, rows), :][:, wet_lane : wet_lane + 1],
        easts[pl.ds(0, rows), :][:, wet_lane : wet_lane + 1],
    )

    def field_step(field, carry):
        chunk(ocean_far, ocean, field, field_rows, arrivals.at[field]).wait()
        back = lax.rem(width - field * (levels // per_tile), width)
        west_cols = pltpu.roll(wests[...], back, 1)
        east_cols = pltpu.roll(easts[...], back, 1)
        number = mixing[field] * wet_cells
        for level in range(levels):
            block = field * levels + level
            start = pl.multiple_of(block * rows, rows)
            first_level, last_level = level == 0, level == levels - 1
            cells = ocean[pl.ds(start, rows), :]
            upper = cells if first_level else ocean[pl.ds(start - rows, rows), :]
            lower = cells if last_level else ocean[pl.ds(start + rows, rows), :]
            above = pltpu.roll(cells, 1, 0)
            below = pltpu.roll(cells, rows - 1, 0)
            line = at.atmos_rows + block
            tile, within = level // per_tile, (level % per_tile) * rows
            west_col = pltpu.roll(west_cols[within : within + rows, :], (width - tile) % width, 1)
            east_col = pltpu.roll(east_cols[within : within + rows, :], width - 1 - tile, 1)
            sides = (
                jnp.where(lines == 0, north[pl.ds(line, 1), :], above),
                jnp.where(lines == rows - 1, south[pl.ds(line, 1), :], below),
                jnp.where(lanes == 0, west_col, pltpu.roll(cells, 1, 1)),
                jnp.where(lanes == width - 1, east_col, pltpu.roll(cells, width - 1, 1)),
            )
            total = wet_sides[0] * (sides[0] - cells)
            for side in range(1, 4):
                total = total + wet_sides[side] * (sides[side] - cells)
            tendency = number * total + 0.1 * (upper + lower - 2.0 * cells)
            after = cells + wet_cells * tendency
            out[pl.ds(start, rows), :] = after
            if first_level:
                tops[pl.ds(pl.multiple_of(field * rows, rows), rows), :] = after
        chunk(out, out_far, field, field_rows, departures.at[field]).start()
        return carry

    lax.fori_loop(0, fields, field_step, 0)
    for field in range(fields):
        chunk(out, out_far, field, field_rows, departures.at[field]).wait()


def routes_kernel(index, own, *rest):
    *outs, section, tally = rest
    lanes = lax.broadcasted_iota(jnp.int32, (1, section.shape[1]), 1)
    section[...] = jnp.full(section.shape, own[0].astype(F32))

    def clear(at, carry):
        tally[at] = 0
        return carry

    for row, (slots, labels, tiles) in ((0, outs[:3]), (2, outs[3:])):
        slots[...] = jnp.zeros(slots.shape, F32)
        labels[...] = jnp.full(labels.shape, -1.0, F32)
        lax.fori_loop(0, tally.shape[0], clear, 0)
        for tile in range(index.shape[1]):
            owner = index[row, tile]
            rank = tally[owner]
            tally[owner] = rank + 1
            slot = pl.ds(owner * CAPACITY + rank, 1)
            slots[slot, :] = (lanes == tile).astype(F32)
            labels[slot, :] = jnp.full(lanes.shape, index[row + 1, tile].astype(F32))
        tiles[...] = jnp.transpose(slots[...])[: tiles.shape[0], :]


def inner_kernel(at, state_far, diffusion, out, numbers, top, arrival):
    fields, rows, width = at.fields, at.rows, at.width
    copy = pltpu.make_async_copy(state_far.at[:, pl.ds(at.levels - 2, 2)], top, arrival)
    copy.start()
    lines, lanes = grid_index((rows, width))
    for field in range(fields):
        numbers[pl.ds(field, 1), :] = jnp.full((1, width), diffusion[field])
    copy.wait()
    for field in range(fields):
        cells = top[field, 1]
        sides = (
            jnp.where(lines == 0, 0.0, pltpu.roll(cells, 1, 0)),
            jnp.where(lines == rows - 1, 0.0, pltpu.roll(cells, rows - 1, 0)),
            jnp.where(lanes == 0, 0.0, pltpu.roll(cells, 1, 1)),
            jnp.where(lanes == width - 1, 0.0, pltpu.roll(cells, width - 1, 1)),
        )
        out[pl.ds(field * rows, rows), :] = diffused(
            cells, top[field, 0], cells, sides, diffusion[field]
        )


def pieces_kernel(
    at, inner, north, south, west, east, weights, numbers, routes, labels, sea_labels, out, *scratch
):
    surface, products = scratch
    fields, levels, rows, width = at.fields, at.levels, at.rows, at.width
    slots = routes.shape[0]
    lines, lanes = grid_index((rows, width))
    for field in range(fields):
        part = field // at.half
        held = pl.ds(part * rows, rows)
        lane = (field % at.half) * levels + levels - 1
        line = pl.ds(part * at.part_rows + lane, 1)
        outside = (
            jnp.where(lines == 0, north[line, :], 0.0)
            + jnp.where(lines == rows - 1, south[line, :], 0.0)
            + jnp.where(lanes == 0, pltpu.roll(west[held, :], (width - lane) % width, 1), 0.0)
            + jnp.where(lanes == width - 1, pltpu.roll(east[held, :], width - 1 - lane, 1), 0.0)
        )
        here = pl.ds(field * rows, rows)
        surface[here, :] = inner[here, :] + numbers[pl.ds(field, 1), :] * outside
    surface[pl.ds(fields * rows, (16 - fields) * rows), :] = jnp.zeros(
        ((16 - fields) * rows, width), F32
    )
    for tile in range(rows):
        products[pl.ds(tile * 16, 16), :] = remapped(
            surface[pl.ds(tile, 16, stride=rows), :], weights[tile]
        )
    sent = picked(
        routes[...][:, :rows],
        jnp.concatenate(
            [products[pl.ds(field, rows, stride=16), :] for field in range(fields)], axis=1
        ),
    )
    for field in range(fields):
        out[pl.ds(field, slots, stride=PIECE_ROWS), :] = sent[:, field * width : (field + 1) * width]
    out[pl.ds(fields, slots, stride=PIECE_ROWS), :] = labels[...]
    out[pl.ds(fields + 1, slots, stride=PIECE_ROWS), :] = sea_labels[...]


def flux_kernel(sizes, arrived, remap, routes, out, gather, sea_labels, fluxes, products):
    fields, flux_count, rows, sections = sizes
    width = out.shape[1]
    slots = routes.shape[0]
    select = one_hot(arrived[pl.ds(fields, slots, stride=PIECE_ROWS), :])
    gather[...] = select
    sea_labels[...] = arrived[pl.ds(fields + 1, slots, stride=PIECE_ROWS), :]
    values = jnp.concatenate(
        [arrived[pl.ds(field, slots, stride=PIECE_ROWS), :] for field in range(fields)], axis=1
    )
    exchange = picked(jnp.transpose(select)[:rows, :], values)
    a = [exchange[:, field * width : (field + 1) * width] for field in range(fields)]
    speed = jnp.sqrt(a[2] * a[2] + a[3] * a[3] + 0.5)
    fluxes[pl.ds(0, rows), :] = speed * (a[0] - a[4]) + a[6] + a[7]
    fluxes[pl.ds(rows, rows), :] = speed * a[1] + a[5] + a[8]
    fluxes[pl.ds(2 * rows, rows), :] = speed * a[2] * (1.0 + 0.2 * jnp.tanh(a[9]))
    fluxes[pl.ds(3 * rows, rows), :] = speed * a[3]
    for tile in range(rows):
        products[pl.ds(tile * flux_count, flux_count), :] = remapped(
            fluxes[pl.ds(tile, flux_count, stride=rows), :], both_halves(remap[tile])
        )
    sent = picked(
        routes[...][:, :rows],
        jnp.concatenate(
            [products[pl.ds(flux, rows, stride=flux_count), :] for flux in range(flux_count)],
            axis=1,
        ),
    )
    for flux in range(flux_count):
        for section in range(sections):
            out[pl.ds(section * slots * flux_count + flux, slots, stride=flux_count), :] = sent[
                :, flux * width : (flux + 1) * width
            ]


def sea_kernel(
    sizes, landed, base_tops, wet, own_labels, other_labels, section, base, out, answers, tops, leave
):
    flux_count, sea_rows = sizes
    width = landed.shape[1]
    slots = own_labels.shape[0]
    mine = one_hot(own_labels[...])
    others = one_hot(other_labels[...])
    is_first = section[0:1, :] == 0.0
    select = jnp.concatenate(
        [jnp.where(is_first, mine, others), jnp.where(is_first, others, mine)], axis=0
    )
    values = jnp.concatenate(
        [landed[pl.ds(flux, 2 * slots, stride=flux_count), :] for flux in range(flux_count)], axis=1
    )
    forcing = picked(jnp.transpose(select)[:sea_rows, :], values)
    wet_cells = wet[...].astype(F32)
    copies = []
    for flux in range(flux_count):
        held = pl.ds(flux * sea_rows, sea_rows)
        tops[held, :] = base_tops[held, :] + wet_cells * (
            FORCING_SCALE[flux] * forcing[:, flux * width : (flux + 1) * width]
        )
        copies.append(pltpu.make_async_copy(tops.at[held], out.at[flux, 0], leave.at[flux]))
        copies[flux].start()
    all_tops = jnp.concatenate(
        [tops[pl.ds(flux * sea_rows, sea_rows), :] for flux in range(flux_count)], axis=1
    )
    reply = picked(mine[:, :sea_rows], all_tops)
    for flux in range(flux_count):
        answers[pl.ds(flux, slots, stride=flux_count), :] = reply[
            :, flux * width : (flux + 1) * width
        ]
    for copy in copies:
        copy.wait()


def tops_of_tiles(returned, tiles, flux_count, scratch):
    rows, slots = tiles.shape
    width = returned.shape[1]
    found = picked(
        tiles[...],
        jnp.concatenate(
            [returned[pl.ds(flux, slots, stride=flux_count), :] for flux in range(flux_count)],
            axis=1,
        ),
    )
    for flux in range(flux_count):
        scratch[pl.ds(flux, rows, stride=flux_count), :] = found[
            :, flux * width : (flux + 1) * width
        ]


def reply_kernel(flux_count, answered, remap, tiles, gather, out, tops, on_exchange):
    rows, slots = tiles.shape
    width = out.shape[1]
    tops_of_tiles(answered, tiles, flux_count, tops)
    for tile in range(rows):
        held = pl.ds(tile * flux_count, flux_count)
        on_exchange[held, :] = remapped(
            tops[held, :], both_halves(jnp.transpose(remap[tile]))
        )
    values = jnp.concatenate(
        [on_exchange[pl.ds(flux, rows, stride=flux_count), :] for flux in range(flux_count)], axis=1
    )
    replies = picked(gather[...][:, :rows], values)
    for flux in range(flux_count):
        out[pl.ds(flux, slots, stride=flux_count), :] = replies[
            :, flux * width : (flux + 1) * width
        ]


def surface_kernel(flux_count, returned, weights, tiles, out, tops):
    rows, _ = tiles.shape
    tops_of_tiles(returned, tiles, flux_count, tops)
    for tile in range(rows):
        out[pl.ds(tile, flux_count, stride=rows), :] = remapped(
            tops[pl.ds(tile * flux_count, flux_count), :], weights[tile]
        )


VMEM = pl.BlockSpec(memory_space=pltpu.VMEM)
SMEM = pl.BlockSpec(memory_space=pltpu.SMEM)
ANY = pl.BlockSpec(memory_space=pl.ANY)


def array(*shape):
    return jax.ShapeDtypeStruct(shape, F32)


def call(kernel, name, outs, in_specs, scratch=(), after=(), limit=VMEM_LIMIT, work=1_000_000, **more):
    def body(*refs):
        kernel(*refs[: len(in_specs)], *refs[len(in_specs) + len(after) :])

    run = pl.pallas_call(
        body,
        name=name,
        out_shape=outs,
        in_specs=list(in_specs) + [ANY] * len(after),
        scratch_shapes=list(scratch),
        compiler_params=pltpu.CompilerParams(vmem_limit_bytes=limit),
        cost_estimate=pl.CostEstimate(flops=0, bytes_accessed=work, transcendentals=0),
        **more,
    )
    return lambda *arguments: run(*arguments, *after)


def gated(values, before):
    return lax.optimization_barrier((values, before))[0]


def on_device(
    atmos_state,
    atmos_diffusion,
    remap_atmos,
    exchange_owner,
    exchange_slot,
    remap_ocean,
    ocean_owner,
    ocean_slot,
    ocean_state,
    ocean_mixing,
    wet_mask,
):
    targets = lax.axis_size(SECTION)
    sections = lax.axis_size("comp")
    devices = targets * sections
    fields, levels, rows, width = atmos_state.shape
    sea_fields, sea_levels, sea_rows, _ = ocean_state.shape
    blocks = fields * levels
    sea_blocks = sea_fields * sea_levels
    at = Edges(fields, levels, rows, sea_blocks, sea_rows, width)
    slots = targets * CAPACITY
    ring = ("comp", "gx")

    index = jnp.stack([exchange_owner[:, 0], exchange_slot, ocean_owner[:, 0], ocean_slot])
    section = lax.axis_index("comp").astype(jnp.int32).reshape(1)
    state = atmos_state.reshape(blocks * rows, width)
    ocean = ocean_state.reshape(sea_blocks * sea_rows, width)

    state_copy = pltpu.VMEM((blocks * rows, width), F32)
    ocean_copy = pltpu.VMEM((sea_blocks * sea_rows, width), F32)
    wet_copy = pltpu.VMEM((sea_rows, width), jnp.int32)
    ocean_flags = pltpu.SemaphoreType.DMA((sea_fields,))
    near_first, near_last, far_first, far_last, first_cols, last_cols = call(
        functools.partial(edges_kernel, at),
        "edges",
        (array(at.near_rows, width),) * 2
        + (array(at.far_rows, width),) * 2
        + (array(at.col_rows, width),) * 2,
        [ANY] * 3,
        [state_copy, ocean_copy, wet_copy, pltpu.SemaphoreType.DMA((fields + 5,))],
        limit=EDGES_LIMIT,
    )(state, ocean, wet_mask)
    north = shifted(near_last, ring, 1)
    south = shifted(near_first, ring, -1)
    west = shifted(last_cols, "gy", 1)
    east = shifted(first_cols, "gy", -1)

    def weights_of(remap, transposed, name, before):
        return call(
            functools.partial(weights_kernel, transposed),
            name,
            jax.ShapeDtypeStruct((rows, 2 * width, width), BF16),
            [VMEM],
        )(gated(remap, before))

    tile_slots, piece_labels, slot_tiles, sea_slots, sea_labels, sea_tiles, here = call(
        routes_kernel,
        "routes",
        ((array(slots, width),) * 2 + (array(rows, slots),)) * 2 + (array(8, width),),
        [SMEM, SMEM],
        [pltpu.SMEM((targets,), jnp.int32)],
    )(gated(index, first_cols), section)
    inner, numbers = call(
        functools.partial(inner_kernel, at),
        "inner",
        (array(fields * rows, width), array(-(-fields // 8) * 8, width)),
        [ANY, SMEM],
        [pltpu.VMEM((fields, 2, rows, width), F32), pltpu.SemaphoreType.DMA],
    )(gated(atmos_state, first_cols), atmos_diffusion)
    pieces = call(
        functools.partial(pieces_kernel, at),
        "pieces",
        array(slots * PIECE_ROWS, width),
        [VMEM] * 10,
        [pltpu.VMEM((16 * rows, width), F32)] * 2,
    )(
        inner,
        north,
        south,
        west,
        east,
        weights_of(remap_atmos, False, "piece_weights", first_cols),
        numbers,
        tile_slots,
        piece_labels,
        sea_labels,
    )
    arrived = lax.all_to_all(
        pieces.reshape(targets, CAPACITY * PIECE_ROWS, width), SECTION, 0, 0, tiled=True
    )
    outgoing, gather, own_labels = call(
        functools.partial(flux_kernel, (fields, sea_fields, rows, sections)),
        "fluxes",
        (
            array(sections * slots * sea_fields, width),
            array(slots, width),
            array(slots, width),
        ),
        [VMEM] * 3,
        [pltpu.VMEM((sea_fields * rows, width), F32)] * 2,
    )(arrived.reshape(slots * PIECE_ROWS, width), remap_ocean, sea_slots)
    landed = lax.all_to_all(
        outgoing.reshape(devices, CAPACITY * sea_fields, width), EVERY, 0, 0, tiled=True
    )
    other_labels = shifted(own_labels, "comp", 1)
    to_north, to_south = call(
        functools.partial(corners_kernel, at),
        "corners",
        (array(at.far_rows, width),) * 2,
        [VMEM] * 4,
        after=(outgoing,),
    )(far_first, far_last, west, east)
    far_north = shifted(to_south, ring, 1)
    far_south = shifted(to_north, ring, -1)

    sea_base, base_tops = call(
        functools.partial(ocean_kernel, at, sea_levels),
        "sea_base",
        (array(sea_blocks * sea_rows, width), array(sea_fields * sea_rows, width)),
        [ANY] + [VMEM] * 5 + [SMEM],
        [ocean_copy] * 2 + [pltpu.VMEM((width, width), F32)] * 2 + [ocean_flags] * 2,
        after=(outgoing,),
        limit=SEA_LIMIT,
        work=1_000_000_000,
        out_specs=(ANY, VMEM),
    )(ocean, wet_mask, north, south, west, east, ocean_mixing)

    ocean_next, answers = call(
        functools.partial(sea_kernel, (sea_fields, sea_rows)),
        "sea_top",
        (
            array(sea_fields, sea_levels, sea_rows, width),
            array(slots * sea_fields, width),
        ),
        [VMEM] * 6 + [ANY],
        [pltpu.VMEM((sea_fields * sea_rows, width), F32), ocean_flags],
        after=(far_north, far_south),
        out_specs=(ANY, VMEM),
        input_output_aliases={6: 0},
    )(
        landed.reshape(devices * CAPACITY * sea_fields, width),
        base_tops,
        wet_mask,
        own_labels,
        other_labels,
        here,
        sea_base.reshape(sea_fields, sea_levels, sea_rows, width),
    )
    answered = lax.all_to_all(
        answers.reshape(targets, CAPACITY * sea_fields, width), SECTION, 0, 0, tiled=True
    )
    def both_steps(part, before, **more):
        return call(
            functools.partial(steps_kernel, at, part),
            "steps_" + "ab"[part],
            array(blocks * rows, width),
            [ANY] + [VMEM] * 10 + [SMEM] + [ANY] * part,
            [pltpu.VMEM((at.part * rows, width), F32)] * 3
            + [pltpu.VMEM((at.part_rows, width), F32)] * 2
            + [pltpu.VMEM((rows, width), F32)] * 2
            + [pltpu.SemaphoreType.DMA((at.half,))] * 2,
            after=(before,),
            limit=STEPS_LIMIT,
            work=1_000_000_000,
            out_specs=ANY,
            **more,
        )

    halos = (north, south, west, east, far_north, far_south)
    halos += (near_first, near_last, first_cols, last_cols)
    atmos_next = both_steps(0, answers)(state, *halos, atmos_diffusion)
    answered, atmos_next = lax.optimization_barrier((answered, atmos_next))

    replies = call(
        functools.partial(reply_kernel, sea_fields),
        "replies",
        array(slots * sea_fields, width),
        [VMEM] * 4,
        [pltpu.VMEM((sea_fields * rows, width), F32)] * 2,
    )(answered.reshape(slots * sea_fields, width), remap_ocean, sea_tiles, gather)
    returned = lax.all_to_all(
        replies.reshape(targets, CAPACITY * sea_fields, width), SECTION, 0, 0, tiled=True
    )
    atmos_next = both_steps(1, replies, input_output_aliases={12: 0})(
        state, *halos, atmos_diffusion, atmos_next
    )
    ocean_surface = call(
        functools.partial(surface_kernel, sea_fields),
        "surface",
        array(sea_fields * rows, width),
        [VMEM] * 3,
        [pltpu.VMEM((sea_fields * rows, width), F32)],
    )(
        returned.reshape(slots * sea_fields, width),
        weights_of(remap_atmos, True, "surface_weights", replies),
        slot_tiles,
    )
    return (
        atmos_next.reshape(atmos_state.shape),
        ocean_next,
        ocean_surface.reshape(sea_fields, rows, width),
    )


def solution(mesh):
    in_specs = (
        P(None, None, ("comp", "gx"), "gy"),
        P(),
        P(("comp", "gx", "gy"), None, None),
        P(("comp", "gx", "gy"), None),
        P(("comp", "gx", "gy")),
        P(("comp", "gx", "gy"), None, None),
        P(("comp", "gx", "gy"), None),
        P(("comp", "gx", "gy")),
        P(None, None, "gx", "gy"),
        P(),
        P("gx", "gy"),
    )
    out_specs = (
        P(None, None, ("comp", "gx"), "gy"),
        P(None, None, "gx", "gy"),
        P(None, ("comp", "gx"), "gy"),
    )
    return jax.shard_map(
        on_device, mesh=mesh, in_specs=in_specs, out_specs=out_specs, check_vma=False
    )
```

```python
import functools

import jax
import jax.numpy as jnp
from jax import lax
from jax.experimental import pallas as pl
from jax.experimental.pallas import tpu as pltpu
from jax.sharding import PartitionSpec as P

F32 = jnp.float32
BF16 = jnp.bfloat16
FORCING_SCALE = (0.1, -0.1, 0.1, 0.1)
SECTION = ("gx", "gy")
EVERY = ("comp", "gx", "gy")
CAPACITY = 2
PIECE_ROWS = 8
VMEM_LIMIT = 8 * 1024 * 1024
EDGES_LIMIT = 60 * 1024 * 1024
SEA_LIMIT = 53 * 1024 * 1024
STEPS_LIMIT = 53 * 1024 * 1024


def shifted(block, axis, distance):
    devices = range(lax.axis_size(axis))
    route = [((i - distance) % len(devices), i) for i in devices]
    return lax.ppermute(block, axis, route)


def dot(left, right, transposed=False):
    dims = (((1,), (1 if transposed else 0,)), ((), ()))
    return lax.dot_general(left, right, dims, preferred_element_type=F32)


def halves(values):
    high = values.astype(BF16)
    return high, (values - high.astype(F32)).astype(BF16)


def remapped(rows, weights):
    count, width = rows.shape
    high, low = halves(rows)
    if count < 16:
        filler = jnp.zeros((16 - count, width), F32)
        high, low = halves(jnp.concatenate([rows, filler], axis=0))
    left = jnp.concatenate(
        [
            jnp.concatenate([high, high], axis=1),
            jnp.concatenate([low, jnp.zeros(low.shape, BF16)], axis=1),
        ],
        axis=0,
    )
    product = dot(left, weights)
    return product[:count, :] + product[16 : 16 + count, :]


def both_halves(block):
    return jnp.concatenate(halves(block), axis=0)


def weights_kernel(transposed, remap, weights):
    for tile in range(remap.shape[0]):
        block = remap[tile]
        weights[tile] = both_halves(jnp.transpose(block) if transposed else block)


def picked(selection, values):
    chosen = selection.astype(BF16)
    high = values.astype(BF16)
    rest = values - high.astype(F32)
    middle = rest.astype(BF16)
    low = (rest - middle.astype(F32)).astype(BF16)
    return dot(chosen, high) + dot(chosen, middle) + dot(chosen, low)


def one_hot(labels):
    lanes = lax.broadcasted_iota(jnp.int32, labels.shape, 1).astype(F32)
    return (labels == lanes).astype(F32)


def grid_index(shape):
    return lax.broadcasted_iota(jnp.int32, shape, 0), lax.broadcasted_iota(jnp.int32, shape, 1)


def around(cells, north, south, west, east):
    rows, lanes = grid_index(cells.shape)
    row_count, width = cells.shape
    return (
        jnp.where(rows == 0, north, pltpu.roll(cells, 1, 0)),
        jnp.where(rows == row_count - 1, south, pltpu.roll(cells, row_count - 1, 0)),
        jnp.where(lanes == 0, west, pltpu.roll(cells, 1, 1)),
        jnp.where(lanes == width - 1, east, pltpu.roll(cells, width - 1, 1)),
    )


def diffused(cells, upper, lower, sides, diffusion):
    beside = sides[0] + sides[1] + sides[2] + sides[3] - 4.0 * cells
    return cells + diffusion * beside + 0.1 * (upper + lower - 2.0 * cells)


class Edges:
    def __init__(self, fields, levels, rows, sea_blocks, sea_rows, width):
        self.fields, self.levels, self.rows, self.width = fields, levels, rows, width
        self.sea_blocks, self.sea_rows = sea_blocks, sea_rows
        self.half = fields // 2
        self.part = self.half * levels
        self.part_rows = -(-self.part // 8) * 8
        self.atmos_rows = 2 * self.part_rows
        self.wet_row = self.atmos_rows + sea_blocks
        self.near_rows = -(-(self.wet_row + 1) // 8) * 8
        self.corner_row = self.atmos_rows
        self.far_rows = self.atmos_rows + 8
        self.sea_tiles = sea_blocks * sea_rows // width
        self.sea_cols = 4 * rows
        self.sea_col_rows = -(-(self.sea_tiles + 1) // 8) * 8
        self.col_rows = self.sea_cols + self.sea_col_rows


def squared(values):
    rows, width = values.shape
    if rows == width:
        return values
    return jnp.concatenate([values, jnp.zeros((width - rows, width), F32)], axis=0)


def chunk(source, target, at, rows, arrival):
    part = pl.ds(pl.multiple_of(at * rows, 8), rows)
    return pltpu.make_async_copy(source.at[part], target.at[part], arrival)


def edges_kernel(
    at,
    state_far,
    ocean_far,
    wet_far,
    near_first,
    near_last,
    far_first,
    far_last,
    first,
    last,
    state,
    ocean,
    wet,
    arrivals,
):
    rows, part, width = at.rows, at.part, at.width
    field_rows = at.levels * rows
    sea_parts = 4
    copies = [
        chunk(state_far, state, field, field_rows, arrivals.at[field])
        for field in range(at.fields)
    ]
    copies += [
        chunk(ocean_far, ocean, field, ocean.shape[0] // sea_parts, arrivals.at[at.fields + field])
        for field in range(sea_parts)
    ]
    copies.append(pltpu.make_async_copy(wet_far, wet, arrivals.at[at.fields + sea_parts]))
    for copy in copies:
        copy.start()
    for out in (near_first, near_last, far_first, far_last):
        out[...] = jnp.zeros(out.shape, F32)
    for cols in (first, last):
        cols[pl.ds(at.sea_cols, at.sea_col_rows), :] = jnp.zeros((at.sea_col_rows, width), F32)
    for half in range(2):
        for field in range(half * at.half, (half + 1) * at.half):
            copies[field].wait()
        for row in range(rows):
            lines = state[pl.ds(half * part * rows + row, part, stride=rows), :]
            held = pl.ds(half * at.part_rows, part)
            if row < 2:
                (near_first, far_first)[row][held, :] = lines
            if row >= rows - 2:
                (near_last, far_last)[rows - 1 - row][held, :] = lines
            turned = jnp.transpose(squared(lines))
            near, far = half * rows + row, (2 + half) * rows + row
            first[pl.ds(near, 1), :] = turned[0:1, :]
            first[pl.ds(far, 1), :] = turned[1:2, :]
            last[pl.ds(near, 1), :] = turned[width - 1 : width, :]
            last[pl.ds(far, 1), :] = turned[width - 2 : width - 1, :]
    for copy in copies[at.fields :]:
        copy.wait()
    for out, sea_row in ((near_first, 0), (near_last, at.sea_rows - 1)):
        out[pl.ds(at.atmos_rows, at.sea_blocks), :] = ocean[
            pl.ds(sea_row, at.sea_blocks, stride=at.sea_rows), :
        ]
        out[pl.ds(at.wet_row, 1), :] = wet[pl.ds(sea_row, 1), :].astype(F32)
    for tile in range(at.sea_tiles + 1):
        if tile < at.sea_tiles:
            lines = ocean[pl.ds(tile * width, width), :]
        else:
            lines = squared(wet[...].astype(F32))
        turned = jnp.transpose(lines)
        first[pl.ds(at.sea_cols + tile, 1), :] = turned[0:1, :]
        last[pl.ds(at.sea_cols + tile, 1), :] = turned[width - 1 : width, :]


def corners_kernel(at, far_first, far_last, west, east, to_north, to_south):
    for out, lines, row in ((to_north, far_first, 0), (to_south, far_last, at.rows - 1)):
        out[...] = lines[...]
        for place, (cols, half) in enumerate(((west, 0), (west, 1), (east, 0), (east, 1))):
            out[pl.ds(at.corner_row + place, 1), :] = cols[pl.ds(half * at.rows + row, 1), :]


def spread(at, diffusion, part, places):
    numbers = jnp.zeros(places.shape, F32)
    is_first = places < 0
    is_last = places < 0
    for field in range(at.half):
        start = field * at.levels
        numbers = jnp.where(places >= start, diffusion[part * at.half + field], numbers)
        is_first = is_first | (places == start)
        is_last = is_last | (places == start + at.levels - 1)
    return numbers, is_first, is_last


def ring_step(at, part, halos, edges, diffusion, outs):
    north, south, west, east, far_north, far_south = halos
    near_first, near_last, first, last = edges
    rows, width = at.rows, at.width
    shape = (at.part_rows, width)
    held = pl.ds(part * at.part_rows, shape[0])
    lines, lanes = grid_index(shape)
    numbers, is_first, is_last = spread(at, diffusion, part, lines)
    for out, outside, further, own, is_north in (
        (outs[0], north, far_north, near_first, True),
        (outs[1], south, far_south, near_last, False),
    ):
        turned = jnp.transpose(squared(further[pl.ds(at.corner_row, 8), :]))[: shape[0], :]
        cells, beyond, inside = outside[held, :], further[held, :], own[held, :]
        west_col = jnp.where(lanes == 0, turned[:, part : part + 1], pltpu.roll(cells, 1, 1))
        east_col = jnp.where(
            lanes == width - 1, turned[:, 2 + part : 3 + part], pltpu.roll(cells, width - 1, 1)
        )
        sides = (
            beyond if is_north else inside,
            inside if is_north else beyond,
            west_col,
            east_col,
        )
        upper = jnp.where(is_first, cells, pltpu.roll(cells, 1, 0))
        lower = jnp.where(is_last, cells, pltpu.roll(cells, shape[0] - 1, 0))
        out[...] = diffused(cells, upper, lower, sides, numbers)

    shape = (rows, width)
    near, far = pl.ds(part * rows, rows), pl.ds((2 + part) * rows, rows)
    lines, lanes = grid_index(shape)
    numbers, is_first, is_last = spread(at, diffusion, part, lanes)
    for out, outside, own, corner, is_west in (
        (outs[2], west, first, 0, True),
        (outs[3], east, last, 2, False),
    ):
        cells, beyond, inside = outside[near, :], outside[far, :], own[near, :]
        place = pl.ds(at.corner_row + corner + part, 1)
        sides = (
            jnp.where(lines == 0, far_north[place, :], pltpu.roll(cells, 1, 0)),
            jnp.where(lines == rows - 1, far_south[place, :], pltpu.roll(cells, rows - 1, 0)),
            beyond if is_west else inside,
            inside if is_west else beyond,
        )
        upper = jnp.where(is_first, cells, pltpu.roll(cells, 1, 1))
        lower = jnp.where(is_last, cells, pltpu.roll(cells, width - 1, 1))
        out[...] = diffused(cells, upper, lower, sides, numbers)


def field_step(at, field, state, out, north, south, first_line, west_cols, east_cols, number):
    levels, rows, width = at.levels, at.rows, at.width
    lines, lanes = grid_index((rows, width))
    for level in range(levels):
        line = first_line + field * levels + level
        start = pl.multiple_of((field * levels + level) * rows, rows)
        cells = state[pl.ds(start, rows), :]
        first_level, last_level = level == 0, level == levels - 1
        upper = cells if first_level else state[pl.ds(start - rows, rows), :]
        lower = cells if last_level else state[pl.ds(start + rows, rows), :]
        sides = (
            jnp.where(lines == 0, north[pl.ds(line, 1), :], pltpu.roll(cells, 1, 0)),
            jnp.where(
                lines == rows - 1, south[pl.ds(line, 1), :], pltpu.roll(cells, rows - 1, 0)
            ),
            jnp.where(lanes == 0, pltpu.roll(west_cols, (width - level) % width, 1), pltpu.roll(cells, 1, 1)),
            jnp.where(
                lanes == width - 1,
                pltpu.roll(east_cols, width - 1 - level, 1),
                pltpu.roll(cells, width - 1, 1),
            ),
        )
        out[pl.ds(start, rows), :] = diffused(cells, upper, lower, sides, number)


def steps_kernel(
    at,
    part,
    state_far,
    north,
    south,
    west,
    east,
    far_north,
    far_south,
    near_first,
    near_last,
    first,
    last,
    diffusion,
    *rest,
):
    if part:
        rest = rest[1:]
    out_far, state, middle, out, *ring, arrivals, departures = rest
    rows, width, levels = at.rows, at.width, at.levels
    field_rows = levels * rows
    whole = part * at.half

    def coming(field):
        return pltpu.make_async_copy(
            state_far.at[pl.ds(pl.multiple_of((whole + field) * field_rows, 8), field_rows)],
            state.at[pl.ds(pl.multiple_of(field * field_rows, 8), field_rows)],
            arrivals.at[field],
        )

    def going(field):
        return pltpu.make_async_copy(
            out.at[pl.ds(pl.multiple_of(field * field_rows, 8), field_rows)],
            out_far.at[pl.ds(pl.multiple_of((whole + field) * field_rows, 8), field_rows)],
            departures.at[field],
        )

    for field in range(at.half):
        coming(field).start()
    halos = (north, south, west, east, far_north, far_south)
    ring_step(at, part, halos, (near_first, near_last, first, last), diffusion, ring)
    held = pl.ds(part * rows, rows)

    def both_steps(field, carry):
        back = lax.rem(width - field * levels, width)
        number = diffusion[whole + field]
        west_cols = pltpu.roll(west[held, :], back, 1)
        east_cols = pltpu.roll(east[held, :], back, 1)
        coming(field).wait()
        line = part * at.part_rows
        field_step(at, field, state, middle, north, south, line, west_cols, east_cols, number)
        west_cols = pltpu.roll(ring[2][...], back, 1)
        east_cols = pltpu.roll(ring[3][...], back, 1)
        field_step(at, field, middle, out, ring[0], ring[1], 0, west_cols, east_cols, number)
        going(field).start()
        return carry

    lax.fori_loop(0, at.half, both_steps, 0)
    for field in range(at.half):
        going(field).wait()


def ocean_kernel(
    at,
    levels,
    ocean_far,
    wet,
    north,
    south,
    west,
    east,
    mixing,
    out_far,
    tops,
    ocean,
    out,
    wests,
    easts,
    arrivals,
    departures,
):
    fields, field_rows = at.sea_blocks // levels, levels * at.sea_rows
    for field in range(fields):
        chunk(ocean_far, ocean, field, field_rows, arrivals.at[field]).start()
    rows, width = at.sea_rows, at.width
    lines, lanes = grid_index((rows, width))
    per_tile = width // rows
    held = pl.ds(at.sea_cols, at.sea_col_rows)
    wests[...] = jnp.transpose(squared(west[held, :]))
    easts[...] = jnp.transpose(squared(east[held, :]))
    wet_cells = wet[...].astype(F32)
    wet_lane = at.sea_tiles
    wet_sides = around(
        wet_cells,
        north[pl.ds(at.wet_row, 1), :],
        south[pl.ds(at.wet_row, 1), :],
        wests[pl.ds(0, rows), :][:, wet_lane : wet_lane + 1],
        easts[pl.ds(0, rows), :][:, wet_lane : wet_lane + 1],
    )

    def field_step(field, carry):
        chunk(ocean_far, ocean, field, field_rows, arrivals.at[field]).wait()
        back = lax.rem(width - field * (levels // per_tile), width)
        west_cols = pltpu.roll(wests[...], back, 1)
        east_cols = pltpu.roll(easts[...], back, 1)
        number = mixing[field] * wet_cells
        for level in range(levels):
            block = field * levels + level
            start = pl.multiple_of(block * rows, rows)
            first_level, last_level = level == 0, level == levels - 1
            cells = ocean[pl.ds(start, rows), :]
            upper = cells if first_level else ocean[pl.ds(start - rows, rows), :]
            lower = cells if last_level else ocean[pl.ds(start + rows, rows), :]
            above = pltpu.roll(cells, 1, 0)
            below = pltpu.roll(cells, rows - 1, 0)
            line = at.atmos_rows + block
            tile, within = level // per_tile, (level % per_tile) * rows
            west_col = pltpu.roll(west_cols[within : within + rows, :], (width - tile) % width, 1)
            east_col = pltpu.roll(east_cols[within : within + rows, :], width - 1 - tile, 1)
            sides = (
                jnp.where(lines == 0, north[pl.ds(line, 1), :], above),
                jnp.where(lines == rows - 1, south[pl.ds(line, 1), :], below),
                jnp.where(lanes == 0, west_col, pltpu.roll(cells, 1, 1)),
                jnp.where(lanes == width - 1, east_col, pltpu.roll(cells, width - 1, 1)),
            )
            total = wet_sides[0] * (sides[0] - cells)
            for side in range(1, 4):
                total = total + wet_sides[side] * (sides[side] - cells)
            tendency = number * total + 0.1 * (upper + lower - 2.0 * cells)
            after = cells + wet_cells * tendency
            out[pl.ds(start, rows), :] = after
            if first_level:
                tops[pl.ds(pl.multiple_of(field * rows, rows), rows), :] = after
        chunk(out, out_far, field, field_rows, departures.at[field]).start()
        return carry

    lax.fori_loop(0, fields, field_step, 0)
    for field in range(fields):
        chunk(out, out_far, field, field_rows, departures.at[field]).wait()


def label_base(rows):
    return 2.0 * rows


def routes_kernel(index, own, diffusion, *rest):
    *outs, labels_out, section, numbers, tally, piece_labels, sea_labels = rest
    lanes = lax.broadcasted_iota(jnp.int32, (1, section.shape[1]), 1)
    section[...] = jnp.full(section.shape, own[0].astype(F32))
    for field in range(diffusion.shape[0]):
        numbers[pl.ds(field, 1), :] = jnp.full(lanes.shape, diffusion[field])

    def clear(at, carry):
        tally[at] = 0
        return carry

    for row, slots, labels in ((0, outs[0], piece_labels), (2, outs[1], sea_labels)):
        slots[...] = jnp.zeros(slots.shape, F32)
        labels[...] = jnp.full(labels.shape, -1.0, F32)
        lax.fori_loop(0, tally.shape[0], clear, 0)
        for tile in range(index.shape[1]):
            owner = index[row, tile]
            rank = tally[owner]
            tally[owner] = rank + 1
            slot = pl.ds(owner * CAPACITY + rank, 1)
            slots[slot, :] = (lanes == tile).astype(F32)
            labels[slot, :] = jnp.full(lanes.shape, index[row + 1, tile].astype(F32))
    base = label_base(index.shape[1])
    labels_out[...] = (piece_labels[...] + 1.0) + base * (sea_labels[...] + 1.0)


def inner_kernel(at, state_far, numbers, out, top, arrival):
    fields, rows, width = at.fields, at.rows, at.width
    copy = pltpu.make_async_copy(state_far.at[:, pl.ds(at.levels - 2, 2)], top, arrival)
    copy.start()
    lines, lanes = grid_index((rows, width))
    copy.wait()
    for field in range(fields):
        cells = top[field, 1]
        sides = (
            jnp.where(lines == 0, 0.0, pltpu.roll(cells, 1, 0)),
            jnp.where(lines == rows - 1, 0.0, pltpu.roll(cells, rows - 1, 0)),
            jnp.where(lanes == 0, 0.0, pltpu.roll(cells, 1, 1)),
            jnp.where(lanes == width - 1, 0.0, pltpu.roll(cells, width - 1, 1)),
        )
        out[pl.ds(field * rows, rows), :] = diffused(
            cells, top[field, 0], cells, sides, numbers[pl.ds(field, 1), :]
        )


def pieces_kernel(
    at, inner, north, south, west, east, weights, numbers, routes, labels, out, surface, products
):
    fields, levels, rows, width = at.fields, at.levels, at.rows, at.width
    slots = routes.shape[0]
    lines, lanes = grid_index((rows, width))
    a = []
    for field in range(fields):
        part = field // at.half
        held = pl.ds(part * rows, rows)
        lane = (field % at.half) * levels + levels - 1
        line = pl.ds(part * at.part_rows + lane, 1)
        outside = (
            jnp.where(lines == 0, north[line, :], 0.0)
            + jnp.where(lines == rows - 1, south[line, :], 0.0)
            + jnp.where(lanes == 0, pltpu.roll(west[held, :], (width - lane) % width, 1), 0.0)
            + jnp.where(lanes == width - 1, pltpu.roll(east[held, :], width - 1 - lane, 1), 0.0)
        )
        a.append(inner[pl.ds(field * rows, rows), :] + numbers[pl.ds(field, 1), :] * outside)
    sums = (a[0] - a[4], a[1], a[2], a[3], a[6] + a[7], a[5] + a[8], a[9])
    for place in range(16):
        surface[pl.ds(place * rows, rows), :] = (
            sums[place] if place < len(sums) else jnp.zeros((rows, width), F32)
        )
    for tile in range(rows):
        products[pl.ds(tile * 16, 16), :] = remapped(
            surface[pl.ds(tile, 16, stride=rows), :], weights[tile]
        )
    count = PIECE_ROWS - 1
    sent = picked(
        routes[...][:, :rows],
        jnp.concatenate(
            [products[pl.ds(place, rows, stride=16), :] for place in range(count)], axis=1
        ),
    )
    for place in range(count):
        out[pl.ds(place, slots, stride=PIECE_ROWS), :] = sent[:, place * width : (place + 1) * width]
    out[pl.ds(count, slots, stride=PIECE_ROWS), :] = labels[...]


def flux_kernel(sizes, arrived, remap, routes, out, gather, sea_labels, fluxes, products):
    flux_count, rows, sections = sizes
    width = out.shape[1]
    slots = routes.shape[0]
    count = PIECE_ROWS - 1
    labels = arrived[pl.ds(count, slots, stride=PIECE_ROWS), :]
    upper = jnp.floor(labels * (1.0 / label_base(rows)))
    select = one_hot(labels - label_base(rows) * upper - 1.0)
    gather[...] = select
    sea_labels[...] = upper - 1.0
    values = jnp.concatenate(
        [arrived[pl.ds(place, slots, stride=PIECE_ROWS), :] for place in range(count)], axis=1
    )
    exchange = picked(jnp.transpose(select)[:rows, :], values)
    a04, a1, a2, a3, a67, a58, a9 = (
        exchange[:, place * width : (place + 1) * width] for place in range(count)
    )
    speed = jnp.sqrt(a2 * a2 + a3 * a3 + 0.5)
    fluxes[pl.ds(0, rows), :] = speed * a04 + a67
    fluxes[pl.ds(rows, rows), :] = speed * a1 + a58
    fluxes[pl.ds(2 * rows, rows), :] = speed * a2 * (1.0 + 0.2 * jnp.tanh(a9))
    fluxes[pl.ds(3 * rows, rows), :] = speed * a3
    for tile in range(rows):
        products[pl.ds(tile * flux_count, flux_count), :] = remapped(
            fluxes[pl.ds(tile, flux_count, stride=rows), :], both_halves(remap[tile])
        )
    sent = picked(
        routes[...][:, :rows],
        jnp.concatenate(
            [products[pl.ds(flux, rows, stride=flux_count), :] for flux in range(flux_count)],
            axis=1,
        ),
    )
    for flux in range(flux_count):
        for section in range(sections):
            out[pl.ds(section * slots * flux_count + flux, slots, stride=flux_count), :] = sent[
                :, flux * width : (flux + 1) * width
            ]


def sea_kernel(
    sizes, landed, base_tops, wet, own_labels, other_labels, section, base, out, answers, tops, leave
):
    flux_count, sea_rows = sizes
    width = landed.shape[1]
    slots = own_labels.shape[0]
    mine = one_hot(own_labels[...])
    others = one_hot(other_labels[...])
    is_first = section[0:1, :] == 0.0
    select = jnp.concatenate(
        [jnp.where(is_first, mine, others), jnp.where(is_first, others, mine)], axis=0
    )
    values = jnp.concatenate(
        [landed[pl.ds(flux, 2 * slots, stride=flux_count), :] for flux in range(flux_count)], axis=1
    )
    forcing = picked(jnp.transpose(select)[:sea_rows, :], values)
    wet_cells = wet[...].astype(F32)
    copies = []
    for flux in range(flux_count):
        held = pl.ds(flux * sea_rows, sea_rows)
        tops[held, :] = base_tops[held, :] + wet_cells * (
            FORCING_SCALE[flux] * forcing[:, flux * width : (flux + 1) * width]
        )
        copies.append(pltpu.make_async_copy(tops.at[held], out.at[flux, 0], leave.at[flux]))
        copies[flux].start()
    all_tops = jnp.concatenate(
        [tops[pl.ds(flux * sea_rows, sea_rows), :] for flux in range(flux_count)], axis=1
    )
    reply = picked(mine[:, :sea_rows], all_tops)
    for flux in range(flux_count):
        answers[pl.ds(flux, slots, stride=flux_count), :] = reply[
            :, flux * width : (flux + 1) * width
        ]
    for copy in copies:
        copy.wait()


def tops_of_tiles(returned, routes, flux_count, scratch):
    slots, width = routes.shape
    rows = scratch.shape[0] // flux_count
    found = picked(
        jnp.transpose(routes[...])[:rows, :],
        jnp.concatenate(
            [returned[pl.ds(flux, slots, stride=flux_count), :] for flux in range(flux_count)],
            axis=1,
        ),
    )
    for flux in range(flux_count):
        scratch[pl.ds(flux, rows, stride=flux_count), :] = found[
            :, flux * width : (flux + 1) * width
        ]


def reply_kernel(flux_count, answered, remap, routes, gather, out, tops, on_exchange):
    slots, width = routes.shape
    rows = remap.shape[0]
    tops_of_tiles(answered, routes, flux_count, tops)
    for tile in range(rows):
        held = pl.ds(tile * flux_count, flux_count)
        on_exchange[held, :] = remapped(
            tops[held, :], both_halves(jnp.transpose(remap[tile]))
        )
    values = jnp.concatenate(
        [on_exchange[pl.ds(flux, rows, stride=flux_count), :] for flux in range(flux_count)], axis=1
    )
    replies = picked(gather[...][:, :rows], values)
    for flux in range(flux_count):
        out[pl.ds(flux, slots, stride=flux_count), :] = replies[
            :, flux * width : (flux + 1) * width
        ]


def surface_kernel(flux_count, returned, weights, routes, out, tops):
    rows = weights.shape[0]
    tops_of_tiles(returned, routes, flux_count, tops)
    for tile in range(rows):
        out[pl.ds(tile, flux_count, stride=rows), :] = remapped(
            tops[pl.ds(tile * flux_count, flux_count), :], weights[tile]
        )


VMEM = pl.BlockSpec(memory_space=pltpu.VMEM)
SMEM = pl.BlockSpec(memory_space=pltpu.SMEM)
ANY = pl.BlockSpec(memory_space=pl.ANY)


def array(*shape):
    return jax.ShapeDtypeStruct(shape, F32)


def call(kernel, name, outs, in_specs, scratch=(), after=(), limit=VMEM_LIMIT, work=1_000_000, **more):
    def body(*refs):
        kernel(*refs[: len(in_specs)], *refs[len(in_specs) + len(after) :])

    run = pl.pallas_call(
        body,
        name=name,
        out_shape=outs,
        in_specs=list(in_specs) + [ANY] * len(after),
        scratch_shapes=list(scratch),
        compiler_params=pltpu.CompilerParams(vmem_limit_bytes=limit),
        cost_estimate=pl.CostEstimate(flops=0, bytes_accessed=work, transcendentals=0),
        **more,
    )
    return lambda *arguments: run(*arguments, *after)


def gated(values, before):
    return lax.optimization_barrier((values, before))[0]


def on_device(
    atmos_state,
    atmos_diffusion,
    remap_atmos,
    exchange_owner,
    exchange_slot,
    remap_ocean,
    ocean_owner,
    ocean_slot,
    ocean_state,
    ocean_mixing,
    wet_mask,
):
    targets = lax.axis_size(SECTION)
    sections = lax.axis_size("comp")
    devices = targets * sections
    fields, levels, rows, width = atmos_state.shape
    sea_fields, sea_levels, sea_rows, _ = ocean_state.shape
    blocks = fields * levels
    sea_blocks = sea_fields * sea_levels
    at = Edges(fields, levels, rows, sea_blocks, sea_rows, width)
    slots = targets * CAPACITY
    ring = ("comp", "gx")

    index = jnp.stack([exchange_owner[:, 0], exchange_slot, ocean_owner[:, 0], ocean_slot])
    section = lax.axis_index("comp").astype(jnp.int32).reshape(1)
    state = atmos_state.reshape(blocks * rows, width)
    ocean = ocean_state.reshape(sea_blocks * sea_rows, width)

    state_copy = pltpu.VMEM((blocks * rows, width), F32)
    ocean_copy = pltpu.VMEM((sea_blocks * sea_rows, width), F32)
    wet_copy = pltpu.VMEM((sea_rows, width), jnp.int32)
    ocean_flags = pltpu.SemaphoreType.DMA((sea_fields,))
    near_first, near_last, far_first, far_last, first_cols, last_cols = call(
        functools.partial(edges_kernel, at),
        "edges",
        (array(at.near_rows, width),) * 2
        + (array(at.far_rows, width),) * 2
        + (array(at.col_rows, width),) * 2,
        [ANY] * 3,
        [state_copy, ocean_copy, wet_copy, pltpu.SemaphoreType.DMA((fields + 5,))],
        limit=EDGES_LIMIT,
    )(state, ocean, wet_mask)
    north = shifted(near_last, ring, 1)
    south = shifted(near_first, ring, -1)
    west = shifted(last_cols, "gy", 1)
    east = shifted(first_cols, "gy", -1)

    def weights_of(remap, transposed, name, before):
        return call(
            functools.partial(weights_kernel, transposed),
            name,
            jax.ShapeDtypeStruct((rows, 2 * width, width), BF16),
            [VMEM],
        )(gated(remap, before))

    tile_slots, sea_slots, labels, here, numbers = call(
        routes_kernel,
        "routes",
        (array(slots, width),) * 3 + (array(8, width), array(-(-fields // 8) * 8, width)),
        [SMEM] * 3,
        [pltpu.SMEM((targets,), jnp.int32)] + [pltpu.VMEM((slots, width), F32)] * 2,
    )(gated(index, first_cols), section, atmos_diffusion)
    inner = call(
        functools.partial(inner_kernel, at),
        "inner",
        array(fields * rows, width),
        [ANY, VMEM],
        [pltpu.VMEM((fields, 2, rows, width), F32), pltpu.SemaphoreType.DMA],
    )(gated(atmos_state, first_cols), numbers)
    pieces = call(
        functools.partial(pieces_kernel, at),
        "pieces",
        array(slots * PIECE_ROWS, width),
        [VMEM] * 9,
        [pltpu.VMEM((16 * rows, width), F32)] * 2,
    )(
        inner,
        north,
        south,
        west,
        east,
        weights_of(remap_atmos, False, "piece_weights", first_cols),
        numbers,
        tile_slots,
        labels,
    )
    arrived = lax.all_to_all(
        pieces.reshape(targets, CAPACITY * PIECE_ROWS, width), SECTION, 0, 0, tiled=True
    )
    outgoing, gather, own_labels = call(
        functools.partial(flux_kernel, (sea_fields, rows, sections)),
        "fluxes",
        (
            array(sections * slots * sea_fields, width),
            array(slots, width),
            array(slots, width),
        ),
        [VMEM] * 3,
        [pltpu.VMEM((sea_fields * rows, width), F32)] * 2,
    )(arrived.reshape(slots * PIECE_ROWS, width), remap_ocean, sea_slots)
    landed = lax.all_to_all(
        outgoing.reshape(devices, CAPACITY * sea_fields, width), EVERY, 0, 0, tiled=True
    )
    other_labels = shifted(own_labels, "comp", 1)
    to_north, to_south = call(
        functools.partial(corners_kernel, at),
        "corners",
        (array(at.far_rows, width),) * 2,
        [VMEM] * 4,
        after=(outgoing,),
    )(far_first, far_last, west, east)
    far_north = shifted(to_south, ring, 1)
    far_south = shifted(to_north, ring, -1)

    sea_base, base_tops = call(
        functools.partial(ocean_kernel, at, sea_levels),
        "sea_base",
        (array(sea_blocks * sea_rows, width), array(sea_fields * sea_rows, width)),
        [ANY] + [VMEM] * 5 + [SMEM],
        [ocean_copy] * 2 + [pltpu.VMEM((width, width), F32)] * 2 + [ocean_flags] * 2,
        after=(outgoing,),
        limit=SEA_LIMIT,
        work=1_000_000_000,
        out_specs=(ANY, VMEM),
    )(ocean, wet_mask, north, south, west, east, ocean_mixing)

    ocean_next, answers = call(
        functools.partial(sea_kernel, (sea_fields, sea_rows)),
        "sea_top",
        (
            array(sea_fields, sea_levels, sea_rows, width),
            array(slots * sea_fields, width),
        ),
        [VMEM] * 6 + [ANY],
        [pltpu.VMEM((sea_fields * sea_rows, width), F32), ocean_flags],
        after=(far_north, far_south),
        out_specs=(ANY, VMEM),
        input_output_aliases={6: 0},
    )(
        landed.reshape(devices * CAPACITY * sea_fields, width),
        base_tops,
        wet_mask,
        own_labels,
        other_labels,
        here,
        sea_base.reshape(sea_fields, sea_levels, sea_rows, width),
    )
    answered = lax.all_to_all(
        answers.reshape(targets, CAPACITY * sea_fields, width), SECTION, 0, 0, tiled=True
    )
    def both_steps(part, before, **more):
        return call(
            functools.partial(steps_kernel, at, part),
            "steps_" + "ab"[part],
            array(blocks * rows, width),
            [ANY] + [VMEM] * 10 + [SMEM] + [ANY] * part,
            [pltpu.VMEM((at.part * rows, width), F32)] * 3
            + [pltpu.VMEM((at.part_rows, width), F32)] * 2
            + [pltpu.VMEM((rows, width), F32)] * 2
            + [pltpu.SemaphoreType.DMA((at.half,))] * 2,
            after=(before,),
            limit=STEPS_LIMIT,
            work=1_000_000_000,
            out_specs=ANY,
            **more,
        )

    halos = (north, south, west, east, far_north, far_south)
    halos += (near_first, near_last, first_cols, last_cols)
    atmos_next = both_steps(0, answers)(state, *halos, atmos_diffusion)
    answered, atmos_next = lax.optimization_barrier((answered, atmos_next))

    replies = call(
        functools.partial(reply_kernel, sea_fields),
        "replies",
        array(slots * sea_fields, width),
        [VMEM] * 4,
        [pltpu.VMEM((sea_fields * rows, width), F32)] * 2,
    )(answered.reshape(slots * sea_fields, width), remap_ocean, sea_slots, gather)
    returned = lax.all_to_all(
        replies.reshape(targets, CAPACITY * sea_fields, width), SECTION, 0, 0, tiled=True
    )
    atmos_next = both_steps(1, replies, input_output_aliases={12: 0})(
        state, *halos, atmos_diffusion, atmos_next
    )
    ocean_surface = call(
        functools.partial(surface_kernel, sea_fields),
        "surface",
        array(sea_fields * rows, width),
        [VMEM] * 3,
        [pltpu.VMEM((sea_fields * rows, width), F32)],
    )(
        returned.reshape(slots * sea_fields, width),
        weights_of(remap_atmos, True, "surface_weights", replies),
        tile_slots,
    )
    return (
        atmos_next.reshape(atmos_state.shape),
        ocean_next,
        ocean_surface.reshape(sea_fields, rows, width),
    )


def solution(mesh):
    in_specs = (
        P(None, None, ("comp", "gx"), "gy"),
        P(),
        P(("comp", "gx", "gy"), None, None),
        P(("comp", "gx", "gy"), None),
        P(("comp", "gx", "gy")),
        P(("comp", "gx", "gy"), None, None),
        P(("comp", "gx", "gy"), None),
        P(("comp", "gx", "gy")),
        P(None, None, "gx", "gy"),
        P(),
        P("gx", "gy"),
    )
    out_specs = (
        P(None, None, ("comp", "gx"), "gy"),
        P(None, None, "gx", "gy"),
        P(None, ("comp", "gx"), "gy"),
    )
    return jax.shard_map(
        on_device, mesh=mesh, in_specs=in_specs, out_specs=out_specs, check_vma=False
    )
```

```python
import functools

import jax
import jax.numpy as jnp
from jax import lax
from jax.experimental import pallas as pl
from jax.experimental.pallas import tpu as pltpu
from jax.sharding import PartitionSpec as P

F32 = jnp.float32
BF16 = jnp.bfloat16
FORCING_SCALE = (0.1, -0.1, 0.1, 0.1)
SECTION = ("gx", "gy")
EVERY = ("comp", "gx", "gy")
CAPACITY = 2
PIECE_ROWS = 8
VMEM_LIMIT = 8 * 1024 * 1024
EDGES_LIMIT = 60 * 1024 * 1024
SEA_LIMIT = 53 * 1024 * 1024
STEPS_LIMIT = 53 * 1024 * 1024


def shifted(block, axis, distance):
    devices = range(lax.axis_size(axis))
    route = [((i - distance) % len(devices), i) for i in devices]
    return lax.ppermute(block, axis, route)


def dot(left, right, transposed=False):
    dims = (((1,), (1 if transposed else 0,)), ((), ()))
    return lax.dot_general(left, right, dims, preferred_element_type=F32)


def halves(values):
    high = values.astype(BF16)
    return high, (values - high.astype(F32)).astype(BF16)


def remapped(rows, weights):
    count, width = rows.shape
    high, low = halves(rows)
    if count < 16:
        filler = jnp.zeros((16 - count, width), F32)
        high, low = halves(jnp.concatenate([rows, filler], axis=0))
    left = jnp.concatenate(
        [
            jnp.concatenate([high, high], axis=1),
            jnp.concatenate([low, jnp.zeros(low.shape, BF16)], axis=1),
        ],
        axis=0,
    )
    product = dot(left, weights)
    return product[:count, :] + product[16 : 16 + count, :]


def both_halves(block):
    return jnp.concatenate(halves(block), axis=0)


def weights_kernel(transposed, remap, weights):
    for tile in range(remap.shape[0]):
        block = remap[tile]
        weights[tile] = both_halves(jnp.transpose(block) if transposed else block)


def picked(selection, values):
    chosen = selection.astype(BF16)
    high = values.astype(BF16)
    rest = values - high.astype(F32)
    middle = rest.astype(BF16)
    low = (rest - middle.astype(F32)).astype(BF16)
    return dot(chosen, high) + dot(chosen, middle) + dot(chosen, low)


def placed(values, selection):
    chosen = selection.astype(BF16)
    high = values.astype(BF16)
    rest = values - high.astype(F32)
    middle = rest.astype(BF16)
    low = (rest - middle.astype(F32)).astype(BF16)
    return dot(high, chosen) + dot(middle, chosen) + dot(low, chosen)


def one_hot(labels):
    lanes = lax.broadcasted_iota(jnp.int32, labels.shape, 1).astype(F32)
    return (labels == lanes).astype(F32)


def grid_index(shape):
    return lax.broadcasted_iota(jnp.int32, shape, 0), lax.broadcasted_iota(jnp.int32, shape, 1)


def around(cells, north, south, west, east):
    rows, lanes = grid_index(cells.shape)
    row_count, width = cells.shape
    return (
        jnp.where(rows == 0, north, pltpu.roll(cells, 1, 0)),
        jnp.where(rows == row_count - 1, south, pltpu.roll(cells, row_count - 1, 0)),
        jnp.where(lanes == 0, west, pltpu.roll(cells, 1, 1)),
        jnp.where(lanes == width - 1, east, pltpu.roll(cells, width - 1, 1)),
    )


def diffused(cells, upper, lower, sides, diffusion):
    beside = sides[0] + sides[1] + sides[2] + sides[3] - 4.0 * cells
    return cells + diffusion * beside + 0.1 * (upper + lower - 2.0 * cells)


class Edges:
    def __init__(self, fields, levels, rows, sea_blocks, sea_rows, width):
        self.fields, self.levels, self.rows, self.width = fields, levels, rows, width
        self.sea_blocks, self.sea_rows = sea_blocks, sea_rows
        self.half = fields // 2
        self.part = self.half * levels
        self.part_rows = -(-self.part // 8) * 8
        self.atmos_rows = 2 * self.part_rows
        self.wet_row = self.atmos_rows + sea_blocks
        self.near_rows = -(-(self.wet_row + 1) // 8) * 8
        self.corner_row = self.atmos_rows
        self.far_rows = self.atmos_rows + 8
        self.sea_tiles = sea_blocks * sea_rows // width
        self.sea_cols = 4 * rows
        self.sea_col_rows = -(-(self.sea_tiles + 1) // 8) * 8
        self.col_rows = self.sea_cols + self.sea_col_rows


def squared(values):
    rows, width = values.shape
    if rows == width:
        return values
    return jnp.concatenate([values, jnp.zeros((width - rows, width), F32)], axis=0)


def chunk(source, target, at, rows, arrival):
    part = pl.ds(pl.multiple_of(at * rows, 8), rows)
    return pltpu.make_async_copy(source.at[part], target.at[part], arrival)


def edges_kernel(
    at,
    state_far,
    ocean_far,
    wet_far,
    near_first,
    near_last,
    far_first,
    far_last,
    first,
    last,
    state,
    ocean,
    wet,
    arrivals,
):
    rows, part, width = at.rows, at.part, at.width
    field_rows = at.levels * rows
    sea_parts = 4
    copies = [
        chunk(state_far, state, field, field_rows, arrivals.at[field])
        for field in range(at.fields)
    ]
    copies += [
        chunk(ocean_far, ocean, field, ocean.shape[0] // sea_parts, arrivals.at[at.fields + field])
        for field in range(sea_parts)
    ]
    copies.append(pltpu.make_async_copy(wet_far, wet, arrivals.at[at.fields + sea_parts]))
    for copy in copies:
        copy.start()
    for out in (near_first, near_last, far_first, far_last):
        out[...] = jnp.zeros(out.shape, F32)
    for cols in (first, last):
        cols[pl.ds(at.sea_cols, at.sea_col_rows), :] = jnp.zeros((at.sea_col_rows, width), F32)
    for half in range(2):
        for field in range(half * at.half, (half + 1) * at.half):
            copies[field].wait()
        for row in range(rows):
            lines = state[pl.ds(half * part * rows + row, part, stride=rows), :]
            held = pl.ds(half * at.part_rows, part)
            if row < 2:
                (near_first, far_first)[row][held, :] = lines
            if row >= rows - 2:
                (near_last, far_last)[rows - 1 - row][held, :] = lines
            turned = jnp.transpose(squared(lines))
            near, far = half * rows + row, (2 + half) * rows + row
            first[pl.ds(near, 1), :] = turned[0:1, :]
            first[pl.ds(far, 1), :] = turned[1:2, :]
            last[pl.ds(near, 1), :] = turned[width - 1 : width, :]
            last[pl.ds(far, 1), :] = turned[width - 2 : width - 1, :]
    for copy in copies[at.fields :]:
        copy.wait()
    for out, sea_row in ((near_first, 0), (near_last, at.sea_rows - 1)):
        out[pl.ds(at.atmos_rows, at.sea_blocks), :] = ocean[
            pl.ds(sea_row, at.sea_blocks, stride=at.sea_rows), :
        ]
        out[pl.ds(at.wet_row, 1), :] = wet[pl.ds(sea_row, 1), :].astype(F32)
    for tile in range(at.sea_tiles + 1):
        if tile < at.sea_tiles:
            lines = ocean[pl.ds(tile * width, width), :]
        else:
            lines = squared(wet[...].astype(F32))
        turned = jnp.transpose(lines)
        first[pl.ds(at.sea_cols + tile, 1), :] = turned[0:1, :]
        last[pl.ds(at.sea_cols + tile, 1), :] = turned[width - 1 : width, :]


def corners_kernel(at, far_first, far_last, west, east, to_north, to_south):
    for out, lines, row in ((to_north, far_first, 0), (to_south, far_last, at.rows - 1)):
        out[...] = lines[...]
        for place, (cols, half) in enumerate(((west, 0), (west, 1), (east, 0), (east, 1))):
            out[pl.ds(at.corner_row + place, 1), :] = cols[pl.ds(half * at.rows + row, 1), :]


def spread(at, diffusion, part, places):
    numbers = jnp.zeros(places.shape, F32)
    is_first = places < 0
    is_last = places < 0
    for field in range(at.half):
        start = field * at.levels
        numbers = jnp.where(places >= start, diffusion[part * at.half + field], numbers)
        is_first = is_first | (places == start)
        is_last = is_last | (places == start + at.levels - 1)
    return numbers, is_first, is_last


def ring_step(at, part, halos, edges, diffusion, outs):
    north, south, west, east, far_north, far_south = halos
    near_first, near_last, first, last = edges
    rows, width = at.rows, at.width
    shape = (at.part_rows, width)
    held = pl.ds(part * at.part_rows, shape[0])
    lines, lanes = grid_index(shape)
    numbers, is_first, is_last = spread(at, diffusion, part, lines)
    for out, outside, further, own, is_north in (
        (outs[0], north, far_north, near_first, True),
        (outs[1], south, far_south, near_last, False),
    ):
        turned = jnp.transpose(squared(further[pl.ds(at.corner_row, 8), :]))[: shape[0], :]
        cells, beyond, inside = outside[held, :], further[held, :], own[held, :]
        west_col = jnp.where(lanes == 0, turned[:, part : part + 1], pltpu.roll(cells, 1, 1))
        east_col = jnp.where(
            lanes == width - 1, turned[:, 2 + part : 3 + part], pltpu.roll(cells, width - 1, 1)
        )
        sides = (
            beyond if is_north else inside,
            inside if is_north else beyond,
            west_col,
            east_col,
        )
        upper = jnp.where(is_first, cells, pltpu.roll(cells, 1, 0))
        lower = jnp.where(is_last, cells, pltpu.roll(cells, shape[0] - 1, 0))
        out[...] = diffused(cells, upper, lower, sides, numbers)

    shape = (rows, width)
    near, far = pl.ds(part * rows, rows), pl.ds((2 + part) * rows, rows)
    lines, lanes = grid_index(shape)
    numbers, is_first, is_last = spread(at, diffusion, part, lanes)
    for out, outside, own, corner, is_west in (
        (outs[2], west, first, 0, True),
        (outs[3], east, last, 2, False),
    ):
        cells, beyond, inside = outside[near, :], outside[far, :], own[near, :]
        place = pl.ds(at.corner_row + corner + part, 1)
        sides = (
            jnp.where(lines == 0, far_north[place, :], pltpu.roll(cells, 1, 0)),
            jnp.where(lines == rows - 1, far_south[place, :], pltpu.roll(cells, rows - 1, 0)),
            beyond if is_west else inside,
            inside if is_west else beyond,
        )
        upper = jnp.where(is_first, cells, pltpu.roll(cells, 1, 1))
        lower = jnp.where(is_last, cells, pltpu.roll(cells, width - 1, 1))
        out[...] = diffused(cells, upper, lower, sides, numbers)


def interleaved(at, west, east):
    width = at.width
    fields_each = width // 2 // at.levels
    columns = jnp.concatenate([east, west], axis=1)
    source, target = grid_index((2 * width, width))
    out = []
    for first in range(0, at.half, fields_each):
        block = jnp.where(source < width, source, source - width) - first * at.levels
        lane = 2 * block + jnp.where(source < width, 0, 1)
        out.append(placed(columns, (lane == target).astype(F32)))
    return out


def field_step(at, field, state, out, north, south, first_line, beside, number):
    levels, rows, width = at.levels, at.rows, at.width
    fields_each = width // 2 // levels
    lines, lanes = grid_index((rows, width))
    for level in range(levels):
        line = first_line + field * levels + level
        start = (field * levels + level) * rows
        cells = state[pl.ds(start, rows), :]
        first_level, last_level = level == 0, level == levels - 1
        upper = cells if first_level else state[pl.ds(start - rows, rows), :]
        lower = cells if last_level else state[pl.ds(start + rows, rows), :]
        lane = 2 * ((field % fields_each) * levels + level) + 1
        edge = pltpu.roll(beside[field // fields_each], width - lane, 1)
        sides = (
            jnp.where(lines == 0, north[pl.ds(line, 1), :], pltpu.roll(cells, 1, 0)),
            jnp.where(
                lines == rows - 1, south[pl.ds(line, 1), :], pltpu.roll(cells, rows - 1, 0)
            ),
            jnp.where(lanes == 0, edge, pltpu.roll(cells, 1, 1)),
            jnp.where(lanes == width - 1, edge, pltpu.roll(cells, width - 1, 1)),
        )
        out[pl.ds(start, rows), :] = diffused(cells, upper, lower, sides, number)


def steps_kernel(
    at,
    part,
    state_far,
    north,
    south,
    west,
    east,
    far_north,
    far_south,
    near_first,
    near_last,
    first,
    last,
    diffusion,
    *rest,
):
    if part:
        rest = rest[1:]
    out_far, state, middle, out, *ring, arrivals, departures = rest
    rows, width, levels = at.rows, at.width, at.levels
    field_rows = levels * rows
    whole = part * at.half

    def coming(field):
        return pltpu.make_async_copy(
            state_far.at[pl.ds((whole + field) * field_rows, field_rows)],
            state.at[pl.ds(field * field_rows, field_rows)],
            arrivals.at[field],
        )

    def going(field):
        return pltpu.make_async_copy(
            out.at[pl.ds(field * field_rows, field_rows)],
            out_far.at[pl.ds((whole + field) * field_rows, field_rows)],
            departures.at[field],
        )

    for field in range(at.half):
        coming(field).start()
    halos = (north, south, west, east, far_north, far_south)
    ring_step(at, part, halos, (near_first, near_last, first, last), diffusion, ring)
    held = pl.ds(part * rows, rows)
    outer = interleaved(at, west[held, :], east[held, :])
    inner = interleaved(at, ring[2][...], ring[3][...])
    for field in range(at.half):
        number = diffusion[whole + field]
        coming(field).wait()
        field_step(
            at, field, state, middle, north, south, part * at.part_rows, outer, number
        )
        field_step(at, field, middle, out, ring[0], ring[1], 0, inner, number)
        going(field).start()
    for field in range(at.half):
        going(field).wait()


def ocean_kernel(
    at,
    levels,
    ocean_far,
    wet,
    north,
    south,
    west,
    east,
    mixing,
    out_far,
    tops,
    ocean,
    out,
    wests,
    easts,
    arrivals,
    departures,
):
    fields, field_rows = at.sea_blocks // levels, levels * at.sea_rows
    for field in range(fields):
        chunk(ocean_far, ocean, field, field_rows, arrivals.at[field]).start()
    rows, width = at.sea_rows, at.width
    lines, lanes = grid_index((rows, width))
    per_tile = width // rows
    held = pl.ds(at.sea_cols, at.sea_col_rows)
    wests[...] = jnp.transpose(squared(west[held, :]))
    easts[...] = jnp.transpose(squared(east[held, :]))
    wet_cells = wet[...].astype(F32)
    wet_lane = at.sea_tiles
    wet_sides = around(
        wet_cells,
        north[pl.ds(at.wet_row, 1), :],
        south[pl.ds(at.wet_row, 1), :],
        wests[pl.ds(0, rows), :][:, wet_lane : wet_lane + 1],
        easts[pl.ds(0, rows), :][:, wet_lane : wet_lane + 1],
    )

    def field_step(field, carry):
        chunk(ocean_far, ocean, field, field_rows, arrivals.at[field]).wait()
        back = lax.rem(width - field * (levels // per_tile), width)
        west_cols = pltpu.roll(wests[...], back, 1)
        east_cols = pltpu.roll(easts[...], back, 1)
        number = mixing[field] * wet_cells
        for level in range(levels):
            block = field * levels + level
            start = pl.multiple_of(block * rows, rows)
            first_level, last_level = level == 0, level == levels - 1
            cells = ocean[pl.ds(start, rows), :]
            upper = cells if first_level else ocean[pl.ds(start - rows, rows), :]
            lower = cells if last_level else ocean[pl.ds(start + rows, rows), :]
            above = pltpu.roll(cells, 1, 0)
            below = pltpu.roll(cells, rows - 1, 0)
            line = at.atmos_rows + block
            tile, within = level // per_tile, (level % per_tile) * rows
            west_col = pltpu.roll(west_cols[within : within + rows, :], (width - tile) % width, 1)
            east_col = pltpu.roll(east_cols[within : within + rows, :], width - 1 - tile, 1)
            sides = (
                jnp.where(lines == 0, north[pl.ds(line, 1), :], above),
                jnp.where(lines == rows - 1, south[pl.ds(line, 1), :], below),
                jnp.where(lanes == 0, west_col, pltpu.roll(cells, 1, 1)),
                jnp.where(lanes == width - 1, east_col, pltpu.roll(cells, width - 1, 1)),
            )
            total = wet_sides[0] * (sides[0] - cells)
            for side in range(1, 4):
                total = total + wet_sides[side] * (sides[side] - cells)
            tendency = number * total + 0.1 * (upper + lower - 2.0 * cells)
            after = cells + wet_cells * tendency
            out[pl.ds(start, rows), :] = after
            if first_level:
                tops[pl.ds(pl.multiple_of(field * rows, rows), rows), :] = after
        chunk(out, out_far, field, field_rows, departures.at[field]).start()
        return carry

    lax.fori_loop(0, fields, field_step, 0)
    for field in range(fields):
        chunk(out, out_far, field, field_rows, departures.at[field]).wait()


def label_base(rows):
    return 2.0 * rows


def routes_kernel(index, own, diffusion, *rest):
    *outs, labels_out, section, numbers, tally, piece_labels, sea_labels = rest
    lanes = lax.broadcasted_iota(jnp.int32, (1, section.shape[1]), 1)
    section[...] = jnp.full(section.shape, own[0].astype(F32))
    for field in range(diffusion.shape[0]):
        numbers[pl.ds(field, 1), :] = jnp.full(lanes.shape, diffusion[field])

    def clear(at, carry):
        tally[at] = 0
        return carry

    for row, slots, labels in ((0, outs[0], piece_labels), (2, outs[1], sea_labels)):
        slots[...] = jnp.zeros(slots.shape, F32)
        labels[...] = jnp.full(labels.shape, -1.0, F32)
        lax.fori_loop(0, tally.shape[0], clear, 0)
        for tile in range(index.shape[1]):
            owner = index[row, tile]
            rank = tally[owner]
            tally[owner] = rank + 1
            slot = pl.ds(owner * CAPACITY + rank, 1)
            slots[slot, :] = (lanes == tile).astype(F32)
            labels[slot, :] = jnp.full(lanes.shape, index[row + 1, tile].astype(F32))
    base = label_base(index.shape[1])
    labels_out[...] = (piece_labels[...] + 1.0) + base * (sea_labels[...] + 1.0)


def inner_kernel(at, state_far, numbers, out, top, arrival):
    fields, rows, width = at.fields, at.rows, at.width
    copy = pltpu.make_async_copy(state_far.at[:, pl.ds(at.levels - 2, 2)], top, arrival)
    copy.start()
    lines, lanes = grid_index((rows, width))
    copy.wait()
    for field in range(fields):
        cells = top[field, 1]
        sides = (
            jnp.where(lines == 0, 0.0, pltpu.roll(cells, 1, 0)),
            jnp.where(lines == rows - 1, 0.0, pltpu.roll(cells, rows - 1, 0)),
            jnp.where(lanes == 0, 0.0, pltpu.roll(cells, 1, 1)),
            jnp.where(lanes == width - 1, 0.0, pltpu.roll(cells, width - 1, 1)),
        )
        out[pl.ds(field * rows, rows), :] = diffused(
            cells, top[field, 0], cells, sides, numbers[pl.ds(field, 1), :]
        )


def pieces_kernel(
    at, inner, north, south, west, east, weights, numbers, routes, labels, out, surface, products
):
    fields, levels, rows, width = at.fields, at.levels, at.rows, at.width
    slots = routes.shape[0]
    lines, lanes = grid_index((rows, width))
    a = []
    for field in range(fields):
        part = field // at.half
        held = pl.ds(part * rows, rows)
        lane = (field % at.half) * levels + levels - 1
        line = pl.ds(part * at.part_rows + lane, 1)
        outside = (
            jnp.where(lines == 0, north[line, :], 0.0)
            + jnp.where(lines == rows - 1, south[line, :], 0.0)
            + jnp.where(lanes == 0, pltpu.roll(west[held, :], (width - lane) % width, 1), 0.0)
            + jnp.where(lanes == width - 1, pltpu.roll(east[held, :], width - 1 - lane, 1), 0.0)
        )
        a.append(inner[pl.ds(field * rows, rows), :] + numbers[pl.ds(field, 1), :] * outside)
    sums = (a[0] - a[4], a[1], a[2], a[3], a[6] + a[7], a[5] + a[8], a[9])
    for place in range(16):
        surface[pl.ds(place * rows, rows), :] = (
            sums[place] if place < len(sums) else jnp.zeros((rows, width), F32)
        )
    for tile in range(rows):
        products[pl.ds(tile * 16, 16), :] = remapped(
            surface[pl.ds(tile, 16, stride=rows), :], weights[tile]
        )
    count = PIECE_ROWS - 1
    sent = picked(
        routes[...][:, :rows],
        jnp.concatenate(
            [products[pl.ds(place, rows, stride=16), :] for place in range(count)], axis=1
        ),
    )
    for place in range(count):
        out[pl.ds(place, slots, stride=PIECE_ROWS), :] = sent[:, place * width : (place + 1) * width]
    out[pl.ds(count, slots, stride=PIECE_ROWS), :] = labels[...]


def flux_kernel(sizes, arrived, remap, routes, out, gather, sea_labels, fluxes, products):
    flux_count, rows, sections = sizes
    width = out.shape[1]
    slots = routes.shape[0]
    count = PIECE_ROWS - 1
    labels = arrived[pl.ds(count, slots, stride=PIECE_ROWS), :]
    upper = jnp.floor(labels * (1.0 / label_base(rows)))
    select = one_hot(labels - label_base(rows) * upper - 1.0)
    gather[...] = select
    sea_labels[...] = upper - 1.0
    values = jnp.concatenate(
        [arrived[pl.ds(place, slots, stride=PIECE_ROWS), :] for place in range(count)], axis=1
    )
    exchange = picked(jnp.transpose(select)[:rows, :], values)
    a04, a1, a2, a3, a67, a58, a9 = (
        exchange[:, place * width : (place + 1) * width] for place in range(count)
    )
    speed = jnp.sqrt(a2 * a2 + a3 * a3 + 0.5)
    fluxes[pl.ds(0, rows), :] = speed * a04 + a67
    fluxes[pl.ds(rows, rows), :] = speed * a1 + a58
    fluxes[pl.ds(2 * rows, rows), :] = speed * a2 * (1.0 + 0.2 * jnp.tanh(a9))
    fluxes[pl.ds(3 * rows, rows), :] = speed * a3
    for tile in range(rows):
        products[pl.ds(tile * flux_count, flux_count), :] = remapped(
            fluxes[pl.ds(tile, flux_count, stride=rows), :], both_halves(remap[tile])
        )
    sent = picked(
        routes[...][:, :rows],
        jnp.concatenate(
            [products[pl.ds(flux, rows, stride=flux_count), :] for flux in range(flux_count)],
            axis=1,
        ),
    )
    for flux in range(flux_count):
        for section in range(sections):
            out[pl.ds(section * slots * flux_count + flux, slots, stride=flux_count), :] = sent[
                :, flux * width : (flux + 1) * width
            ]


def sea_kernel(
    sizes, landed, base_tops, wet, own_labels, other_labels, section, tops, answers
):
    flux_count, sea_rows = sizes
    width = landed.shape[1]
    slots = own_labels.shape[0]
    mine = one_hot(own_labels[...])
    others = one_hot(other_labels[...])
    is_first = section[0:1, :] == 0.0
    select = jnp.concatenate(
        [jnp.where(is_first, mine, others), jnp.where(is_first, others, mine)], axis=0
    )
    values = jnp.concatenate(
        [landed[pl.ds(flux, 2 * slots, stride=flux_count), :] for flux in range(flux_count)], axis=1
    )
    forcing = picked(jnp.transpose(select)[:sea_rows, :], values)
    wet_cells = wet[...].astype(F32)
    for flux in range(flux_count):
        held = pl.ds(flux * sea_rows, sea_rows)
        tops[held, :] = base_tops[held, :] + wet_cells * (
            FORCING_SCALE[flux] * forcing[:, flux * width : (flux + 1) * width]
        )
    all_tops = jnp.concatenate(
        [tops[pl.ds(flux * sea_rows, sea_rows), :] for flux in range(flux_count)], axis=1
    )
    reply = picked(mine[:, :sea_rows], all_tops)
    for flux in range(flux_count):
        answers[pl.ds(flux, slots, stride=flux_count), :] = reply[
            :, flux * width : (flux + 1) * width
        ]


def store_kernel(sea_rows, tops, base, out, leave):
    copies = [
        pltpu.make_async_copy(
            tops.at[pl.ds(flux * sea_rows, sea_rows)], out.at[flux, 0], leave.at[flux]
        )
        for flux in range(out.shape[0])
    ]
    for copy in copies:
        copy.start()
    for copy in copies:
        copy.wait()


def tops_of_tiles(returned, routes, flux_count, scratch):
    slots, width = routes.shape
    rows = scratch.shape[0] // flux_count
    found = picked(
        jnp.transpose(routes[...])[:rows, :],
        jnp.concatenate(
            [returned[pl.ds(flux, slots, stride=flux_count), :] for flux in range(flux_count)],
            axis=1,
        ),
    )
    for flux in range(flux_count):
        scratch[pl.ds(flux, rows, stride=flux_count), :] = found[
            :, flux * width : (flux + 1) * width
        ]


def reply_kernel(flux_count, answered, remap, routes, gather, out, tops, on_exchange):
    slots, width = routes.shape
    rows = remap.shape[0]
    tops_of_tiles(answered, routes, flux_count, tops)
    for tile in range(rows):
        held = pl.ds(tile * flux_count, flux_count)
        on_exchange[held, :] = remapped(
            tops[held, :], both_halves(jnp.transpose(remap[tile]))
        )
    values = jnp.concatenate(
        [on_exchange[pl.ds(flux, rows, stride=flux_count), :] for flux in range(flux_count)], axis=1
    )
    replies = picked(gather[...][:, :rows], values)
    for flux in range(flux_count):
        out[pl.ds(flux, slots, stride=flux_count), :] = replies[
            :, flux * width : (flux + 1) * width
        ]


def surface_kernel(flux_count, returned, weights, routes, out, tops):
    rows = weights.shape[0]
    tops_of_tiles(returned, routes, flux_count, tops)
    for tile in range(rows):
        out[pl.ds(tile, flux_count, stride=rows), :] = remapped(
            tops[pl.ds(tile * flux_count, flux_count), :], weights[tile]
        )


VMEM = pl.BlockSpec(memory_space=pltpu.VMEM)
SMEM = pl.BlockSpec(memory_space=pltpu.SMEM)
ANY = pl.BlockSpec(memory_space=pl.ANY)


def array(*shape):
    return jax.ShapeDtypeStruct(shape, F32)


def call(kernel, name, outs, in_specs, scratch=(), after=(), limit=VMEM_LIMIT, work=1_000_000, **more):
    def body(*refs):
        kernel(*refs[: len(in_specs)], *refs[len(in_specs) + len(after) :])

    run = pl.pallas_call(
        body,
        name=name,
        out_shape=outs,
        in_specs=list(in_specs) + [ANY] * len(after),
        scratch_shapes=list(scratch),
        compiler_params=pltpu.CompilerParams(vmem_limit_bytes=limit),
        cost_estimate=pl.CostEstimate(flops=0, bytes_accessed=work, transcendentals=0),
        **more,
    )
    return lambda *arguments: run(*arguments, *after)


def gated(values, before):
    return lax.optimization_barrier((values, before))[0]


def on_device(
    atmos_state,
    atmos_diffusion,
    remap_atmos,
    exchange_owner,
    exchange_slot,
    remap_ocean,
    ocean_owner,
    ocean_slot,
    ocean_state,
    ocean_mixing,
    wet_mask,
):
    targets = lax.axis_size(SECTION)
    sections = lax.axis_size("comp")
    devices = targets * sections
    fields, levels, rows, width = atmos_state.shape
    sea_fields, sea_levels, sea_rows, _ = ocean_state.shape
    blocks = fields * levels
    sea_blocks = sea_fields * sea_levels
    at = Edges(fields, levels, rows, sea_blocks, sea_rows, width)
    slots = targets * CAPACITY
    ring = ("comp", "gx")

    index = jnp.stack([exchange_owner[:, 0], exchange_slot, ocean_owner[:, 0], ocean_slot])
    section = lax.axis_index("comp").astype(jnp.int32).reshape(1)
    state = atmos_state.reshape(blocks * rows, width)
    ocean = ocean_state.reshape(sea_blocks * sea_rows, width)

    state_copy = pltpu.VMEM((blocks * rows, width), F32)
    ocean_copy = pltpu.VMEM((sea_blocks * sea_rows, width), F32)
    wet_copy = pltpu.VMEM((sea_rows, width), jnp.int32)
    ocean_flags = pltpu.SemaphoreType.DMA((sea_fields,))
    near_first, near_last, far_first, far_last, first_cols, last_cols = call(
        functools.partial(edges_kernel, at),
        "edges",
        (array(at.near_rows, width),) * 2
        + (array(at.far_rows, width),) * 2
        + (array(at.col_rows, width),) * 2,
        [ANY] * 3,
        [state_copy, ocean_copy, wet_copy, pltpu.SemaphoreType.DMA((fields + 5,))],
        limit=EDGES_LIMIT,
    )(state, ocean, wet_mask)
    north = shifted(near_last, ring, 1)
    south = shifted(near_first, ring, -1)
    west = shifted(last_cols, "gy", 1)
    east = shifted(first_cols, "gy", -1)

    def weights_of(remap, transposed, name, before):
        return call(
            functools.partial(weights_kernel, transposed),
            name,
            jax.ShapeDtypeStruct((rows, 2 * width, width), BF16),
            [VMEM],
        )(gated(remap, before))

    tile_slots, sea_slots, labels, here, numbers = call(
        routes_kernel,
        "routes",
        (array(slots, width),) * 3 + (array(8, width), array(-(-fields // 8) * 8, width)),
        [SMEM] * 3,
        [pltpu.SMEM((targets,), jnp.int32)] + [pltpu.VMEM((slots, width), F32)] * 2,
    )(gated(index, first_cols), section, atmos_diffusion)
    inner = call(
        functools.partial(inner_kernel, at),
        "inner",
        array(fields * rows, width),
        [ANY, VMEM],
        [pltpu.VMEM((fields, 2, rows, width), F32), pltpu.SemaphoreType.DMA],
    )(gated(atmos_state, first_cols), numbers)
    pieces = call(
        functools.partial(pieces_kernel, at),
        "pieces",
        array(slots * PIECE_ROWS, width),
        [VMEM] * 9,
        [pltpu.VMEM((16 * rows, width), F32)] * 2,
    )(
        inner,
        north,
        south,
        west,
        east,
        weights_of(remap_atmos, False, "piece_weights", first_cols),
        numbers,
        tile_slots,
        labels,
    )
    arrived = lax.all_to_all(
        pieces.reshape(targets, CAPACITY * PIECE_ROWS, width), SECTION, 0, 0, tiled=True
    )
    outgoing, gather, own_labels = call(
        functools.partial(flux_kernel, (sea_fields, rows, sections)),
        "fluxes",
        (
            array(sections * slots * sea_fields, width),
            array(slots, width),
            array(slots, width),
        ),
        [VMEM] * 3,
        [pltpu.VMEM((sea_fields * rows, width), F32)] * 2,
    )(arrived.reshape(slots * PIECE_ROWS, width), remap_ocean, sea_slots)
    landed = lax.all_to_all(
        outgoing.reshape(devices, CAPACITY * sea_fields, width), EVERY, 0, 0, tiled=True
    )
    other_labels = shifted(own_labels, "comp", 1)
    to_north, to_south = call(
        functools.partial(corners_kernel, at),
        "corners",
        (array(at.far_rows, width),) * 2,
        [VMEM] * 4,
        after=(outgoing,),
    )(far_first, far_last, west, east)
    far_north = shifted(to_south, ring, 1)
    far_south = shifted(to_north, ring, -1)

    sea_base, base_tops = call(
        functools.partial(ocean_kernel, at, sea_levels),
        "sea_base",
        (array(sea_blocks * sea_rows, width), array(sea_fields * sea_rows, width)),
        [ANY] + [VMEM] * 5 + [SMEM],
        [ocean_copy] * 2 + [pltpu.VMEM((width, width), F32)] * 2 + [ocean_flags] * 2,
        after=(outgoing,),
        limit=SEA_LIMIT,
        work=1_000_000_000,
        out_specs=(ANY, VMEM),
    )(ocean, wet_mask, north, south, west, east, ocean_mixing)

    tops, answers = call(
        functools.partial(sea_kernel, (sea_fields, sea_rows)),
        "sea_top",
        (array(sea_fields * sea_rows, width), array(slots * sea_fields, width)),
        [VMEM] * 6,
        after=(far_north, far_south),
    )(
        landed.reshape(devices * CAPACITY * sea_fields, width),
        base_tops,
        wet_mask,
        own_labels,
        other_labels,
        here,
    )
    ocean_next = call(
        functools.partial(store_kernel, sea_rows),
        "store",
        array(sea_fields, sea_levels, sea_rows, width),
        [VMEM, ANY],
        [ocean_flags],
        out_specs=ANY,
        input_output_aliases={1: 0},
    )(tops, sea_base.reshape(sea_fields, sea_levels, sea_rows, width))
    answered = lax.all_to_all(
        answers.reshape(targets, CAPACITY * sea_fields, width), SECTION, 0, 0, tiled=True
    )
    def both_steps(part, before, **more):
        return call(
            functools.partial(steps_kernel, at, part),
            "steps_" + "ab"[part],
            array(blocks * rows, width),
            [ANY] + [VMEM] * 10 + [SMEM] + [ANY] * part,
            [pltpu.VMEM((at.part * rows, width), F32)] * 3
            + [pltpu.VMEM((at.part_rows, width), F32)] * 2
            + [pltpu.VMEM((rows, width), F32)] * 2
            + [pltpu.SemaphoreType.DMA((at.half,))] * 2,
            after=(before,),
            limit=STEPS_LIMIT,
            work=1_000_000_000,
            out_specs=ANY,
            **more,
        )

    halos = (north, south, west, east, far_north, far_south)
    halos += (near_first, near_last, first_cols, last_cols)
    atmos_next = both_steps(0, answers)(state, *halos, atmos_diffusion)
    answered, atmos_next, ocean_next = lax.optimization_barrier((answered, atmos_next, ocean_next))

    replies = call(
        functools.partial(reply_kernel, sea_fields),
        "replies",
        array(slots * sea_fields, width),
        [VMEM] * 4,
        [pltpu.VMEM((sea_fields * rows, width), F32)] * 2,
    )(answered.reshape(slots * sea_fields, width), remap_ocean, sea_slots, gather)
    returned = lax.all_to_all(
        replies.reshape(targets, CAPACITY * sea_fields, width), SECTION, 0, 0, tiled=True
    )
    atmos_next = both_steps(1, replies, input_output_aliases={12: 0})(
        state, *halos, atmos_diffusion, atmos_next
    )
    ocean_surface = call(
        functools.partial(surface_kernel, sea_fields),
        "surface",
        array(sea_fields * rows, width),
        [VMEM] * 3,
        [pltpu.VMEM((sea_fields * rows, width), F32)],
    )(
        returned.reshape(slots * sea_fields, width),
        weights_of(remap_atmos, True, "surface_weights", replies),
        tile_slots,
    )
    return (
        atmos_next.reshape(atmos_state.shape),
        ocean_next,
        ocean_surface.reshape(sea_fields, rows, width),
    )


def solution(mesh):
    in_specs = (
        P(None, None, ("comp", "gx"), "gy"),
        P(),
        P(("comp", "gx", "gy"), None, None),
        P(("comp", "gx", "gy"), None),
        P(("comp", "gx", "gy")),
        P(("comp", "gx", "gy"), None, None),
        P(("comp", "gx", "gy"), None),
        P(("comp", "gx", "gy")),
        P(None, None, "gx", "gy"),
        P(),
        P("gx", "gy"),
    )
    out_specs = (
        P(None, None, ("comp", "gx"), "gy"),
        P(None, None, "gx", "gy"),
        P(None, ("comp", "gx"), "gy"),
    )
    return jax.shard_map(
        on_device, mesh=mesh, in_specs=in_specs, out_specs=out_specs, check_vma=False
    )
```

```python
import functools

import jax
import jax.numpy as jnp
from jax import lax
from jax.experimental import pallas as pl
from jax.experimental.pallas import tpu as pltpu
from jax.sharding import PartitionSpec as P

F32 = jnp.float32
BF16 = jnp.bfloat16
FORCING_SCALE = (0.1, -0.1, 0.1, 0.1)
SECTION = ("gx", "gy")
EVERY = ("comp", "gx", "gy")
CAPACITY = 2
PIECE_ROWS = 8
VMEM_LIMIT = 8 * 1024 * 1024
EDGES_LIMIT = 52 * 1024 * 1024
SEA_LIMIT = 53 * 1024 * 1024
STEPS_LIMIT = 53 * 1024 * 1024


def shifted(block, axis, distance):
    devices = range(lax.axis_size(axis))
    route = [((i - distance) % len(devices), i) for i in devices]
    return lax.ppermute(block, axis, route)


def dot(left, right, transposed=False):
    dims = (((1,), (1 if transposed else 0,)), ((), ()))
    return lax.dot_general(left, right, dims, preferred_element_type=F32)


def halves(values):
    high = values.astype(BF16)
    return high, (values - high.astype(F32)).astype(BF16)


def remapped(rows, weights):
    count, width = rows.shape
    high, low = halves(rows)
    if count < 16:
        filler = jnp.zeros((16 - count, width), F32)
        high, low = halves(jnp.concatenate([rows, filler], axis=0))
    left = jnp.concatenate(
        [
            jnp.concatenate([high, high], axis=1),
            jnp.concatenate([low, jnp.zeros(low.shape, BF16)], axis=1),
        ],
        axis=0,
    )
    product = dot(left, weights)
    return product[:count, :] + product[16 : 16 + count, :]


def both_halves(block):
    return jnp.concatenate(halves(block), axis=0)


def weights_kernel(transposed, remap, weights):
    for tile in range(remap.shape[0]):
        block = remap[tile]
        weights[tile] = both_halves(jnp.transpose(block) if transposed else block)


def picked(selection, values):
    chosen = selection.astype(BF16)
    high = values.astype(BF16)
    rest = values - high.astype(F32)
    middle = rest.astype(BF16)
    low = (rest - middle.astype(F32)).astype(BF16)
    return dot(chosen, high) + dot(chosen, middle) + dot(chosen, low)


def placed(values, selection):
    chosen = selection.astype(BF16)
    high = values.astype(BF16)
    rest = values - high.astype(F32)
    middle = rest.astype(BF16)
    low = (rest - middle.astype(F32)).astype(BF16)
    return dot(high, chosen) + dot(middle, chosen) + dot(low, chosen)


def one_hot(labels):
    lanes = lax.broadcasted_iota(jnp.int32, labels.shape, 1).astype(F32)
    return (labels == lanes).astype(F32)


def grid_index(shape):
    return lax.broadcasted_iota(jnp.int32, shape, 0), lax.broadcasted_iota(jnp.int32, shape, 1)


def around(cells, north, south, west, east):
    rows, lanes = grid_index(cells.shape)
    row_count, width = cells.shape
    return (
        jnp.where(rows == 0, north, pltpu.roll(cells, 1, 0)),
        jnp.where(rows == row_count - 1, south, pltpu.roll(cells, row_count - 1, 0)),
        jnp.where(lanes == 0, west, pltpu.roll(cells, 1, 1)),
        jnp.where(lanes == width - 1, east, pltpu.roll(cells, width - 1, 1)),
    )


def diffused(cells, upper, lower, sides, diffusion):
    beside = sides[0] + sides[1] + sides[2] + sides[3] - 4.0 * cells
    return cells + diffusion * beside + 0.1 * (upper + lower - 2.0 * cells)


class Edges:
    def __init__(self, fields, levels, rows, sea_blocks, sea_rows, width):
        self.fields, self.levels, self.rows, self.width = fields, levels, rows, width
        self.sea_blocks, self.sea_rows = sea_blocks, sea_rows
        self.half = fields // 2
        self.part = self.half * levels
        self.ring_rows = -(-self.part // 8) * 8
        self.atmos_rows = 2 * self.part
        self.wet_row = self.atmos_rows + sea_blocks
        self.near_rows = -(-(self.wet_row + 1) // 8) * 8
        self.corner_row = self.atmos_rows
        self.far_rows = -(-(self.atmos_rows + 4) // 8) * 8
        self.sea_tiles = sea_blocks * sea_rows // width
        self.sea_cols = 4 * rows
        self.sea_col_rows = -(-(self.sea_tiles + 1) // 8) * 8
        self.col_rows = self.sea_cols + self.sea_col_rows


def squared(values):
    rows, width = values.shape
    if rows == width:
        return values
    return jnp.concatenate([values, jnp.zeros((width - rows, width), F32)], axis=0)


def chunk(source, target, at, rows, arrival):
    part = pl.ds(pl.multiple_of(at * rows, 8), rows)
    return pltpu.make_async_copy(source.at[part], target.at[part], arrival)


def edges_kernel(
    at, state_far, near_first, near_last, far_first, far_last, first, last, state, arrivals
):
    rows, part, width = at.rows, at.part, at.width
    field_rows = at.levels * rows
    copies = [
        chunk(state_far, state, field, field_rows, arrivals.at[field])
        for field in range(at.fields)
    ]
    for copy in copies:
        copy.start()
    for out in (near_first, near_last, far_first, far_last):
        out[...] = jnp.zeros(out.shape, F32)
    for cols in (first, last):
        cols[pl.ds(at.sea_cols, at.sea_col_rows), :] = jnp.zeros((at.sea_col_rows, width), F32)
    for half in range(2):
        for field in range(half * at.half, (half + 1) * at.half):
            copies[field].wait()
        for row in range(rows):
            lines = state[pl.ds(half * part * rows + row, part, stride=rows), :]
            held = pl.ds(half * at.part, part)
            if row < 2:
                (near_first, far_first)[row][held, :] = lines
            if row >= rows - 2:
                (near_last, far_last)[rows - 1 - row][held, :] = lines
            turned = jnp.transpose(squared(lines))
            near, far = half * rows + row, (2 + half) * rows + row
            first[pl.ds(near, 1), :] = turned[0:1, :]
            first[pl.ds(far, 1), :] = turned[1:2, :]
            last[pl.ds(near, 1), :] = turned[width - 1 : width, :]
            last[pl.ds(far, 1), :] = turned[width - 2 : width - 1, :]


def sea_edges_kernel(at, ocean, wet, near_first, near_last, first, last, *outs):
    width = at.width
    for out, rows in zip(outs, (near_first, near_last, first, last)):
        out[...] = rows[...]
    for out, sea_row in ((outs[0], 0), (outs[1], at.sea_rows - 1)):
        out[pl.ds(at.atmos_rows, at.sea_blocks), :] = ocean[
            pl.ds(sea_row, at.sea_blocks, stride=at.sea_rows), :
        ]
        out[pl.ds(at.wet_row, 1), :] = wet[pl.ds(sea_row, 1), :].astype(F32)
    for tile in range(at.sea_tiles + 1):
        if tile < at.sea_tiles:
            lines = ocean[pl.ds(tile * width, width), :]
        else:
            lines = squared(wet[...].astype(F32))
        turned = jnp.transpose(lines)
        outs[2][pl.ds(at.sea_cols + tile, 1), :] = turned[0:1, :]
        outs[3][pl.ds(at.sea_cols + tile, 1), :] = turned[width - 1 : width, :]


def corners_kernel(at, far_first, far_last, west, east, to_north, to_south):
    for out, lines, row in ((to_north, far_first, 0), (to_south, far_last, at.rows - 1)):
        out[...] = lines[...]
        for place, (cols, half) in enumerate(((west, 0), (west, 1), (east, 0), (east, 1))):
            out[pl.ds(at.corner_row + place, 1), :] = cols[pl.ds(half * at.rows + row, 1), :]


def spread(at, diffusion, part, places):
    numbers = jnp.zeros(places.shape, F32)
    is_first = places < 0
    is_last = places < 0
    for field in range(at.half):
        start = field * at.levels
        numbers = jnp.where(places >= start, diffusion[part * at.half + field], numbers)
        is_first = is_first | (places == start)
        is_last = is_last | (places == start + at.levels - 1)
    return numbers, is_first, is_last


def ring_step(at, part, halos, edges, diffusion, outs):
    north, south, west, east, far_north, far_south = halos
    near_first, near_last, first, last = edges
    rows, width = at.rows, at.width
    shape = (at.ring_rows, width)
    held = pl.ds(part * at.part, shape[0])
    lines, lanes = grid_index(shape)
    numbers, is_first, is_last = spread(at, diffusion, part, lines)
    for out, outside, further, own, is_north in (
        (outs[0], north, far_north, near_first, True),
        (outs[1], south, far_south, near_last, False),
    ):
        turned = jnp.transpose(squared(further[pl.ds(at.corner_row, 8), :]))[: shape[0], :]
        cells, beyond, inside = outside[held, :], further[held, :], own[held, :]
        west_col = jnp.where(lanes == 0, turned[:, part : part + 1], pltpu.roll(cells, 1, 1))
        east_col = jnp.where(
            lanes == width - 1, turned[:, 2 + part : 3 + part], pltpu.roll(cells, width - 1, 1)
        )
        sides = (
            beyond if is_north else inside,
            inside if is_north else beyond,
            west_col,
            east_col,
        )
        upper = jnp.where(is_first, cells, pltpu.roll(cells, 1, 0))
        lower = jnp.where(is_last, cells, pltpu.roll(cells, shape[0] - 1, 0))
        out[...] = diffused(cells, upper, lower, sides, numbers)

    shape = (rows, width)
    near, far = pl.ds(part * rows, rows), pl.ds((2 + part) * rows, rows)
    lines, lanes = grid_index(shape)
    numbers, is_first, is_last = spread(at, diffusion, part, lanes)
    for out, outside, own, corner, is_west in (
        (outs[2], west, first, 0, True),
        (outs[3], east, last, 2, False),
    ):
        cells, beyond, inside = outside[near, :], outside[far, :], own[near, :]
        place = pl.ds(at.corner_row + corner + part, 1)
        sides = (
            jnp.where(lines == 0, far_north[place, :], pltpu.roll(cells, 1, 0)),
            jnp.where(lines == rows - 1, far_south[place, :], pltpu.roll(cells, rows - 1, 0)),
            beyond if is_west else inside,
            inside if is_west else beyond,
        )
        upper = jnp.where(is_first, cells, pltpu.roll(cells, 1, 1))
        lower = jnp.where(is_last, cells, pltpu.roll(cells, width - 1, 1))
        out[...] = diffused(cells, upper, lower, sides, numbers)


def interleaved(at, west, east):
    width = at.width
    fields_each = width // 2 // at.levels
    columns = jnp.concatenate([east, west], axis=1)
    source, target = grid_index((2 * width, width))
    out = []
    for first in range(0, at.half, fields_each):
        block = jnp.where(source < width, source, source - width) - first * at.levels
        lane = 2 * block + jnp.where(source < width, 0, 1)
        out.append(placed(columns, (lane == target).astype(F32)))
    return out


def field_step(at, field, state, out, north, south, first_line, beside, number):
    levels, rows, width = at.levels, at.rows, at.width
    fields_each = width // 2 // levels
    lines, lanes = grid_index((rows, width))
    for level in range(levels):
        line = first_line + field * levels + level
        start = (field * levels + level) * rows
        cells = state[pl.ds(start, rows), :]
        first_level, last_level = level == 0, level == levels - 1
        upper = cells if first_level else state[pl.ds(start - rows, rows), :]
        lower = cells if last_level else state[pl.ds(start + rows, rows), :]
        lane = 2 * ((field % fields_each) * levels + level) + 1
        edge = pltpu.roll(beside[field // fields_each], width - lane, 1)
        sides = (
            jnp.where(lines == 0, north[pl.ds(line, 1), :], pltpu.roll(cells, 1, 0)),
            jnp.where(
                lines == rows - 1, south[pl.ds(line, 1), :], pltpu.roll(cells, rows - 1, 0)
            ),
            jnp.where(lanes == 0, edge, pltpu.roll(cells, 1, 1)),
            jnp.where(lanes == width - 1, edge, pltpu.roll(cells, width - 1, 1)),
        )
        out[pl.ds(start, rows), :] = diffused(cells, upper, lower, sides, number)


def steps_kernel(
    at,
    part,
    state_far,
    north,
    south,
    west,
    east,
    far_north,
    far_south,
    near_first,
    near_last,
    first,
    last,
    diffusion,
    *rest,
):
    if part:
        rest = rest[1:]
    out_far, state, middle, out, *ring, arrivals, departures = rest
    rows, width, levels = at.rows, at.width, at.levels
    field_rows = levels * rows
    whole = part * at.half

    def coming(field):
        return pltpu.make_async_copy(
            state_far.at[pl.ds((whole + field) * field_rows, field_rows)],
            state.at[pl.ds(field * field_rows, field_rows)],
            arrivals.at[field],
        )

    def going(field):
        return pltpu.make_async_copy(
            out.at[pl.ds(field * field_rows, field_rows)],
            out_far.at[pl.ds((whole + field) * field_rows, field_rows)],
            departures.at[field],
        )

    for field in range(at.half):
        coming(field).start()
    halos = (north, south, west, east, far_north, far_south)
    ring_step(at, part, halos, (near_first, near_last, first, last), diffusion, ring)
    held = pl.ds(part * rows, rows)
    outer = interleaved(at, west[held, :], east[held, :])
    inner = interleaved(at, ring[2][...], ring[3][...])
    for field in range(at.half):
        number = diffusion[whole + field]
        coming(field).wait()
        field_step(
            at, field, state, middle, north, south, part * at.part, outer, number
        )
        field_step(at, field, middle, out, ring[0], ring[1], 0, inner, number)
        going(field).start()
    for field in range(at.half):
        going(field).wait()


def ocean_kernel(
    at,
    levels,
    ocean_far,
    wet,
    north,
    south,
    west,
    east,
    mixing,
    out_far,
    tops,
    ocean,
    out,
    wests,
    easts,
    arrivals,
    departures,
):
    fields, field_rows = at.sea_blocks // levels, levels * at.sea_rows
    for field in range(fields):
        chunk(ocean_far, ocean, field, field_rows, arrivals.at[field]).start()
    rows, width = at.sea_rows, at.width
    lines, lanes = grid_index((rows, width))
    per_tile = width // rows
    held = pl.ds(at.sea_cols, at.sea_col_rows)
    wests[...] = jnp.transpose(squared(west[held, :]))
    easts[...] = jnp.transpose(squared(east[held, :]))
    wet_cells = wet[...].astype(F32)
    wet_lane = at.sea_tiles
    wet_sides = around(
        wet_cells,
        north[pl.ds(at.wet_row, 1), :],
        south[pl.ds(at.wet_row, 1), :],
        wests[pl.ds(0, rows), :][:, wet_lane : wet_lane + 1],
        easts[pl.ds(0, rows), :][:, wet_lane : wet_lane + 1],
    )

    def field_step(field, carry):
        chunk(ocean_far, ocean, field, field_rows, arrivals.at[field]).wait()
        back = lax.rem(width - field * (levels // per_tile), width)
        west_cols = pltpu.roll(wests[...], back, 1)
        east_cols = pltpu.roll(easts[...], back, 1)
        number = mixing[field] * wet_cells
        for level in range(levels):
            block = field * levels + level
            start = pl.multiple_of(block * rows, rows)
            first_level, last_level = level == 0, level == levels - 1
            cells = ocean[pl.ds(start, rows), :]
            upper = cells if first_level else ocean[pl.ds(start - rows, rows), :]
            lower = cells if last_level else ocean[pl.ds(start + rows, rows), :]
            above = pltpu.roll(cells, 1, 0)
            below = pltpu.roll(cells, rows - 1, 0)
            line = at.atmos_rows + block
            tile, within = level // per_tile, (level % per_tile) * rows
            west_col = pltpu.roll(west_cols[within : within + rows, :], (width - tile) % width, 1)
            east_col = pltpu.roll(east_cols[within : within + rows, :], width - 1 - tile, 1)
            sides = (
                jnp.where(lines == 0, north[pl.ds(line, 1), :], above),
                jnp.where(lines == rows - 1, south[pl.ds(line, 1), :], below),
                jnp.where(lanes == 0, west_col, pltpu.roll(cells, 1, 1)),
                jnp.where(lanes == width - 1, east_col, pltpu.roll(cells, width - 1, 1)),
            )
            total = wet_sides[0] * (sides[0] - cells)
            for side in range(1, 4):
                total = total + wet_sides[side] * (sides[side] - cells)
            tendency = number * total + 0.1 * (upper + lower - 2.0 * cells)
            after = cells + wet_cells * tendency
            out[pl.ds(start, rows), :] = after
            if first_level:
                tops[pl.ds(pl.multiple_of(field * rows, rows), rows), :] = after
        chunk(out, out_far, field, field_rows, departures.at[field]).start()
        return carry

    lax.fori_loop(0, fields, field_step, 0)
    for field in range(fields):
        chunk(out, out_far, field, field_rows, departures.at[field]).wait()


def label_base(rows):
    return 2.0 * rows


def routes_kernel(index, own, diffusion, *rest):
    *outs, labels_out, section, numbers, tally, piece_labels, sea_labels = rest
    lanes = lax.broadcasted_iota(jnp.int32, (1, section.shape[1]), 1)
    section[...] = jnp.full(section.shape, own[0].astype(F32))
    for field in range(diffusion.shape[0]):
        numbers[pl.ds(field, 1), :] = jnp.full(lanes.shape, diffusion[field])

    def clear(at, carry):
        tally[at] = 0
        return carry

    for row, slots, labels in ((0, outs[0], piece_labels), (2, outs[1], sea_labels)):
        slots[...] = jnp.zeros(slots.shape, F32)
        labels[...] = jnp.full(labels.shape, -1.0, F32)
        lax.fori_loop(0, tally.shape[0], clear, 0)
        for tile in range(index.shape[1]):
            owner = index[row, tile]
            rank = tally[owner]
            tally[owner] = rank + 1
            slot = pl.ds(owner * CAPACITY + rank, 1)
            slots[slot, :] = (lanes == tile).astype(F32)
            labels[slot, :] = jnp.full(lanes.shape, index[row + 1, tile].astype(F32))
    base = label_base(index.shape[1])
    labels_out[...] = (piece_labels[...] + 1.0) + base * (sea_labels[...] + 1.0)


def inner_kernel(at, state_far, numbers, out, top, arrival):
    fields, rows, width = at.fields, at.rows, at.width
    copy = pltpu.make_async_copy(state_far.at[:, pl.ds(at.levels - 2, 2)], top, arrival)
    copy.start()
    lines, lanes = grid_index((rows, width))
    copy.wait()
    for field in range(fields):
        cells = top[field, 1]
        sides = (
            jnp.where(lines == 0, 0.0, pltpu.roll(cells, 1, 0)),
            jnp.where(lines == rows - 1, 0.0, pltpu.roll(cells, rows - 1, 0)),
            jnp.where(lanes == 0, 0.0, pltpu.roll(cells, 1, 1)),
            jnp.where(lanes == width - 1, 0.0, pltpu.roll(cells, width - 1, 1)),
        )
        out[pl.ds(field * rows, rows), :] = diffused(
            cells, top[field, 0], cells, sides, numbers[pl.ds(field, 1), :]
        )


def pieces_kernel(
    at, inner, north, south, west, east, weights, numbers, routes, labels, out, surface, products
):
    fields, levels, rows, width = at.fields, at.levels, at.rows, at.width
    slots = routes.shape[0]
    lines, lanes = grid_index((rows, width))
    a = []
    for field in range(fields):
        part = field // at.half
        held = pl.ds(part * rows, rows)
        lane = (field % at.half) * levels + levels - 1
        line = pl.ds(part * at.part + lane, 1)
        outside = (
            jnp.where(lines == 0, north[line, :], 0.0)
            + jnp.where(lines == rows - 1, south[line, :], 0.0)
            + jnp.where(lanes == 0, pltpu.roll(west[held, :], (width - lane) % width, 1), 0.0)
            + jnp.where(lanes == width - 1, pltpu.roll(east[held, :], width - 1 - lane, 1), 0.0)
        )
        a.append(inner[pl.ds(field * rows, rows), :] + numbers[pl.ds(field, 1), :] * outside)
    sums = (a[0] - a[4], a[1], a[2], a[3], a[6] + a[7], a[5] + a[8], a[9])
    for place in range(16):
        surface[pl.ds(place * rows, rows), :] = (
            sums[place] if place < len(sums) else jnp.zeros((rows, width), F32)
        )
    for tile in range(rows):
        products[pl.ds(tile * 16, 16), :] = remapped(
            surface[pl.ds(tile, 16, stride=rows), :], weights[tile]
        )
    count = PIECE_ROWS - 1
    sent = picked(
        routes[...][:, :rows],
        jnp.concatenate(
            [products[pl.ds(place, rows, stride=16), :] for place in range(count)], axis=1
        ),
    )
    for place in range(count):
        out[pl.ds(place, slots, stride=PIECE_ROWS), :] = sent[:, place * width : (place + 1) * width]
    out[pl.ds(count, slots, stride=PIECE_ROWS), :] = labels[...]


def flux_kernel(sizes, arrived, remap, routes, out, gather, sea_labels, fluxes, products):
    flux_count, rows, sections = sizes
    width = out.shape[1]
    slots = routes.shape[0]
    count = PIECE_ROWS - 1
    labels = arrived[pl.ds(count, slots, stride=PIECE_ROWS), :]
    upper = jnp.floor(labels * (1.0 / label_base(rows)))
    select = one_hot(labels - label_base(rows) * upper - 1.0)
    gather[...] = select
    sea_labels[...] = upper - 1.0
    values = jnp.concatenate(
        [arrived[pl.ds(place, slots, stride=PIECE_ROWS), :] for place in range(count)], axis=1
    )
    exchange = picked(jnp.transpose(select)[:rows, :], values)
    a04, a1, a2, a3, a67, a58, a9 = (
        exchange[:, place * width : (place + 1) * width] for place in range(count)
    )
    speed = jnp.sqrt(a2 * a2 + a3 * a3 + 0.5)
    fluxes[pl.ds(0, rows), :] = speed * a04 + a67
    fluxes[pl.ds(rows, rows), :] = speed * a1 + a58
    fluxes[pl.ds(2 * rows, rows), :] = speed * a2 * (1.0 + 0.2 * jnp.tanh(a9))
    fluxes[pl.ds(3 * rows, rows), :] = speed * a3
    for tile in range(rows):
        products[pl.ds(tile * flux_count, flux_count), :] = remapped(
            fluxes[pl.ds(tile, flux_count, stride=rows), :], both_halves(remap[tile])
        )
    sent = picked(
        routes[...][:, :rows],
        jnp.concatenate(
            [products[pl.ds(flux, rows, stride=flux_count), :] for flux in range(flux_count)],
            axis=1,
        ),
    )
    for flux in range(flux_count):
        for section in range(sections):
            out[pl.ds(section * slots * flux_count + flux, slots, stride=flux_count), :] = sent[
                :, flux * width : (flux + 1) * width
            ]


def sea_kernel(
    sizes, landed, base_tops, wet, own_labels, other_labels, section, tops, answers
):
    flux_count, sea_rows = sizes
    width = landed.shape[1]
    slots = own_labels.shape[0]
    mine = one_hot(own_labels[...])
    others = one_hot(other_labels[...])
    is_first = section[0:1, :] == 0.0
    select = jnp.concatenate(
        [jnp.where(is_first, mine, others), jnp.where(is_first, others, mine)], axis=0
    )
    values = jnp.concatenate(
        [landed[pl.ds(flux, 2 * slots, stride=flux_count), :] for flux in range(flux_count)], axis=1
    )
    forcing = picked(jnp.transpose(select)[:sea_rows, :], values)
    wet_cells = wet[...].astype(F32)
    for flux in range(flux_count):
        held = pl.ds(flux * sea_rows, sea_rows)
        tops[held, :] = base_tops[held, :] + wet_cells * (
            FORCING_SCALE[flux] * forcing[:, flux * width : (flux + 1) * width]
        )
    all_tops = jnp.concatenate(
        [tops[pl.ds(flux * sea_rows, sea_rows), :] for flux in range(flux_count)], axis=1
    )
    reply = picked(mine[:, :sea_rows], all_tops)
    for flux in range(flux_count):
        answers[pl.ds(flux, slots, stride=flux_count), :] = reply[
            :, flux * width : (flux + 1) * width
        ]


def store_kernel(sea_rows, tops, base, out, leave):
    copies = [
        pltpu.make_async_copy(
            tops.at[pl.ds(flux * sea_rows, sea_rows)], out.at[flux, 0], leave.at[flux]
        )
        for flux in range(out.shape[0])
    ]
    for copy in copies:
        copy.start()
    for copy in copies:
        copy.wait()


def tops_of_tiles(returned, routes, flux_count, scratch):
    slots, width = routes.shape
    rows = scratch.shape[0] // flux_count
    found = picked(
        jnp.transpose(routes[...])[:rows, :],
        jnp.concatenate(
            [returned[pl.ds(flux, slots, stride=flux_count), :] for flux in range(flux_count)],
            axis=1,
        ),
    )
    for flux in range(flux_count):
        scratch[pl.ds(flux, rows, stride=flux_count), :] = found[
            :, flux * width : (flux + 1) * width
        ]


def reply_kernel(flux_count, answered, remap, routes, gather, out, tops, on_exchange):
    slots, width = routes.shape
    rows = remap.shape[0]
    tops_of_tiles(answered, routes, flux_count, tops)
    for tile in range(rows):
        held = pl.ds(tile * flux_count, flux_count)
        on_exchange[held, :] = remapped(
            tops[held, :], both_halves(jnp.transpose(remap[tile]))
        )
    values = jnp.concatenate(
        [on_exchange[pl.ds(flux, rows, stride=flux_count), :] for flux in range(flux_count)], axis=1
    )
    replies = picked(gather[...][:, :rows], values)
    for flux in range(flux_count):
        out[pl.ds(flux, slots, stride=flux_count), :] = replies[
            :, flux * width : (flux + 1) * width
        ]


def surface_kernel(flux_count, returned, weights, routes, out, tops):
    rows = weights.shape[0]
    tops_of_tiles(returned, routes, flux_count, tops)
    for tile in range(rows):
        out[pl.ds(tile, flux_count, stride=rows), :] = remapped(
            tops[pl.ds(tile * flux_count, flux_count), :], weights[tile]
        )


VMEM = pl.BlockSpec(memory_space=pltpu.VMEM)
SMEM = pl.BlockSpec(memory_space=pltpu.SMEM)
ANY = pl.BlockSpec(memory_space=pl.ANY)


def array(*shape):
    return jax.ShapeDtypeStruct(shape, F32)


def call(kernel, name, outs, in_specs, scratch=(), after=(), limit=VMEM_LIMIT, work=1_000_000, **more):
    def body(*refs):
        kernel(*refs[: len(in_specs)], *refs[len(in_specs) + len(after) :])

    run = pl.pallas_call(
        body,
        name=name,
        out_shape=outs,
        in_specs=list(in_specs) + [ANY] * len(after),
        scratch_shapes=list(scratch),
        compiler_params=pltpu.CompilerParams(vmem_limit_bytes=limit),
        cost_estimate=pl.CostEstimate(flops=0, bytes_accessed=work, transcendentals=0),
        **more,
    )
    return lambda *arguments: run(*arguments, *after)


def gated(values, before):
    return lax.optimization_barrier((values, before))[0]


def on_device(
    atmos_state,
    atmos_diffusion,
    remap_atmos,
    exchange_owner,
    exchange_slot,
    remap_ocean,
    ocean_owner,
    ocean_slot,
    ocean_state,
    ocean_mixing,
    wet_mask,
):
    targets = lax.axis_size(SECTION)
    sections = lax.axis_size("comp")
    devices = targets * sections
    fields, levels, rows, width = atmos_state.shape
    sea_fields, sea_levels, sea_rows, _ = ocean_state.shape
    blocks = fields * levels
    sea_blocks = sea_fields * sea_levels
    at = Edges(fields, levels, rows, sea_blocks, sea_rows, width)
    slots = targets * CAPACITY
    ring = ("comp", "gx")

    index = jnp.stack([exchange_owner[:, 0], exchange_slot, ocean_owner[:, 0], ocean_slot])
    section = lax.axis_index("comp").astype(jnp.int32).reshape(1)
    state = atmos_state.reshape(blocks * rows, width)
    ocean = ocean_state.reshape(sea_blocks * sea_rows, width)

    state_copy = pltpu.VMEM((blocks * rows, width), F32)
    ocean_copy = pltpu.VMEM((sea_blocks * sea_rows, width), F32)
    ocean_flags = pltpu.SemaphoreType.DMA((sea_fields,))
    near_first, near_last, far_first, far_last, first_cols, last_cols = call(
        functools.partial(edges_kernel, at),
        "edges",
        (array(at.near_rows, width),) * 2
        + (array(at.far_rows, width),) * 2
        + (array(at.col_rows, width),) * 2,
        [ANY],
        [state_copy, pltpu.SemaphoreType.DMA((fields,))],
        limit=EDGES_LIMIT,
    )(state)
    near_first, near_last, first_cols, last_cols = call(
        functools.partial(sea_edges_kernel, at),
        "sea_edges",
        (array(at.near_rows, width),) * 2 + (array(at.col_rows, width),) * 2,
        [VMEM] * 6,
    )(ocean, wet_mask, near_first, near_last, first_cols, last_cols)
    north = shifted(near_last, ring, 1)
    south = shifted(near_first, ring, -1)
    west = shifted(last_cols, "gy", 1)
    east = shifted(first_cols, "gy", -1)

    def weights_of(remap, transposed, name, before):
        return call(
            functools.partial(weights_kernel, transposed),
            name,
            jax.ShapeDtypeStruct((rows, 2 * width, width), BF16),
            [VMEM],
        )(gated(remap, before))

    tile_slots, sea_slots, labels, here, numbers = call(
        routes_kernel,
        "routes",
        (array(slots, width),) * 3 + (array(8, width), array(-(-fields // 8) * 8, width)),
        [SMEM] * 3,
        [pltpu.SMEM((targets,), jnp.int32)] + [pltpu.VMEM((slots, width), F32)] * 2,
    )(gated(index, first_cols), section, atmos_diffusion)
    inner = call(
        functools.partial(inner_kernel, at),
        "inner",
        array(fields * rows, width),
        [ANY, VMEM],
        [pltpu.VMEM((fields, 2, rows, width), F32), pltpu.SemaphoreType.DMA],
    )(gated(atmos_state, first_cols), numbers)
    pieces = call(
        functools.partial(pieces_kernel, at),
        "pieces",
        array(slots * PIECE_ROWS, width),
        [VMEM] * 9,
        [pltpu.VMEM((16 * rows, width), F32)] * 2,
    )(
        inner,
        north,
        south,
        west,
        east,
        weights_of(remap_atmos, False, "piece_weights", first_cols),
        numbers,
        tile_slots,
        labels,
    )
    arrived = lax.all_to_all(
        pieces.reshape(targets, CAPACITY * PIECE_ROWS, width), SECTION, 0, 0, tiled=True
    )
    outgoing, gather, own_labels = call(
        functools.partial(flux_kernel, (sea_fields, rows, sections)),
        "fluxes",
        (
            array(sections * slots * sea_fields, width),
            array(slots, width),
            array(slots, width),
        ),
        [VMEM] * 3,
        [pltpu.VMEM((sea_fields * rows, width), F32)] * 2,
    )(arrived.reshape(slots * PIECE_ROWS, width), remap_ocean, sea_slots)
    landed = lax.all_to_all(
        outgoing.reshape(devices, CAPACITY * sea_fields, width), EVERY, 0, 0, tiled=True
    )
    other_labels = shifted(own_labels, "comp", 1)
    to_north, to_south = call(
        functools.partial(corners_kernel, at),
        "corners",
        (array(at.far_rows, width),) * 2,
        [VMEM] * 4,
        after=(outgoing,),
    )(far_first, far_last, west, east)
    far_north = shifted(to_south, ring, 1)
    far_south = shifted(to_north, ring, -1)

    sea_base, base_tops = call(
        functools.partial(ocean_kernel, at, sea_levels),
        "sea_base",
        (array(sea_blocks * sea_rows, width), array(sea_fields * sea_rows, width)),
        [ANY] + [VMEM] * 5 + [SMEM],
        [ocean_copy] * 2 + [pltpu.VMEM((width, width), F32)] * 2 + [ocean_flags] * 2,
        after=(outgoing,),
        limit=SEA_LIMIT,
        work=1_000_000_000,
        out_specs=(ANY, VMEM),
    )(ocean, wet_mask, north, south, west, east, ocean_mixing)

    tops, answers = call(
        functools.partial(sea_kernel, (sea_fields, sea_rows)),
        "sea_top",
        (array(sea_fields * sea_rows, width), array(slots * sea_fields, width)),
        [VMEM] * 6,
        after=(far_north, far_south),
    )(
        landed.reshape(devices * CAPACITY * sea_fields, width),
        base_tops,
        wet_mask,
        own_labels,
        other_labels,
        here,
    )
    ocean_next = call(
        functools.partial(store_kernel, sea_rows),
        "store",
        array(sea_fields, sea_levels, sea_rows, width),
        [VMEM, ANY],
        [ocean_flags],
        out_specs=ANY,
        input_output_aliases={1: 0},
    )(tops, sea_base.reshape(sea_fields, sea_levels, sea_rows, width))
    answered = lax.all_to_all(
        answers.reshape(targets, CAPACITY * sea_fields, width), SECTION, 0, 0, tiled=True
    )
    def both_steps(part, before, **more):
        return call(
            functools.partial(steps_kernel, at, part),
            "steps_" + "ab"[part],
            array(blocks * rows, width),
            [ANY] + [VMEM] * 10 + [SMEM] + [ANY] * part,
            [pltpu.VMEM((at.part * rows, width), F32)] * 3
            + [pltpu.VMEM((at.ring_rows, width), F32)] * 2
            + [pltpu.VMEM((rows, width), F32)] * 2
            + [pltpu.SemaphoreType.DMA((at.half,))] * 2,
            after=(before,),
            limit=STEPS_LIMIT,
            work=1_000_000_000,
            out_specs=ANY,
            **more,
        )

    halos = (north, south, west, east, far_north, far_south)
    halos += (near_first, near_last, first_cols, last_cols)
    atmos_next = both_steps(0, answers)(state, *halos, atmos_diffusion)
    answered, atmos_next, ocean_next = lax.optimization_barrier((answered, atmos_next, ocean_next))

    replies = call(
        functools.partial(reply_kernel, sea_fields),
        "replies",
        array(slots * sea_fields, width),
        [VMEM] * 4,
        [pltpu.VMEM((sea_fields * rows, width), F32)] * 2,
    )(answered.reshape(slots * sea_fields, width), remap_ocean, sea_slots, gather)
    returned = lax.all_to_all(
        replies.reshape(targets, CAPACITY * sea_fields, width), SECTION, 0, 0, tiled=True
    )
    atmos_next = both_steps(1, replies, input_output_aliases={12: 0})(
        state, *halos, atmos_diffusion, atmos_next
    )
    ocean_surface = call(
        functools.partial(surface_kernel, sea_fields),
        "surface",
        array(sea_fields * rows, width),
        [VMEM] * 3,
        [pltpu.VMEM((sea_fields * rows, width), F32)],
    )(
        returned.reshape(slots * sea_fields, width),
        weights_of(remap_atmos, True, "surface_weights", replies),
        tile_slots,
    )
    return (
        atmos_next.reshape(atmos_state.shape),
        ocean_next,
        ocean_surface.reshape(sea_fields, rows, width),
    )


def solution(mesh):
    in_specs = (
        P(None, None, ("comp", "gx"), "gy"),
        P(),
        P(("comp", "gx", "gy"), None, None),
        P(("comp", "gx", "gy"), None),
        P(("comp", "gx", "gy")),
        P(("comp", "gx", "gy"), None, None),
        P(("comp", "gx", "gy"), None),
        P(("comp", "gx", "gy")),
        P(None, None, "gx", "gy"),
        P(),
        P("gx", "gy"),
    )
    out_specs = (
        P(None, None, ("comp", "gx"), "gy"),
        P(None, None, "gx", "gy"),
        P(None, ("comp", "gx"), "gy"),
    )
    return jax.shard_map(
        on_device, mesh=mesh, in_specs=in_specs, out_specs=out_specs, check_vma=False
    )
```

```python
import functools

import jax
import jax.numpy as jnp
from jax import lax
from jax.experimental import pallas as pl
from jax.experimental.pallas import tpu as pltpu
from jax.sharding import PartitionSpec as P

F32 = jnp.float32
BF16 = jnp.bfloat16
FORCING_SCALE = (0.1, -0.1, 0.1, 0.1)
SECTION = ("gx", "gy")
EVERY = ("comp", "gx", "gy")
CAPACITY = 2
PIECE_ROWS = 8
VMEM_LIMIT = 8 * 1024 * 1024
EDGES_LIMIT = 52 * 1024 * 1024
SEA_LIMIT = 53 * 1024 * 1024
STEPS_LIMIT = 53 * 1024 * 1024


def shifted(block, axis, distance):
    devices = range(lax.axis_size(axis))
    route = [((i - distance) % len(devices), i) for i in devices]
    return lax.ppermute(block, axis, route)


def dot(left, right, transposed=False):
    dims = (((1,), (1 if transposed else 0,)), ((), ()))
    return lax.dot_general(left, right, dims, preferred_element_type=F32)


def halves(values):
    high = values.astype(BF16)
    return high, (values - high.astype(F32)).astype(BF16)


def remapped(rows, weights):
    count, width = rows.shape
    high, low = halves(rows)
    if count < 16:
        filler = jnp.zeros((16 - count, width), F32)
        high, low = halves(jnp.concatenate([rows, filler], axis=0))
    left = jnp.concatenate(
        [
            jnp.concatenate([high, high], axis=1),
            jnp.concatenate([low, jnp.zeros(low.shape, BF16)], axis=1),
        ],
        axis=0,
    )
    product = dot(left, weights)
    return product[:count, :] + product[16 : 16 + count, :]


def both_halves(block):
    return jnp.concatenate(halves(block), axis=0)


def weights_kernel(transposed, remap, weights):
    for tile in range(remap.shape[0]):
        block = remap[tile]
        weights[tile] = both_halves(jnp.transpose(block) if transposed else block)


def picked(selection, values):
    chosen = selection.astype(BF16)
    high = values.astype(BF16)
    rest = values - high.astype(F32)
    middle = rest.astype(BF16)
    low = (rest - middle.astype(F32)).astype(BF16)
    return dot(chosen, high) + dot(chosen, middle) + dot(chosen, low)


def placed(values, selection):
    chosen = selection.astype(BF16)
    high = values.astype(BF16)
    rest = values - high.astype(F32)
    middle = rest.astype(BF16)
    low = (rest - middle.astype(F32)).astype(BF16)
    return dot(high, chosen) + dot(middle, chosen) + dot(low, chosen)


def one_hot(labels):
    lanes = lax.broadcasted_iota(jnp.int32, labels.shape, 1).astype(F32)
    return (labels == lanes).astype(F32)


def grid_index(shape):
    return lax.broadcasted_iota(jnp.int32, shape, 0), lax.broadcasted_iota(jnp.int32, shape, 1)


def around(cells, north, south, west, east):
    rows, lanes = grid_index(cells.shape)
    row_count, width = cells.shape
    return (
        jnp.where(rows == 0, north, pltpu.roll(cells, 1, 0)),
        jnp.where(rows == row_count - 1, south, pltpu.roll(cells, row_count - 1, 0)),
        jnp.where(lanes == 0, west, pltpu.roll(cells, 1, 1)),
        jnp.where(lanes == width - 1, east, pltpu.roll(cells, width - 1, 1)),
    )


def diffused(cells, upper, lower, sides, diffusion):
    beside = sides[0] + sides[1] + sides[2] + sides[3] - 4.0 * cells
    return cells + diffusion * beside + 0.1 * (upper + lower - 2.0 * cells)


class Edges:
    def __init__(self, fields, levels, rows, sea_blocks, sea_rows, width):
        self.fields, self.levels, self.rows, self.width = fields, levels, rows, width
        self.sea_blocks, self.sea_rows = sea_blocks, sea_rows
        self.half = fields // 2
        self.part = self.half * levels
        self.ring_rows = -(-self.part // 8) * 8
        self.atmos_rows = 2 * self.part
        self.wet_row = self.atmos_rows + sea_blocks
        self.near_rows = -(-(self.wet_row + 1) // 8) * 8
        self.corner_row = self.atmos_rows
        self.far_rows = -(-(self.atmos_rows + 4) // 8) * 8
        self.sea_tiles = sea_blocks * sea_rows // width
        self.sea_cols = 4 * rows
        self.sea_col_rows = -(-(self.sea_tiles + 1) // 8) * 8
        self.col_rows = self.sea_cols + self.sea_col_rows


def squared(values):
    rows, width = values.shape
    if rows == width:
        return values
    return jnp.concatenate([values, jnp.zeros((width - rows, width), F32)], axis=0)


def chunk(source, target, at, rows, arrival):
    part = pl.ds(pl.multiple_of(at * rows, 8), rows)
    return pltpu.make_async_copy(source.at[part], target.at[part], arrival)


def edges_kernel(
    at, state_far, near_first, near_last, far_first, far_last, first, last, state, arrivals
):
    rows, part, width = at.rows, at.part, at.width
    field_rows = at.levels * rows
    copies = [
        chunk(state_far, state, field, field_rows, arrivals.at[field])
        for field in range(at.fields)
    ]
    for copy in copies:
        copy.start()
    for out in (near_first, near_last, far_first, far_last):
        out[...] = jnp.zeros(out.shape, F32)
    for cols in (first, last):
        cols[pl.ds(at.sea_cols, at.sea_col_rows), :] = jnp.zeros((at.sea_col_rows, width), F32)
    for half in range(2):
        for field in range(half * at.half, (half + 1) * at.half):
            copies[field].wait()
        for row in range(rows):
            lines = state[pl.ds(half * part * rows + row, part, stride=rows), :]
            held = pl.ds(half * at.part, part)
            if row < 2:
                (near_first, far_first)[row][held, :] = lines
            if row >= rows - 2:
                (near_last, far_last)[rows - 1 - row][held, :] = lines
            turned = jnp.transpose(squared(lines))
            near, far = half * rows + row, (2 + half) * rows + row
            first[pl.ds(near, 1), :] = turned[0:1, :]
            first[pl.ds(far, 1), :] = turned[1:2, :]
            last[pl.ds(near, 1), :] = turned[width - 1 : width, :]
            last[pl.ds(far, 1), :] = turned[width - 2 : width - 1, :]


def sea_edges_kernel(at, ocean, wet, near_first, near_last, first, last, *outs):
    width = at.width
    for out, rows in zip(outs, (near_first, near_last, first, last)):
        out[...] = rows[...]
    for out, sea_row in ((outs[0], 0), (outs[1], at.sea_rows - 1)):
        out[pl.ds(at.atmos_rows, at.sea_blocks), :] = ocean[
            pl.ds(sea_row, at.sea_blocks, stride=at.sea_rows), :
        ]
        out[pl.ds(at.wet_row, 1), :] = wet[pl.ds(sea_row, 1), :].astype(F32)
    for tile in range(at.sea_tiles + 1):
        if tile < at.sea_tiles:
            lines = ocean[pl.ds(tile * width, width), :]
        else:
            lines = squared(wet[...].astype(F32))
        turned = jnp.transpose(lines)
        outs[2][pl.ds(at.sea_cols + tile, 1), :] = turned[0:1, :]
        outs[3][pl.ds(at.sea_cols + tile, 1), :] = turned[width - 1 : width, :]


def corners_kernel(at, far_first, far_last, west, east, to_north, to_south):
    for out, lines, row in ((to_north, far_first, 0), (to_south, far_last, at.rows - 1)):
        out[...] = lines[...]
        for place, (cols, half) in enumerate(((west, 0), (west, 1), (east, 0), (east, 1))):
            out[pl.ds(at.corner_row + place, 1), :] = cols[pl.ds(half * at.rows + row, 1), :]


def spread(at, diffusion, part, places):
    numbers = jnp.zeros(places.shape, F32)
    is_first = places < 0
    is_last = places < 0
    for field in range(at.half):
        start = field * at.levels
        numbers = jnp.where(places >= start, diffusion[part * at.half + field], numbers)
        is_first = is_first | (places == start)
        is_last = is_last | (places == start + at.levels - 1)
    return numbers, is_first, is_last


def ring_step(at, part, halos, edges, diffusion, outs):
    north, south, west, east, far_north, far_south = halos
    near_first, near_last, first, last = edges
    rows, width = at.rows, at.width
    shape = (at.ring_rows, width)
    held = pl.ds(part * at.part, shape[0])
    lines, lanes = grid_index(shape)
    numbers, is_first, is_last = spread(at, diffusion, part, lines)
    for out, outside, further, own, is_north in (
        (outs[0], north, far_north, near_first, True),
        (outs[1], south, far_south, near_last, False),
    ):
        turned = jnp.transpose(squared(further[pl.ds(at.corner_row, 8), :]))[: shape[0], :]
        cells, beyond, inside = outside[held, :], further[held, :], own[held, :]
        west_col = jnp.where(lanes == 0, turned[:, part : part + 1], pltpu.roll(cells, 1, 1))
        east_col = jnp.where(
            lanes == width - 1, turned[:, 2 + part : 3 + part], pltpu.roll(cells, width - 1, 1)
        )
        sides = (
            beyond if is_north else inside,
            inside if is_north else beyond,
            west_col,
            east_col,
        )
        upper = jnp.where(is_first, cells, pltpu.roll(cells, 1, 0))
        lower = jnp.where(is_last, cells, pltpu.roll(cells, shape[0] - 1, 0))
        out[...] = diffused(cells, upper, lower, sides, numbers)

    shape = (rows, width)
    near, far = pl.ds(part * rows, rows), pl.ds((2 + part) * rows, rows)
    lines, lanes = grid_index(shape)
    numbers, is_first, is_last = spread(at, diffusion, part, lanes)
    for out, outside, own, corner, is_west in (
        (outs[2], west, first, 0, True),
        (outs[3], east, last, 2, False),
    ):
        cells, beyond, inside = outside[near, :], outside[far, :], own[near, :]
        place = pl.ds(at.corner_row + corner + part, 1)
        sides = (
            jnp.where(lines == 0, far_north[place, :], pltpu.roll(cells, 1, 0)),
            jnp.where(lines == rows - 1, far_south[place, :], pltpu.roll(cells, rows - 1, 0)),
            beyond if is_west else inside,
            inside if is_west else beyond,
        )
        upper = jnp.where(is_first, cells, pltpu.roll(cells, 1, 1))
        lower = jnp.where(is_last, cells, pltpu.roll(cells, width - 1, 1))
        out[...] = diffused(cells, upper, lower, sides, numbers)


def interleaved(at, west, east):
    width = at.width
    fields_each = width // 2 // at.levels
    columns = jnp.concatenate([east, west], axis=1)
    source, target = grid_index((2 * width, width))
    out = []
    for first in range(0, at.half, fields_each):
        block = jnp.where(source < width, source, source - width) - first * at.levels
        lane = 2 * block + jnp.where(source < width, 0, 1)
        out.append(placed(columns, (lane == target).astype(F32)))
    return out


def field_step(at, field, state, out, north, south, first_line, beside, number):
    levels, rows, width = at.levels, at.rows, at.width
    fields_each = width // 2 // levels
    lines, lanes = grid_index((rows, width))
    for level in range(levels):
        line = first_line + field * levels + level
        start = (field * levels + level) * rows
        cells = state[pl.ds(start, rows), :]
        first_level, last_level = level == 0, level == levels - 1
        upper = cells if first_level else state[pl.ds(start - rows, rows), :]
        lower = cells if last_level else state[pl.ds(start + rows, rows), :]
        lane = 2 * ((field % fields_each) * levels + level) + 1
        edge = pltpu.roll(beside[field // fields_each], width - lane, 1)
        sides = (
            jnp.where(lines == 0, north[pl.ds(line, 1), :], pltpu.roll(cells, 1, 0)),
            jnp.where(
                lines == rows - 1, south[pl.ds(line, 1), :], pltpu.roll(cells, rows - 1, 0)
            ),
            jnp.where(lanes == 0, edge, pltpu.roll(cells, 1, 1)),
            jnp.where(lanes == width - 1, edge, pltpu.roll(cells, width - 1, 1)),
        )
        out[pl.ds(start, rows), :] = diffused(cells, upper, lower, sides, number)


def steps_kernel(
    at,
    state_far,
    north,
    south,
    west,
    east,
    far_north,
    far_south,
    near_first,
    near_last,
    first,
    last,
    diffusion,
    tops,
    sea_before,
    out_far,
    sea_out,
    state,
    middle,
    out,
    *rest,
):
    *rings, arrivals, departures, sea_departures = rest
    rows, levels = at.rows, at.levels
    field_rows = levels * rows

    def coming(field):
        return chunk(state_far, state, field, field_rows, arrivals.at[field])

    def going(field):
        return chunk(out, out_far, field, field_rows, departures.at[field])

    for field in range(at.fields):
        coming(field).start()
    stored = [
        pltpu.make_async_copy(
            tops.at[pl.ds(flux * at.sea_rows, at.sea_rows)],
            sea_out.at[flux, 0],
            sea_departures.at[flux],
        )
        for flux in range(sea_out.shape[0])
    ]
    for copy in stored:
        copy.start()
    halos = (north, south, west, east, far_north, far_south)
    for part in range(2):
        ring = rings[4 * part : 4 * part + 4]
        ring_step(at, part, halos, (near_first, near_last, first, last), diffusion, ring)
    for part in range(2):
        ring = rings[4 * part : 4 * part + 4]
        held = pl.ds(part * rows, rows)
        outer = interleaved(at, west[held, :], east[held, :])
        inner = interleaved(at, ring[2][...], ring[3][...])
        cells = pl.ds(part * at.part * rows, at.part * rows)
        parts = [array.at[cells] for array in (state, middle, out)]
        for field in range(at.half):
            whole = part * at.half + field
            number = diffusion[whole]
            coming(whole).wait()
            field_step(
                at, field, parts[0], parts[1], north, south, part * at.part, outer, number
            )
            field_step(at, field, parts[1], parts[2], ring[0], ring[1], 0, inner, number)
            going(whole).start()
    for copy in stored:
        copy.wait()
    for field in range(at.fields):
        going(field).wait()


def ocean_kernel(
    at,
    levels,
    ocean_far,
    wet,
    north,
    south,
    west,
    east,
    mixing,
    out_far,
    tops,
    ocean,
    out,
    wests,
    easts,
    arrivals,
    departures,
):
    fields, field_rows = at.sea_blocks // levels, levels * at.sea_rows
    for field in range(fields):
        chunk(ocean_far, ocean, field, field_rows, arrivals.at[field]).start()
    rows, width = at.sea_rows, at.width
    lines, lanes = grid_index((rows, width))
    per_tile = width // rows
    held = pl.ds(at.sea_cols, at.sea_col_rows)
    wests[...] = jnp.transpose(squared(west[held, :]))
    easts[...] = jnp.transpose(squared(east[held, :]))
    wet_cells = wet[...].astype(F32)
    wet_lane = at.sea_tiles
    wet_sides = around(
        wet_cells,
        north[pl.ds(at.wet_row, 1), :],
        south[pl.ds(at.wet_row, 1), :],
        wests[pl.ds(0, rows), :][:, wet_lane : wet_lane + 1],
        easts[pl.ds(0, rows), :][:, wet_lane : wet_lane + 1],
    )

    def field_step(field, carry):
        chunk(ocean_far, ocean, field, field_rows, arrivals.at[field]).wait()
        back = lax.rem(width - field * (levels // per_tile), width)
        west_cols = pltpu.roll(wests[...], back, 1)
        east_cols = pltpu.roll(easts[...], back, 1)
        number = mixing[field] * wet_cells
        for level in range(levels):
            block = field * levels + level
            start = pl.multiple_of(block * rows, rows)
            first_level, last_level = level == 0, level == levels - 1
            cells = ocean[pl.ds(start, rows), :]
            upper = cells if first_level else ocean[pl.ds(start - rows, rows), :]
            lower = cells if last_level else ocean[pl.ds(start + rows, rows), :]
            above = pltpu.roll(cells, 1, 0)
            below = pltpu.roll(cells, rows - 1, 0)
            line = at.atmos_rows + block
            tile, within = level // per_tile, (level % per_tile) * rows
            west_col = pltpu.roll(west_cols[within : within + rows, :], (width - tile) % width, 1)
            east_col = pltpu.roll(east_cols[within : within + rows, :], width - 1 - tile, 1)
            sides = (
                jnp.where(lines == 0, north[pl.ds(line, 1), :], above),
                jnp.where(lines == rows - 1, south[pl.ds(line, 1), :], below),
                jnp.where(lanes == 0, west_col, pltpu.roll(cells, 1, 1)),
                jnp.where(lanes == width - 1, east_col, pltpu.roll(cells, width - 1, 1)),
            )
            total = wet_sides[0] * (sides[0] - cells)
            for side in range(1, 4):
                total = total + wet_sides[side] * (sides[side] - cells)
            tendency = number * total + 0.1 * (upper + lower - 2.0 * cells)
            after = cells + wet_cells * tendency
            out[pl.ds(start, rows), :] = after
            if first_level:
                tops[pl.ds(pl.multiple_of(field * rows, rows), rows), :] = after
        chunk(out, out_far, field, field_rows, departures.at[field]).start()
        return carry

    lax.fori_loop(0, fields, field_step, 0)
    for field in range(fields):
        chunk(out, out_far, field, field_rows, departures.at[field]).wait()


def label_base(rows):
    return 2.0 * rows


def routes_kernel(index, own, diffusion, *rest):
    *outs, labels_out, section, numbers, tally, piece_labels, sea_labels = rest
    lanes = lax.broadcasted_iota(jnp.int32, (1, section.shape[1]), 1)
    section[...] = jnp.full(section.shape, own[0].astype(F32))
    for field in range(diffusion.shape[0]):
        numbers[pl.ds(field, 1), :] = jnp.full(lanes.shape, diffusion[field])

    def clear(at, carry):
        tally[at] = 0
        return carry

    for row, slots, labels in ((0, outs[0], piece_labels), (2, outs[1], sea_labels)):
        slots[...] = jnp.zeros(slots.shape, F32)
        labels[...] = jnp.full(labels.shape, -1.0, F32)
        lax.fori_loop(0, tally.shape[0], clear, 0)
        for tile in range(index.shape[1]):
            owner = index[row, tile]
            rank = tally[owner]
            tally[owner] = rank + 1
            slot = pl.ds(owner * CAPACITY + rank, 1)
            slots[slot, :] = (lanes == tile).astype(F32)
            labels[slot, :] = jnp.full(lanes.shape, index[row + 1, tile].astype(F32))
    base = label_base(index.shape[1])
    labels_out[...] = (piece_labels[...] + 1.0) + base * (sea_labels[...] + 1.0)


def inner_kernel(at, state_far, numbers, out, top, arrival):
    fields, rows, width = at.fields, at.rows, at.width
    copy = pltpu.make_async_copy(state_far.at[:, pl.ds(at.levels - 2, 2)], top, arrival)
    copy.start()
    lines, lanes = grid_index((rows, width))
    copy.wait()
    for field in range(fields):
        cells = top[field, 1]
        sides = (
            jnp.where(lines == 0, 0.0, pltpu.roll(cells, 1, 0)),
            jnp.where(lines == rows - 1, 0.0, pltpu.roll(cells, rows - 1, 0)),
            jnp.where(lanes == 0, 0.0, pltpu.roll(cells, 1, 1)),
            jnp.where(lanes == width - 1, 0.0, pltpu.roll(cells, width - 1, 1)),
        )
        out[pl.ds(field * rows, rows), :] = diffused(
            cells, top[field, 0], cells, sides, numbers[pl.ds(field, 1), :]
        )


def pieces_kernel(
    at, inner, north, south, west, east, weights, numbers, routes, labels, out, surface, products
):
    fields, levels, rows, width = at.fields, at.levels, at.rows, at.width
    slots = routes.shape[0]
    lines, lanes = grid_index((rows, width))
    a = []
    for field in range(fields):
        part = field // at.half
        held = pl.ds(part * rows, rows)
        lane = (field % at.half) * levels + levels - 1
        line = pl.ds(part * at.part + lane, 1)
        outside = (
            jnp.where(lines == 0, north[line, :], 0.0)
            + jnp.where(lines == rows - 1, south[line, :], 0.0)
            + jnp.where(lanes == 0, pltpu.roll(west[held, :], (width - lane) % width, 1), 0.0)
            + jnp.where(lanes == width - 1, pltpu.roll(east[held, :], width - 1 - lane, 1), 0.0)
        )
        a.append(inner[pl.ds(field * rows, rows), :] + numbers[pl.ds(field, 1), :] * outside)
    sums = (a[0] - a[4], a[1], a[2], a[3], a[6] + a[7], a[5] + a[8], a[9])
    for place in range(16):
        surface[pl.ds(place * rows, rows), :] = (
            sums[place] if place < len(sums) else jnp.zeros((rows, width), F32)
        )
    for tile in range(rows):
        products[pl.ds(tile * 16, 16), :] = remapped(
            surface[pl.ds(tile, 16, stride=rows), :], weights[tile]
        )
    count = PIECE_ROWS - 1
    sent = picked(
        routes[...][:, :rows],
        jnp.concatenate(
            [products[pl.ds(place, rows, stride=16), :] for place in range(count)], axis=1
        ),
    )
    for place in range(count):
        out[pl.ds(place, slots, stride=PIECE_ROWS), :] = sent[:, place * width : (place + 1) * width]
    out[pl.ds(count, slots, stride=PIECE_ROWS), :] = labels[...]


def flux_kernel(sizes, arrived, remap, routes, out, gather, sea_labels, fluxes, products):
    flux_count, rows, sections = sizes
    width = out.shape[1]
    slots = routes.shape[0]
    count = PIECE_ROWS - 1
    labels = arrived[pl.ds(count, slots, stride=PIECE_ROWS), :]
    upper = jnp.floor(labels * (1.0 / label_base(rows)))
    select = one_hot(labels - label_base(rows) * upper - 1.0)
    gather[...] = select
    sea_labels[...] = upper - 1.0
    values = jnp.concatenate(
        [arrived[pl.ds(place, slots, stride=PIECE_ROWS), :] for place in range(count)], axis=1
    )
    exchange = picked(jnp.transpose(select)[:rows, :], values)
    a04, a1, a2, a3, a67, a58, a9 = (
        exchange[:, place * width : (place + 1) * width] for place in range(count)
    )
    speed = jnp.sqrt(a2 * a2 + a3 * a3 + 0.5)
    fluxes[pl.ds(0, rows), :] = speed * a04 + a67
    fluxes[pl.ds(rows, rows), :] = speed * a1 + a58
    fluxes[pl.ds(2 * rows, rows), :] = speed * a2 * (1.0 + 0.2 * jnp.tanh(a9))
    fluxes[pl.ds(3 * rows, rows), :] = speed * a3
    for tile in range(rows):
        products[pl.ds(tile * flux_count, flux_count), :] = remapped(
            fluxes[pl.ds(tile, flux_count, stride=rows), :], both_halves(remap[tile])
        )
    sent = picked(
        routes[...][:, :rows],
        jnp.concatenate(
            [products[pl.ds(flux, rows, stride=flux_count), :] for flux in range(flux_count)],
            axis=1,
        ),
    )
    for flux in range(flux_count):
        for section in range(sections):
            out[pl.ds(section * slots * flux_count + flux, slots, stride=flux_count), :] = sent[
                :, flux * width : (flux + 1) * width
            ]


def sea_kernel(
    sizes, landed, base_tops, wet, own_labels, other_labels, section, tops, answers
):
    flux_count, sea_rows = sizes
    width = landed.shape[1]
    slots = own_labels.shape[0]
    mine = one_hot(own_labels[...])
    others = one_hot(other_labels[...])
    is_first = section[0:1, :] == 0.0
    select = jnp.concatenate(
        [jnp.where(is_first, mine, others), jnp.where(is_first, others, mine)], axis=0
    )
    values = jnp.concatenate(
        [landed[pl.ds(flux, 2 * slots, stride=flux_count), :] for flux in range(flux_count)], axis=1
    )
    forcing = picked(jnp.transpose(select)[:sea_rows, :], values)
    wet_cells = wet[...].astype(F32)
    for flux in range(flux_count):
        held = pl.ds(flux * sea_rows, sea_rows)
        tops[held, :] = base_tops[held, :] + wet_cells * (
            FORCING_SCALE[flux] * forcing[:, flux * width : (flux + 1) * width]
        )
    all_tops = jnp.concatenate(
        [tops[pl.ds(flux * sea_rows, sea_rows), :] for flux in range(flux_count)], axis=1
    )
    reply = picked(mine[:, :sea_rows], all_tops)
    for flux in range(flux_count):
        answers[pl.ds(flux, slots, stride=flux_count), :] = reply[
            :, flux * width : (flux + 1) * width
        ]


def tops_of_tiles(returned, routes, flux_count, scratch):
    slots, width = routes.shape
    rows = scratch.shape[0] // flux_count
    found = picked(
        jnp.transpose(routes[...])[:rows, :],
        jnp.concatenate(
            [returned[pl.ds(flux, slots, stride=flux_count), :] for flux in range(flux_count)],
            axis=1,
        ),
    )
    for flux in range(flux_count):
        scratch[pl.ds(flux, rows, stride=flux_count), :] = found[
            :, flux * width : (flux + 1) * width
        ]


def reply_kernel(flux_count, answered, remap, routes, gather, out, tops, on_exchange):
    slots, width = routes.shape
    rows = remap.shape[0]
    tops_of_tiles(answered, routes, flux_count, tops)
    for tile in range(rows):
        held = pl.ds(tile * flux_count, flux_count)
        on_exchange[held, :] = remapped(
            tops[held, :], both_halves(jnp.transpose(remap[tile]))
        )
    values = jnp.concatenate(
        [on_exchange[pl.ds(flux, rows, stride=flux_count), :] for flux in range(flux_count)], axis=1
    )
    replies = picked(gather[...][:, :rows], values)
    for flux in range(flux_count):
        out[pl.ds(flux, slots, stride=flux_count), :] = replies[
            :, flux * width : (flux + 1) * width
        ]


def surface_kernel(flux_count, returned, weights, routes, out, tops):
    rows = weights.shape[0]
    tops_of_tiles(returned, routes, flux_count, tops)
    for tile in range(rows):
        out[pl.ds(tile, flux_count, stride=rows), :] = remapped(
            tops[pl.ds(tile * flux_count, flux_count), :], weights[tile]
        )


VMEM = pl.BlockSpec(memory_space=pltpu.VMEM)
SMEM = pl.BlockSpec(memory_space=pltpu.SMEM)
ANY = pl.BlockSpec(memory_space=pl.ANY)


def array(*shape):
    return jax.ShapeDtypeStruct(shape, F32)


def call(kernel, name, outs, in_specs, scratch=(), after=(), limit=VMEM_LIMIT, work=1_000_000, **more):
    def body(*refs):
        kernel(*refs[: len(in_specs)], *refs[len(in_specs) + len(after) :])

    run = pl.pallas_call(
        body,
        name=name,
        out_shape=outs,
        in_specs=list(in_specs) + [ANY] * len(after),
        scratch_shapes=list(scratch),
        compiler_params=pltpu.CompilerParams(vmem_limit_bytes=limit),
        cost_estimate=pl.CostEstimate(flops=0, bytes_accessed=work, transcendentals=0),
        **more,
    )
    return lambda *arguments: run(*arguments, *after)


def gated(values, before):
    return lax.optimization_barrier((values, before))[0]


def on_device(
    atmos_state,
    atmos_diffusion,
    remap_atmos,
    exchange_owner,
    exchange_slot,
    remap_ocean,
    ocean_owner,
    ocean_slot,
    ocean_state,
    ocean_mixing,
    wet_mask,
):
    targets = lax.axis_size(SECTION)
    sections = lax.axis_size("comp")
    devices = targets * sections
    fields, levels, rows, width = atmos_state.shape
    sea_fields, sea_levels, sea_rows, _ = ocean_state.shape
    blocks = fields * levels
    sea_blocks = sea_fields * sea_levels
    at = Edges(fields, levels, rows, sea_blocks, sea_rows, width)
    slots = targets * CAPACITY
    ring = ("comp", "gx")

    index = jnp.stack([exchange_owner[:, 0], exchange_slot, ocean_owner[:, 0], ocean_slot])
    section = lax.axis_index("comp").astype(jnp.int32).reshape(1)
    state = atmos_state.reshape(blocks * rows, width)
    ocean = ocean_state.reshape(sea_blocks * sea_rows, width)

    state_copy = pltpu.VMEM((blocks * rows, width), F32)
    ocean_copy = pltpu.VMEM((sea_blocks * sea_rows, width), F32)
    ocean_flags = pltpu.SemaphoreType.DMA((sea_fields,))
    near_first, near_last, far_first, far_last, first_cols, last_cols = call(
        functools.partial(edges_kernel, at),
        "edges",
        (array(at.near_rows, width),) * 2
        + (array(at.far_rows, width),) * 2
        + (array(at.col_rows, width),) * 2,
        [ANY],
        [state_copy, pltpu.SemaphoreType.DMA((fields,))],
        limit=EDGES_LIMIT,
    )(state)
    near_first, near_last, first_cols, last_cols = call(
        functools.partial(sea_edges_kernel, at),
        "sea_edges",
        (array(at.near_rows, width),) * 2 + (array(at.col_rows, width),) * 2,
        [VMEM] * 6,
    )(ocean, wet_mask, near_first, near_last, first_cols, last_cols)
    north = shifted(near_last, ring, 1)
    south = shifted(near_first, ring, -1)
    west = shifted(last_cols, "gy", 1)
    east = shifted(first_cols, "gy", -1)

    def weights_of(remap, transposed, name, before):
        return call(
            functools.partial(weights_kernel, transposed),
            name,
            jax.ShapeDtypeStruct((rows, 2 * width, width), BF16),
            [VMEM],
        )(gated(remap, before))

    tile_slots, sea_slots, labels, here, numbers = call(
        routes_kernel,
        "routes",
        (array(slots, width),) * 3 + (array(8, width), array(-(-fields // 8) * 8, width)),
        [SMEM] * 3,
        [pltpu.SMEM((targets,), jnp.int32)] + [pltpu.VMEM((slots, width), F32)] * 2,
    )(gated(index, first_cols), section, atmos_diffusion)
    inner = call(
        functools.partial(inner_kernel, at),
        "inner",
        array(fields * rows, width),
        [ANY, VMEM],
        [pltpu.VMEM((fields, 2, rows, width), F32), pltpu.SemaphoreType.DMA],
    )(gated(atmos_state, first_cols), numbers)
    pieces = call(
        functools.partial(pieces_kernel, at),
        "pieces",
        array(slots * PIECE_ROWS, width),
        [VMEM] * 9,
        [pltpu.VMEM((16 * rows, width), F32)] * 2,
    )(
        inner,
        north,
        south,
        west,
        east,
        weights_of(remap_atmos, False, "piece_weights", first_cols),
        numbers,
        tile_slots,
        labels,
    )
    arrived = lax.all_to_all(
        pieces.reshape(targets, CAPACITY * PIECE_ROWS, width), SECTION, 0, 0, tiled=True
    )
    outgoing, gather, own_labels = call(
        functools.partial(flux_kernel, (sea_fields, rows, sections)),
        "fluxes",
        (
            array(sections * slots * sea_fields, width),
            array(slots, width),
            array(slots, width),
        ),
        [VMEM] * 3,
        [pltpu.VMEM((sea_fields * rows, width), F32)] * 2,
    )(arrived.reshape(slots * PIECE_ROWS, width), remap_ocean, sea_slots)
    landed = lax.all_to_all(
        outgoing.reshape(devices, CAPACITY * sea_fields, width), EVERY, 0, 0, tiled=True
    )
    other_labels = shifted(own_labels, "comp", 1)
    to_north, to_south = call(
        functools.partial(corners_kernel, at),
        "corners",
        (array(at.far_rows, width),) * 2,
        [VMEM] * 4,
        after=(outgoing,),
    )(far_first, far_last, west, east)
    far_north = shifted(to_south, ring, 1)
    far_south = shifted(to_north, ring, -1)

    sea_base, base_tops = call(
        functools.partial(ocean_kernel, at, sea_levels),
        "sea_base",
        (array(sea_blocks * sea_rows, width), array(sea_fields * sea_rows, width)),
        [ANY] + [VMEM] * 5 + [SMEM],
        [ocean_copy] * 2 + [pltpu.VMEM((width, width), F32)] * 2 + [ocean_flags] * 2,
        after=(outgoing,),
        limit=SEA_LIMIT,
        work=1_000_000_000,
        out_specs=(ANY, VMEM),
    )(ocean, wet_mask, north, south, west, east, ocean_mixing)

    tops, answers = call(
        functools.partial(sea_kernel, (sea_fields, sea_rows)),
        "sea_top",
        (array(sea_fields * sea_rows, width), array(slots * sea_fields, width)),
        [VMEM] * 6,
        after=(far_north, far_south),
    )(
        landed.reshape(devices * CAPACITY * sea_fields, width),
        base_tops,
        wet_mask,
        own_labels,
        other_labels,
        here,
    )
    answered = lax.all_to_all(
        answers.reshape(targets, CAPACITY * sea_fields, width), SECTION, 0, 0, tiled=True
    )
    replies = call(
        functools.partial(reply_kernel, sea_fields),
        "replies",
        array(slots * sea_fields, width),
        [VMEM] * 4,
        [pltpu.VMEM((sea_fields * rows, width), F32)] * 2,
    )(answered.reshape(slots * sea_fields, width), remap_ocean, sea_slots, gather)
    returned = lax.all_to_all(
        replies.reshape(targets, CAPACITY * sea_fields, width), SECTION, 0, 0, tiled=True
    )
    atmos_next, ocean_next = call(
        functools.partial(steps_kernel, at),
        "steps",
        (array(blocks * rows, width), array(sea_fields, sea_levels, sea_rows, width)),
        [ANY] + [VMEM] * 10 + [SMEM, ANY, ANY],
        [state_copy] * 3
        + (
            [pltpu.VMEM((at.ring_rows, width), F32)] * 2 + [pltpu.VMEM((rows, width), F32)] * 2
        )
        * 2
        + [pltpu.SemaphoreType.DMA((fields,))] * 2
        + [ocean_flags],
        after=(replies,),
        limit=STEPS_LIMIT,
        work=1_000_000_000,
        out_specs=(ANY, ANY),
        input_output_aliases={13: 1},
    )(
        state,
        north,
        south,
        west,
        east,
        far_north,
        far_south,
        near_first,
        near_last,
        first_cols,
        last_cols,
        atmos_diffusion,
        tops,
        sea_base.reshape(sea_fields, sea_levels, sea_rows, width),
    )
    ocean_surface = call(
        functools.partial(surface_kernel, sea_fields),
        "surface",
        array(sea_fields * rows, width),
        [VMEM] * 3,
        [pltpu.VMEM((sea_fields * rows, width), F32)],
    )(
        returned.reshape(slots * sea_fields, width),
        weights_of(remap_atmos, True, "surface_weights", replies),
        tile_slots,
    )
    return (
        atmos_next.reshape(atmos_state.shape),
        ocean_next,
        ocean_surface.reshape(sea_fields, rows, width),
    )


def solution(mesh):
    in_specs = (
        P(None, None, ("comp", "gx"), "gy"),
        P(),
        P(("comp", "gx", "gy"), None, None),
        P(("comp", "gx", "gy"), None),
        P(("comp", "gx", "gy")),
        P(("comp", "gx", "gy"), None, None),
        P(("comp", "gx", "gy"), None),
        P(("comp", "gx", "gy")),
        P(None, None, "gx", "gy"),
        P(),
        P("gx", "gy"),
    )
    out_specs = (
        P(None, None, ("comp", "gx"), "gy"),
        P(None, None, "gx", "gy"),
        P(None, ("comp", "gx"), "gy"),
    )
    return jax.shard_map(
        on_device, mesh=mesh, in_specs=in_specs, out_specs=out_specs, check_vma=False
    )
```

```python
import functools

import jax
import jax.numpy as jnp
from jax import lax
from jax.experimental import pallas as pl
from jax.experimental.pallas import tpu as pltpu
from jax.sharding import PartitionSpec as P

F32 = jnp.float32
BF16 = jnp.bfloat16
FORCING_SCALE = (0.1, -0.1, 0.1, 0.1)
SECTION = ("gx", "gy")
EVERY = ("comp", "gx", "gy")
CAPACITY = 2
PIECE_ROWS = 8
VMEM_LIMIT = 8 * 1024 * 1024
EDGES_LIMIT = 52 * 1024 * 1024
SEA_LIMIT = 53 * 1024 * 1024
STEPS_LIMIT = 53 * 1024 * 1024


def shifted(block, axis, distance):
    devices = range(lax.axis_size(axis))
    route = [((i - distance) % len(devices), i) for i in devices]
    return lax.ppermute(block, axis, route)


def dot(left, right, transposed=False):
    dims = (((1,), (1 if transposed else 0,)), ((), ()))
    return lax.dot_general(left, right, dims, preferred_element_type=F32)


def halves(values):
    high = values.astype(BF16)
    return high, (values - high.astype(F32)).astype(BF16)


def remapped(rows, weights):
    count, width = rows.shape
    high, low = halves(rows)
    if count < 16:
        filler = jnp.zeros((16 - count, width), F32)
        high, low = halves(jnp.concatenate([rows, filler], axis=0))
    left = jnp.concatenate(
        [
            jnp.concatenate([high, high], axis=1),
            jnp.concatenate([low, jnp.zeros(low.shape, BF16)], axis=1),
        ],
        axis=0,
    )
    product = dot(left, weights)
    return product[:count, :] + product[16 : 16 + count, :]


def both_halves(block):
    return jnp.concatenate(halves(block), axis=0)


def weights_kernel(transposed, remap, weights):
    for tile in range(remap.shape[0]):
        block = remap[tile]
        weights[tile] = both_halves(jnp.transpose(block) if transposed else block)


def picked(selection, values):
    chosen = selection.astype(BF16)
    high = values.astype(BF16)
    rest = values - high.astype(F32)
    middle = rest.astype(BF16)
    low = (rest - middle.astype(F32)).astype(BF16)
    return dot(chosen, high) + dot(chosen, middle) + dot(chosen, low)


def placed(values, selection):
    chosen = selection.astype(BF16)
    high = values.astype(BF16)
    rest = values - high.astype(F32)
    middle = rest.astype(BF16)
    low = (rest - middle.astype(F32)).astype(BF16)
    return dot(high, chosen) + dot(middle, chosen) + dot(low, chosen)


def one_hot(labels):
    lanes = lax.broadcasted_iota(jnp.int32, labels.shape, 1).astype(F32)
    return (labels == lanes).astype(F32)


def grid_index(shape):
    return lax.broadcasted_iota(jnp.int32, shape, 0), lax.broadcasted_iota(jnp.int32, shape, 1)


def around(cells, north, south, west, east):
    rows, lanes = grid_index(cells.shape)
    row_count, width = cells.shape
    return (
        jnp.where(rows == 0, north, pltpu.roll(cells, 1, 0)),
        jnp.where(rows == row_count - 1, south, pltpu.roll(cells, row_count - 1, 0)),
        jnp.where(lanes == 0, west, pltpu.roll(cells, 1, 1)),
        jnp.where(lanes == width - 1, east, pltpu.roll(cells, width - 1, 1)),
    )


def diffused(cells, upper, lower, sides, diffusion):
    beside = sides[0] + sides[1] + sides[2] + sides[3] - 4.0 * cells
    return cells + diffusion * beside + 0.1 * (upper + lower - 2.0 * cells)


class Edges:
    def __init__(self, fields, levels, rows, sea_blocks, sea_rows, width):
        self.fields, self.levels, self.rows, self.width = fields, levels, rows, width
        self.sea_blocks, self.sea_rows = sea_blocks, sea_rows
        self.half = fields // 2
        self.part = self.half * levels
        self.ring_rows = -(-self.part // 8) * 8
        self.atmos_rows = 2 * self.part
        self.wet_row = self.atmos_rows + sea_blocks
        self.near_rows = -(-(self.wet_row + 1) // 8) * 8
        self.corner_row = self.atmos_rows
        self.far_rows = -(-(self.atmos_rows + 4) // 8) * 8
        self.sea_tiles = sea_blocks * sea_rows // width
        self.sea_cols = 4 * rows
        self.sea_col_rows = -(-(self.sea_tiles + 1) // 8) * 8
        self.col_rows = self.sea_cols + self.sea_col_rows


def squared(values):
    rows, width = values.shape
    if rows == width:
        return values
    return jnp.concatenate([values, jnp.zeros((width - rows, width), F32)], axis=0)


def chunk(source, target, at, rows, arrival):
    part = pl.ds(pl.multiple_of(at * rows, 8), rows)
    return pltpu.make_async_copy(source.at[part], target.at[part], arrival)


def edges_kernel(
    at, state_far, near_first, near_last, far_first, far_last, first, last, state, arrivals
):
    rows, part, width = at.rows, at.part, at.width
    field_rows = at.levels * rows
    copies = [
        chunk(state_far, state, field, field_rows, arrivals.at[field])
        for field in range(at.fields)
    ]
    for copy in copies:
        copy.start()
    for out in (near_first, near_last, far_first, far_last):
        out[...] = jnp.zeros(out.shape, F32)
    for cols in (first, last):
        cols[pl.ds(at.sea_cols, at.sea_col_rows), :] = jnp.zeros((at.sea_col_rows, width), F32)
    for half in range(2):
        for field in range(half * at.half, (half + 1) * at.half):
            copies[field].wait()
        for row in range(rows):
            lines = state[pl.ds(half * part * rows + row, part, stride=rows), :]
            held = pl.ds(half * at.part, part)
            if row < 2:
                (near_first, far_first)[row][held, :] = lines
            if row >= rows - 2:
                (near_last, far_last)[rows - 1 - row][held, :] = lines
            turned = jnp.transpose(squared(lines))
            near, far = half * rows + row, (2 + half) * rows + row
            first[pl.ds(near, 1), :] = turned[0:1, :]
            first[pl.ds(far, 1), :] = turned[1:2, :]
            last[pl.ds(near, 1), :] = turned[width - 1 : width, :]
            last[pl.ds(far, 1), :] = turned[width - 2 : width - 1, :]


def sea_edges_kernel(at, ocean, wet, near_first, near_last, first, last, *outs):
    width = at.width
    for out, rows in zip(outs, (near_first, near_last, first, last)):
        out[...] = rows[...]
    for out, sea_row in ((outs[0], 0), (outs[1], at.sea_rows - 1)):
        out[pl.ds(at.atmos_rows, at.sea_blocks), :] = ocean[
            pl.ds(sea_row, at.sea_blocks, stride=at.sea_rows), :
        ]
        out[pl.ds(at.wet_row, 1), :] = wet[pl.ds(sea_row, 1), :].astype(F32)
    for tile in range(at.sea_tiles + 1):
        if tile < at.sea_tiles:
            lines = ocean[pl.ds(tile * width, width), :]
        else:
            lines = squared(wet[...].astype(F32))
        turned = jnp.transpose(lines)
        outs[2][pl.ds(at.sea_cols + tile, 1), :] = turned[0:1, :]
        outs[3][pl.ds(at.sea_cols + tile, 1), :] = turned[width - 1 : width, :]


def corners_kernel(at, far_first, far_last, west, east, to_north, to_south):
    for out, lines, row in ((to_north, far_first, 0), (to_south, far_last, at.rows - 1)):
        out[...] = lines[...]
        for place, (cols, half) in enumerate(((west, 0), (west, 1), (east, 0), (east, 1))):
            out[pl.ds(at.corner_row + place, 1), :] = cols[pl.ds(half * at.rows + row, 1), :]


def spread(at, diffusion, part, places):
    numbers = jnp.zeros(places.shape, F32)
    is_first = places < 0
    is_last = places < 0
    for field in range(at.half):
        start = field * at.levels
        numbers = jnp.where(places >= start, diffusion[part * at.half + field], numbers)
        is_first = is_first | (places == start)
        is_last = is_last | (places == start + at.levels - 1)
    return numbers, is_first, is_last


def ring_step(at, part, halos, edges, diffusion, outs):
    north, south, west, east, far_north, far_south = halos
    near_first, near_last, first, last = edges
    rows, width = at.rows, at.width
    shape = (at.ring_rows, width)
    held = pl.ds(part * at.part, shape[0])
    lines, lanes = grid_index(shape)
    numbers, is_first, is_last = spread(at, diffusion, part, lines)
    for out, outside, further, own, is_north in (
        (outs[0], north, far_north, near_first, True),
        (outs[1], south, far_south, near_last, False),
    ):
        turned = jnp.transpose(squared(further[pl.ds(at.corner_row, 8), :]))[: shape[0], :]
        cells, beyond, inside = outside[held, :], further[held, :], own[held, :]
        west_col = jnp.where(lanes == 0, turned[:, part : part + 1], pltpu.roll(cells, 1, 1))
        east_col = jnp.where(
            lanes == width - 1, turned[:, 2 + part : 3 + part], pltpu.roll(cells, width - 1, 1)
        )
        sides = (
            beyond if is_north else inside,
            inside if is_north else beyond,
            west_col,
            east_col,
        )
        upper = jnp.where(is_first, cells, pltpu.roll(cells, 1, 0))
        lower = jnp.where(is_last, cells, pltpu.roll(cells, shape[0] - 1, 0))
        out[...] = diffused(cells, upper, lower, sides, numbers)

    shape = (rows, width)
    near, far = pl.ds(part * rows, rows), pl.ds((2 + part) * rows, rows)
    lines, lanes = grid_index(shape)
    numbers, is_first, is_last = spread(at, diffusion, part, lanes)
    for out, outside, own, corner, is_west in (
        (outs[2], west, first, 0, True),
        (outs[3], east, last, 2, False),
    ):
        cells, beyond, inside = outside[near, :], outside[far, :], own[near, :]
        place = pl.ds(at.corner_row + corner + part, 1)
        sides = (
            jnp.where(lines == 0, far_north[place, :], pltpu.roll(cells, 1, 0)),
            jnp.where(lines == rows - 1, far_south[place, :], pltpu.roll(cells, rows - 1, 0)),
            beyond if is_west else inside,
            inside if is_west else beyond,
        )
        upper = jnp.where(is_first, cells, pltpu.roll(cells, 1, 1))
        lower = jnp.where(is_last, cells, pltpu.roll(cells, width - 1, 1))
        out[...] = diffused(cells, upper, lower, sides, numbers)


def interleaved(at, west, east):
    width = at.width
    fields_each = width // 2 // at.levels
    columns = jnp.concatenate([east, west], axis=1)
    source, target = grid_index((2 * width, width))
    out = []
    for first in range(0, at.half, fields_each):
        block = jnp.where(source < width, source, source - width) - first * at.levels
        lane = 2 * block + jnp.where(source < width, 0, 1)
        out.append(placed(columns, (lane == target).astype(F32)))
    return out


def field_step(at, field, state, out, north, south, first_line, beside, number):
    levels, rows, width = at.levels, at.rows, at.width
    fields_each = width // 2 // levels
    lines, lanes = grid_index((rows, width))
    for level in range(levels):
        line = first_line + field * levels + level
        start = (field * levels + level) * rows
        cells = state[pl.ds(start, rows), :]
        first_level, last_level = level == 0, level == levels - 1
        upper = cells if first_level else state[pl.ds(start - rows, rows), :]
        lower = cells if last_level else state[pl.ds(start + rows, rows), :]
        lane = 2 * ((field % fields_each) * levels + level) + 1
        edge = pltpu.roll(beside[field // fields_each], width - lane, 1)
        sides = (
            jnp.where(lines == 0, north[pl.ds(line, 1), :], pltpu.roll(cells, 1, 0)),
            jnp.where(
                lines == rows - 1, south[pl.ds(line, 1), :], pltpu.roll(cells, rows - 1, 0)
            ),
            jnp.where(lanes == 0, edge, pltpu.roll(cells, 1, 1)),
            jnp.where(lanes == width - 1, edge, pltpu.roll(cells, width - 1, 1)),
        )
        out[pl.ds(start, rows), :] = diffused(cells, upper, lower, sides, number)


def steps_kernel(
    at,
    state_far,
    north,
    south,
    west,
    east,
    far_north,
    far_south,
    near_first,
    near_last,
    first,
    last,
    diffusion,
    tops,
    sea_before,
    out_far,
    sea_out,
    state,
    middle,
    out,
    *rest,
):
    *rings, arrivals, departures, sea_departures = rest
    rows, levels = at.rows, at.levels
    field_rows = levels * rows

    def coming(field):
        return chunk(state_far, state, field, field_rows, arrivals.at[field])

    def going(field):
        return chunk(out, out_far, field, field_rows, departures.at[field])

    for field in range(at.fields):
        coming(field).start()
    stored = [
        pltpu.make_async_copy(
            tops.at[pl.ds(flux * at.sea_rows, at.sea_rows)],
            sea_out.at[flux, 0],
            sea_departures.at[flux],
        )
        for flux in range(sea_out.shape[0])
    ]
    for copy in stored:
        copy.start()
    halos = (north, south, west, east, far_north, far_south)
    for part in range(2):
        ring = rings[4 * part : 4 * part + 4]
        ring_step(at, part, halos, (near_first, near_last, first, last), diffusion, ring)
    for part in range(2):
        ring = rings[4 * part : 4 * part + 4]
        held = pl.ds(part * rows, rows)
        outer = interleaved(at, west[held, :], east[held, :])
        inner = interleaved(at, ring[2][...], ring[3][...])
        cells = pl.ds(part * at.part * rows, at.part * rows)
        parts = [array.at[cells] for array in (state, middle, out)]
        for field in range(at.half):
            whole = part * at.half + field
            number = diffusion[whole]
            coming(whole).wait()
            field_step(
                at, field, parts[0], parts[1], north, south, part * at.part, outer, number
            )
            field_step(at, field, parts[1], parts[2], ring[0], ring[1], 0, inner, number)
            going(whole).start()
    for copy in stored:
        copy.wait()
    for field in range(at.fields):
        going(field).wait()


def ocean_kernel(
    at,
    levels,
    ocean_far,
    wet,
    north,
    south,
    west,
    east,
    mixing,
    out_far,
    tops,
    ocean,
    out,
    wests,
    easts,
    arrivals,
    departures,
):
    fields, field_rows = at.sea_blocks // levels, levels * at.sea_rows
    for field in range(fields):
        chunk(ocean_far, ocean, field, field_rows, arrivals.at[field]).start()
    rows, width = at.sea_rows, at.width
    lines, lanes = grid_index((rows, width))
    per_tile = width // rows
    held = pl.ds(at.sea_cols, at.sea_col_rows)
    wests[...] = jnp.transpose(squared(west[held, :]))
    easts[...] = jnp.transpose(squared(east[held, :]))
    wet_cells = wet[...].astype(F32)
    wet_lane = at.sea_tiles
    wet_sides = around(
        wet_cells,
        north[pl.ds(at.wet_row, 1), :],
        south[pl.ds(at.wet_row, 1), :],
        wests[pl.ds(0, rows), :][:, wet_lane : wet_lane + 1],
        easts[pl.ds(0, rows), :][:, wet_lane : wet_lane + 1],
    )

    def field_step(field, carry):
        chunk(ocean_far, ocean, field, field_rows, arrivals.at[field]).wait()
        back = lax.rem(width - field * (levels // per_tile), width)
        west_cols = pltpu.roll(wests[...], back, 1)
        east_cols = pltpu.roll(easts[...], back, 1)
        number = mixing[field] * wet_cells
        for level in range(levels):
            block = field * levels + level
            start = pl.multiple_of(block * rows, rows)
            first_level, last_level = level == 0, level == levels - 1
            cells = ocean[pl.ds(start, rows), :]
            upper = cells if first_level else ocean[pl.ds(start - rows, rows), :]
            lower = cells if last_level else ocean[pl.ds(start + rows, rows), :]
            above = pltpu.roll(cells, 1, 0)
            below = pltpu.roll(cells, rows - 1, 0)
            line = at.atmos_rows + block
            tile, within = level // per_tile, (level % per_tile) * rows
            west_col = pltpu.roll(west_cols[within : within + rows, :], (width - tile) % width, 1)
            east_col = pltpu.roll(east_cols[within : within + rows, :], width - 1 - tile, 1)
            sides = (
                jnp.where(lines == 0, north[pl.ds(line, 1), :], above),
                jnp.where(lines == rows - 1, south[pl.ds(line, 1), :], below),
                jnp.where(lanes == 0, west_col, pltpu.roll(cells, 1, 1)),
                jnp.where(lanes == width - 1, east_col, pltpu.roll(cells, width - 1, 1)),
            )
            total = wet_sides[0] * (sides[0] - cells)
            for side in range(1, 4):
                total = total + wet_sides[side] * (sides[side] - cells)
            tendency = number * total + 0.1 * (upper + lower - 2.0 * cells)
            after = cells + wet_cells * tendency
            out[pl.ds(start, rows), :] = after
            if first_level:
                tops[pl.ds(pl.multiple_of(field * rows, rows), rows), :] = after
        chunk(out, out_far, field, field_rows, departures.at[field]).start()
        return carry

    lax.fori_loop(0, fields, field_step, 0)
    for field in range(fields):
        chunk(out, out_far, field, field_rows, departures.at[field]).wait()


def label_base(rows):
    return 2.0 * rows


def routes_kernel(index, own, diffusion, *rest):
    *outs, labels_out, section, numbers, tally, piece_labels, sea_labels = rest
    lanes = lax.broadcasted_iota(jnp.int32, (1, section.shape[1]), 1)
    section[...] = jnp.full(section.shape, own[0].astype(F32))
    for field in range(diffusion.shape[0]):
        numbers[pl.ds(field, 1), :] = jnp.full(lanes.shape, diffusion[field])

    def clear(at, carry):
        tally[at] = 0
        return carry

    for row, slots, labels in ((0, outs[0], piece_labels), (2, outs[1], sea_labels)):
        slots[...] = jnp.zeros(slots.shape, F32)
        labels[...] = jnp.full(labels.shape, -1.0, F32)
        lax.fori_loop(0, tally.shape[0], clear, 0)
        for tile in range(index.shape[1]):
            owner = index[row, tile]
            rank = tally[owner]
            tally[owner] = rank + 1
            slot = pl.ds(owner * CAPACITY + rank, 1)
            slots[slot, :] = (lanes == tile).astype(F32)
            labels[slot, :] = jnp.full(lanes.shape, index[row + 1, tile].astype(F32))
    base = label_base(index.shape[1])
    labels_out[...] = (piece_labels[...] + 1.0) + base * (sea_labels[...] + 1.0)


def inner_kernel(at, state_far, numbers, out, top, arrival):
    fields, rows, width = at.fields, at.rows, at.width
    copy = pltpu.make_async_copy(state_far.at[:, pl.ds(at.levels - 2, 2)], top, arrival)
    copy.start()
    lines, lanes = grid_index((rows, width))
    copy.wait()
    for field in range(fields):
        cells = top[field, 1]
        sides = (
            jnp.where(lines == 0, 0.0, pltpu.roll(cells, 1, 0)),
            jnp.where(lines == rows - 1, 0.0, pltpu.roll(cells, rows - 1, 0)),
            jnp.where(lanes == 0, 0.0, pltpu.roll(cells, 1, 1)),
            jnp.where(lanes == width - 1, 0.0, pltpu.roll(cells, width - 1, 1)),
        )
        out[pl.ds(field * rows, rows), :] = diffused(
            cells, top[field, 0], cells, sides, numbers[pl.ds(field, 1), :]
        )


def pieces_kernel(
    at, inner, north, south, west, east, weights, numbers, routes, labels, out, surface, products
):
    fields, levels, rows, width = at.fields, at.levels, at.rows, at.width
    slots = routes.shape[0]
    lines, lanes = grid_index((rows, width))
    a = []
    for field in range(fields):
        part = field // at.half
        held = pl.ds(part * rows, rows)
        lane = (field % at.half) * levels + levels - 1
        line = pl.ds(part * at.part + lane, 1)
        outside = (
            jnp.where(lines == 0, north[line, :], 0.0)
            + jnp.where(lines == rows - 1, south[line, :], 0.0)
            + jnp.where(lanes == 0, pltpu.roll(west[held, :], (width - lane) % width, 1), 0.0)
            + jnp.where(lanes == width - 1, pltpu.roll(east[held, :], width - 1 - lane, 1), 0.0)
        )
        a.append(inner[pl.ds(field * rows, rows), :] + numbers[pl.ds(field, 1), :] * outside)
    sums = (a[0] - a[4], a[1], a[2], a[3], a[6] + a[7], a[5] + a[8], a[9])
    for place in range(16):
        surface[pl.ds(place * rows, rows), :] = (
            sums[place] if place < len(sums) else jnp.zeros((rows, width), F32)
        )
    for tile in range(rows):
        products[pl.ds(tile * 16, 16), :] = remapped(
            surface[pl.ds(tile, 16, stride=rows), :], weights[tile]
        )
    count = PIECE_ROWS - 1
    sent = picked(
        routes[...][:, :rows],
        jnp.concatenate(
            [products[pl.ds(place, rows, stride=16), :] for place in range(count)], axis=1
        ),
    )
    for place in range(count):
        out[pl.ds(place, slots, stride=PIECE_ROWS), :] = sent[:, place * width : (place + 1) * width]
    out[pl.ds(count, slots, stride=PIECE_ROWS), :] = labels[...]


def sea_labels_kernel(rows, arrived, sea_labels):
    labels = arrived[pl.ds(PIECE_ROWS - 1, sea_labels.shape[0], stride=PIECE_ROWS), :]
    sea_labels[...] = jnp.floor(labels * (1.0 / label_base(rows))) - 1.0


def flux_kernel(sizes, arrived, remap, routes, out, gather, fluxes, products):
    flux_count, rows, sections = sizes
    width = out.shape[1]
    slots = routes.shape[0]
    count = PIECE_ROWS - 1
    labels = arrived[pl.ds(count, slots, stride=PIECE_ROWS), :]
    upper = jnp.floor(labels * (1.0 / label_base(rows)))
    select = one_hot(labels - label_base(rows) * upper - 1.0)
    gather[...] = select
    values = jnp.concatenate(
        [arrived[pl.ds(place, slots, stride=PIECE_ROWS), :] for place in range(count)], axis=1
    )
    exchange = picked(jnp.transpose(select)[:rows, :], values)
    a04, a1, a2, a3, a67, a58, a9 = (
        exchange[:, place * width : (place + 1) * width] for place in range(count)
    )
    speed = jnp.sqrt(a2 * a2 + a3 * a3 + 0.5)
    fluxes[pl.ds(0, rows), :] = speed * a04 + a67
    fluxes[pl.ds(rows, rows), :] = speed * a1 + a58
    fluxes[pl.ds(2 * rows, rows), :] = speed * a2 * (1.0 + 0.2 * jnp.tanh(a9))
    fluxes[pl.ds(3 * rows, rows), :] = speed * a3
    for tile in range(rows):
        products[pl.ds(tile * flux_count, flux_count), :] = remapped(
            fluxes[pl.ds(tile, flux_count, stride=rows), :], both_halves(remap[tile])
        )
    sent = picked(
        routes[...][:, :rows],
        jnp.concatenate(
            [products[pl.ds(flux, rows, stride=flux_count), :] for flux in range(flux_count)],
            axis=1,
        ),
    )
    for flux in range(flux_count):
        for section in range(sections):
            out[pl.ds(section * slots * flux_count + flux, slots, stride=flux_count), :] = sent[
                :, flux * width : (flux + 1) * width
            ]


def sea_kernel(
    sizes, landed, base_tops, wet, own_labels, other_labels, section, tops, answers
):
    flux_count, sea_rows = sizes
    width = landed.shape[1]
    slots = own_labels.shape[0]
    mine = one_hot(own_labels[...])
    others = one_hot(other_labels[...])
    is_first = section[0:1, :] == 0.0
    select = jnp.concatenate(
        [jnp.where(is_first, mine, others), jnp.where(is_first, others, mine)], axis=0
    )
    values = jnp.concatenate(
        [landed[pl.ds(flux, 2 * slots, stride=flux_count), :] for flux in range(flux_count)], axis=1
    )
    forcing = picked(jnp.transpose(select)[:sea_rows, :], values)
    wet_cells = wet[...].astype(F32)
    for flux in range(flux_count):
        held = pl.ds(flux * sea_rows, sea_rows)
        tops[held, :] = base_tops[held, :] + wet_cells * (
            FORCING_SCALE[flux] * forcing[:, flux * width : (flux + 1) * width]
        )
    all_tops = jnp.concatenate(
        [tops[pl.ds(flux * sea_rows, sea_rows), :] for flux in range(flux_count)], axis=1
    )
    reply = picked(mine[:, :sea_rows], all_tops)
    for flux in range(flux_count):
        answers[pl.ds(flux, slots, stride=flux_count), :] = reply[
            :, flux * width : (flux + 1) * width
        ]


def tops_of_tiles(returned, routes, flux_count, scratch):
    slots, width = routes.shape
    rows = scratch.shape[0] // flux_count
    found = picked(
        jnp.transpose(routes[...])[:rows, :],
        jnp.concatenate(
            [returned[pl.ds(flux, slots, stride=flux_count), :] for flux in range(flux_count)],
            axis=1,
        ),
    )
    for flux in range(flux_count):
        scratch[pl.ds(flux, rows, stride=flux_count), :] = found[
            :, flux * width : (flux + 1) * width
        ]


def reply_kernel(flux_count, answered, remap, routes, gather, out, tops, on_exchange):
    slots, width = routes.shape
    rows = remap.shape[0]
    tops_of_tiles(answered, routes, flux_count, tops)
    for tile in range(rows):
        held = pl.ds(tile * flux_count, flux_count)
        on_exchange[held, :] = remapped(
            tops[held, :], both_halves(jnp.transpose(remap[tile]))
        )
    values = jnp.concatenate(
        [on_exchange[pl.ds(flux, rows, stride=flux_count), :] for flux in range(flux_count)], axis=1
    )
    replies = picked(gather[...][:, :rows], values)
    for flux in range(flux_count):
        out[pl.ds(flux, slots, stride=flux_count), :] = replies[
            :, flux * width : (flux + 1) * width
        ]


def surface_kernel(flux_count, returned, remap, routes, out, tops):
    rows = remap.shape[0]
    tops_of_tiles(returned, routes, flux_count, tops)
    for tile in range(rows):
        out[pl.ds(tile, flux_count, stride=rows), :] = remapped(
            tops[pl.ds(tile * flux_count, flux_count), :], both_halves(jnp.transpose(remap[tile]))
        )


VMEM = pl.BlockSpec(memory_space=pltpu.VMEM)
SMEM = pl.BlockSpec(memory_space=pltpu.SMEM)
ANY = pl.BlockSpec(memory_space=pl.ANY)


def array(*shape):
    return jax.ShapeDtypeStruct(shape, F32)


def call(kernel, name, outs, in_specs, scratch=(), after=(), limit=VMEM_LIMIT, work=1_000_000, **more):
    def body(*refs):
        kernel(*refs[: len(in_specs)], *refs[len(in_specs) + len(after) :])

    run = pl.pallas_call(
        body,
        name=name,
        out_shape=outs,
        in_specs=list(in_specs) + [ANY] * len(after),
        scratch_shapes=list(scratch),
        compiler_params=pltpu.CompilerParams(vmem_limit_bytes=limit),
        cost_estimate=pl.CostEstimate(flops=0, bytes_accessed=work, transcendentals=0),
        **more,
    )
    return lambda *arguments: run(*arguments, *after)


def gated(values, before):
    return lax.optimization_barrier((values, before))[0]


def on_device(
    atmos_state,
    atmos_diffusion,
    remap_atmos,
    exchange_owner,
    exchange_slot,
    remap_ocean,
    ocean_owner,
    ocean_slot,
    ocean_state,
    ocean_mixing,
    wet_mask,
):
    targets = lax.axis_size(SECTION)
    sections = lax.axis_size("comp")
    devices = targets * sections
    fields, levels, rows, width = atmos_state.shape
    sea_fields, sea_levels, sea_rows, _ = ocean_state.shape
    blocks = fields * levels
    sea_blocks = sea_fields * sea_levels
    at = Edges(fields, levels, rows, sea_blocks, sea_rows, width)
    slots = targets * CAPACITY
    ring = ("comp", "gx")

    index = jnp.stack([exchange_owner[:, 0], exchange_slot, ocean_owner[:, 0], ocean_slot])
    section = lax.axis_index("comp").astype(jnp.int32).reshape(1)
    state = atmos_state.reshape(blocks * rows, width)
    ocean = ocean_state.reshape(sea_blocks * sea_rows, width)

    state_copy = pltpu.VMEM((blocks * rows, width), F32)
    ocean_copy = pltpu.VMEM((sea_blocks * sea_rows, width), F32)
    ocean_flags = pltpu.SemaphoreType.DMA((sea_fields,))
    near_first, near_last, far_first, far_last, first_cols, last_cols = call(
        functools.partial(edges_kernel, at),
        "edges",
        (array(at.near_rows, width),) * 2
        + (array(at.far_rows, width),) * 2
        + (array(at.col_rows, width),) * 2,
        [ANY],
        [state_copy, pltpu.SemaphoreType.DMA((fields,))],
        limit=EDGES_LIMIT,
    )(state)
    near_first, near_last, first_cols, last_cols = call(
        functools.partial(sea_edges_kernel, at),
        "sea_edges",
        (array(at.near_rows, width),) * 2 + (array(at.col_rows, width),) * 2,
        [VMEM] * 6,
    )(ocean, wet_mask, near_first, near_last, first_cols, last_cols)
    north = shifted(near_last, ring, 1)
    south = shifted(near_first, ring, -1)
    west = shifted(last_cols, "gy", 1)
    east = shifted(first_cols, "gy", -1)

    def weights_of(remap, transposed, name, before):
        return call(
            functools.partial(weights_kernel, transposed),
            name,
            jax.ShapeDtypeStruct((rows, 2 * width, width), BF16),
            [VMEM],
        )(gated(remap, before))

    tile_slots, sea_slots, labels, here, numbers = call(
        routes_kernel,
        "routes",
        (array(slots, width),) * 3 + (array(8, width), array(-(-fields // 8) * 8, width)),
        [SMEM] * 3,
        [pltpu.SMEM((targets,), jnp.int32)] + [pltpu.VMEM((slots, width), F32)] * 2,
    )(gated(index, first_cols), section, atmos_diffusion)
    inner = call(
        functools.partial(inner_kernel, at),
        "inner",
        array(fields * rows, width),
        [ANY, VMEM],
        [pltpu.VMEM((fields, 2, rows, width), F32), pltpu.SemaphoreType.DMA],
    )(gated(atmos_state, first_cols), numbers)
    pieces = call(
        functools.partial(pieces_kernel, at),
        "pieces",
        array(slots * PIECE_ROWS, width),
        [VMEM] * 9,
        [pltpu.VMEM((16 * rows, width), F32)] * 2,
    )(
        inner,
        north,
        south,
        west,
        east,
        weights_of(remap_atmos, False, "piece_weights", first_cols),
        numbers,
        tile_slots,
        labels,
    )
    arrived = lax.all_to_all(
        pieces.reshape(targets, CAPACITY * PIECE_ROWS, width), SECTION, 0, 0, tiled=True
    )
    to_north, to_south = call(
        functools.partial(corners_kernel, at),
        "corners",
        (array(at.far_rows, width),) * 2,
        [VMEM] * 4,
        after=(pieces,),
    )(far_first, far_last, west, east)
    far_north = shifted(to_south, ring, 1)
    far_south = shifted(to_north, ring, -1)

    sea_base, base_tops = call(
        functools.partial(ocean_kernel, at, sea_levels),
        "sea_base",
        (array(sea_blocks * sea_rows, width), array(sea_fields * sea_rows, width)),
        [ANY] + [VMEM] * 5 + [SMEM],
        [ocean_copy] * 2 + [pltpu.VMEM((width, width), F32)] * 2 + [ocean_flags] * 2,
        after=(pieces,),
        limit=SEA_LIMIT,
        work=1_000_000_000,
        out_specs=(ANY, VMEM),
    )(ocean, wet_mask, north, south, west, east, ocean_mixing)

    arrived, sea_base, far_north, far_south = lax.optimization_barrier(
        (arrived, sea_base, far_north, far_south)
    )
    arrived = arrived.reshape(slots * PIECE_ROWS, width)
    own_labels = call(
        functools.partial(sea_labels_kernel, rows), "sea_labels", array(slots, width), [VMEM]
    )(arrived)
    other_labels = shifted(own_labels, "comp", 1)
    outgoing, gather = call(
        functools.partial(flux_kernel, (sea_fields, rows, sections)),
        "fluxes",
        (array(sections * slots * sea_fields, width), array(slots, width)),
        [VMEM] * 3,
        [pltpu.VMEM((sea_fields * rows, width), F32)] * 2,
    )(arrived, remap_ocean, sea_slots)
    outgoing, other_labels = lax.optimization_barrier((outgoing, other_labels))
    landed = lax.all_to_all(
        outgoing.reshape(devices, CAPACITY * sea_fields, width), EVERY, 0, 0, tiled=True
    )
    tops, answers = call(
        functools.partial(sea_kernel, (sea_fields, sea_rows)),
        "sea_top",
        (array(sea_fields * sea_rows, width), array(slots * sea_fields, width)),
        [VMEM] * 6,
    )(
        landed.reshape(devices * CAPACITY * sea_fields, width),
        base_tops,
        wet_mask,
        own_labels,
        other_labels,
        here,
    )
    answered = lax.all_to_all(
        answers.reshape(targets, CAPACITY * sea_fields, width), SECTION, 0, 0, tiled=True
    )
    replies = call(
        functools.partial(reply_kernel, sea_fields),
        "replies",
        array(slots * sea_fields, width),
        [VMEM] * 4,
        [pltpu.VMEM((sea_fields * rows, width), F32)] * 2,
    )(answered.reshape(slots * sea_fields, width), remap_ocean, sea_slots, gather)
    returned = lax.all_to_all(
        replies.reshape(targets, CAPACITY * sea_fields, width), SECTION, 0, 0, tiled=True
    )
    atmos_next, ocean_next = call(
        functools.partial(steps_kernel, at),
        "steps",
        (array(blocks * rows, width), array(sea_fields, sea_levels, sea_rows, width)),
        [ANY] + [VMEM] * 10 + [SMEM, ANY, ANY],
        [state_copy] * 3
        + (
            [pltpu.VMEM((at.ring_rows, width), F32)] * 2 + [pltpu.VMEM((rows, width), F32)] * 2
        )
        * 2
        + [pltpu.SemaphoreType.DMA((fields,))] * 2
        + [ocean_flags],
        after=(replies,),
        limit=STEPS_LIMIT,
        work=1_000_000_000,
        out_specs=(ANY, ANY),
        input_output_aliases={13: 1},
    )(
        state,
        north,
        south,
        west,
        east,
        far_north,
        far_south,
        near_first,
        near_last,
        first_cols,
        last_cols,
        atmos_diffusion,
        tops,
        sea_base.reshape(sea_fields, sea_levels, sea_rows, width),
    )
    ocean_surface = call(
        functools.partial(surface_kernel, sea_fields),
        "surface",
        array(sea_fields * rows, width),
        [VMEM] * 3,
        [pltpu.VMEM((sea_fields * rows, width), F32)],
    )(
        returned.reshape(slots * sea_fields, width),
        remap_atmos,
        tile_slots,
    )
    return (
        atmos_next.reshape(atmos_state.shape),
        ocean_next,
        ocean_surface.reshape(sea_fields, rows, width),
    )


def solution(mesh):
    in_specs = (
        P(None, None, ("comp", "gx"), "gy"),
        P(),
        P(("comp", "gx", "gy"), None, None),
        P(("comp", "gx", "gy"), None),
        P(("comp", "gx", "gy")),
        P(("comp", "gx", "gy"), None, None),
        P(("comp", "gx", "gy"), None),
        P(("comp", "gx", "gy")),
        P(None, None, "gx", "gy"),
        P(),
        P("gx", "gy"),
    )
    out_specs = (
        P(None, None, ("comp", "gx"), "gy"),
        P(None, None, "gx", "gy"),
        P(None, ("comp", "gx"), "gy"),
    )
    return jax.shard_map(
        on_device, mesh=mesh, in_specs=in_specs, out_specs=out_specs, check_vma=False
    )
```

```python
import functools

import jax
import jax.numpy as jnp
from jax import lax
from jax.experimental import pallas as pl
from jax.experimental.pallas import tpu as pltpu
from jax.sharding import PartitionSpec as P

F32 = jnp.float32
BF16 = jnp.bfloat16
FORCING_SCALE = (0.1, -0.1, 0.1, 0.1)
SECTION = ("gx", "gy")
EVERY = ("comp", "gx", "gy")
CAPACITY = 2
PIECE_ROWS = 8
VMEM_LIMIT = 8 * 1024 * 1024
EDGES_LIMIT = 52 * 1024 * 1024
SEA_LIMIT = 53 * 1024 * 1024
STEPS_LIMIT = 53 * 1024 * 1024


def shifted(block, axis, distance):
    devices = range(lax.axis_size(axis))
    route = [((i - distance) % len(devices), i) for i in devices]
    return lax.ppermute(block, axis, route)


def dot(left, right, transposed=False):
    dims = (((1,), (1 if transposed else 0,)), ((), ()))
    return lax.dot_general(left, right, dims, preferred_element_type=F32)


def halves(values):
    high = values.astype(BF16)
    return high, (values - high.astype(F32)).astype(BF16)


def remapped(rows, weights):
    count, width = rows.shape
    high, low = halves(rows)
    if count < 16:
        filler = jnp.zeros((16 - count, width), F32)
        high, low = halves(jnp.concatenate([rows, filler], axis=0))
    left = jnp.concatenate(
        [
            jnp.concatenate([high, high], axis=1),
            jnp.concatenate([low, jnp.zeros(low.shape, BF16)], axis=1),
        ],
        axis=0,
    )
    product = dot(left, weights)
    return product[:count, :] + product[16 : 16 + count, :]


def both_halves(block):
    return jnp.concatenate(halves(block), axis=0)


def weights_kernel(transposed, remap, weights):
    for tile in range(remap.shape[0]):
        block = remap[tile]
        weights[tile] = both_halves(jnp.transpose(block) if transposed else block)


def picked(selection, values):
    chosen = selection.astype(BF16)
    high = values.astype(BF16)
    rest = values - high.astype(F32)
    middle = rest.astype(BF16)
    low = (rest - middle.astype(F32)).astype(BF16)
    return dot(chosen, high) + dot(chosen, middle) + dot(chosen, low)


def placed(values, selection):
    chosen = selection.astype(BF16)
    high = values.astype(BF16)
    rest = values - high.astype(F32)
    middle = rest.astype(BF16)
    low = (rest - middle.astype(F32)).astype(BF16)
    return dot(high, chosen) + dot(middle, chosen) + dot(low, chosen)


def one_hot(labels):
    lanes = lax.broadcasted_iota(jnp.int32, labels.shape, 1).astype(F32)
    return (labels == lanes).astype(F32)


def grid_index(shape):
    return lax.broadcasted_iota(jnp.int32, shape, 0), lax.broadcasted_iota(jnp.int32, shape, 1)


def around(cells, north, south, west, east):
    rows, lanes = grid_index(cells.shape)
    row_count, width = cells.shape
    return (
        jnp.where(rows == 0, north, pltpu.roll(cells, 1, 0)),
        jnp.where(rows == row_count - 1, south, pltpu.roll(cells, row_count - 1, 0)),
        jnp.where(lanes == 0, west, pltpu.roll(cells, 1, 1)),
        jnp.where(lanes == width - 1, east, pltpu.roll(cells, width - 1, 1)),
    )


def diffused(cells, upper, lower, sides, diffusion):
    beside = sides[0] + sides[1] + sides[2] + sides[3] - 4.0 * cells
    return cells + diffusion * beside + 0.1 * (upper + lower - 2.0 * cells)


class Edges:
    def __init__(self, fields, levels, rows, sea_blocks, sea_rows, width):
        self.fields, self.levels, self.rows, self.width = fields, levels, rows, width
        self.sea_blocks, self.sea_rows = sea_blocks, sea_rows
        self.half = fields // 2
        self.part = self.half * levels
        self.ring_rows = -(-self.part // 8) * 8
        self.atmos_rows = 2 * self.part
        self.wet_row = self.atmos_rows + sea_blocks
        self.near_rows = -(-(self.wet_row + 1) // 8) * 8
        self.corner_row = self.atmos_rows
        self.far_rows = -(-(self.atmos_rows + 4) // 8) * 8
        self.sea_tiles = sea_blocks * sea_rows // width
        self.sea_cols = 4 * rows
        self.sea_col_rows = -(-(self.sea_tiles + 1) // 8) * 8
        self.col_rows = self.sea_cols + self.sea_col_rows


def squared(values):
    rows, width = values.shape
    if rows == width:
        return values
    return jnp.concatenate([values, jnp.zeros((width - rows, width), F32)], axis=0)


def chunk(source, target, at, rows, arrival):
    part = pl.ds(pl.multiple_of(at * rows, 8), rows)
    return pltpu.make_async_copy(source.at[part], target.at[part], arrival)


def edges_kernel(
    at, state_far, near_first, near_last, far_first, far_last, first, last, state, arrivals
):
    rows, part, width = at.rows, at.part, at.width
    field_rows = at.levels * rows
    copies = [
        chunk(state_far, state, field, field_rows, arrivals.at[field])
        for field in range(at.fields)
    ]
    for copy in copies:
        copy.start()
    for out in (near_first, near_last, far_first, far_last):
        out[...] = jnp.zeros(out.shape, F32)
    for cols in (first, last):
        cols[pl.ds(at.sea_cols, at.sea_col_rows), :] = jnp.zeros((at.sea_col_rows, width), F32)
    for half in range(2):
        for field in range(half * at.half, (half + 1) * at.half):
            copies[field].wait()
        for row in range(rows):
            lines = state[pl.ds(half * part * rows + row, part, stride=rows), :]
            held = pl.ds(half * at.part, part)
            if row < 2:
                (near_first, far_first)[row][held, :] = lines
            if row >= rows - 2:
                (near_last, far_last)[rows - 1 - row][held, :] = lines
            turned = jnp.transpose(squared(lines))
            near, far = half * rows + row, (2 + half) * rows + row
            first[pl.ds(near, 1), :] = turned[0:1, :]
            first[pl.ds(far, 1), :] = turned[1:2, :]
            last[pl.ds(near, 1), :] = turned[width - 1 : width, :]
            last[pl.ds(far, 1), :] = turned[width - 2 : width - 1, :]


def sea_edges_kernel(at, ocean, wet, near_first, near_last, first, last, *outs):
    width = at.width
    for out, rows in zip(outs, (near_first, near_last, first, last)):
        out[...] = rows[...]
    for out, sea_row in ((outs[0], 0), (outs[1], at.sea_rows - 1)):
        out[pl.ds(at.atmos_rows, at.sea_blocks), :] = ocean[
            pl.ds(sea_row, at.sea_blocks, stride=at.sea_rows), :
        ]
        out[pl.ds(at.wet_row, 1), :] = wet[pl.ds(sea_row, 1), :].astype(F32)
    for tile in range(at.sea_tiles + 1):
        if tile < at.sea_tiles:
            lines = ocean[pl.ds(tile * width, width), :]
        else:
            lines = squared(wet[...].astype(F32))
        turned = jnp.transpose(lines)
        outs[2][pl.ds(at.sea_cols + tile, 1), :] = turned[0:1, :]
        outs[3][pl.ds(at.sea_cols + tile, 1), :] = turned[width - 1 : width, :]


def corners_kernel(at, far_first, far_last, west, east, to_north, to_south):
    for out, lines, row in ((to_north, far_first, 0), (to_south, far_last, at.rows - 1)):
        out[...] = lines[...]
        for place, (cols, half) in enumerate(((west, 0), (west, 1), (east, 0), (east, 1))):
            out[pl.ds(at.corner_row + place, 1), :] = cols[pl.ds(half * at.rows + row, 1), :]


def spread(at, diffusion, part, places):
    numbers = jnp.zeros(places.shape, F32)
    is_first = places < 0
    is_last = places < 0
    for field in range(at.half):
        start = field * at.levels
        numbers = jnp.where(places >= start, diffusion[part * at.half + field], numbers)
        is_first = is_first | (places == start)
        is_last = is_last | (places == start + at.levels - 1)
    return numbers, is_first, is_last


def ring_step(at, part, halos, edges, diffusion, outs):
    north, south, west, east, far_north, far_south = halos
    near_first, near_last, first, last = edges
    rows, width = at.rows, at.width
    shape = (at.ring_rows, width)
    held = pl.ds(part * at.part, shape[0])
    lines, lanes = grid_index(shape)
    numbers, is_first, is_last = spread(at, diffusion, part, lines)
    for out, outside, further, own, is_north in (
        (outs[0], north, far_north, near_first, True),
        (outs[1], south, far_south, near_last, False),
    ):
        turned = jnp.transpose(squared(further[pl.ds(at.corner_row, 8), :]))[: shape[0], :]
        cells, beyond, inside = outside[held, :], further[held, :], own[held, :]
        west_col = jnp.where(lanes == 0, turned[:, part : part + 1], pltpu.roll(cells, 1, 1))
        east_col = jnp.where(
            lanes == width - 1, turned[:, 2 + part : 3 + part], pltpu.roll(cells, width - 1, 1)
        )
        sides = (
            beyond if is_north else inside,
            inside if is_north else beyond,
            west_col,
            east_col,
        )
        upper = jnp.where(is_first, cells, pltpu.roll(cells, 1, 0))
        lower = jnp.where(is_last, cells, pltpu.roll(cells, shape[0] - 1, 0))
        out[...] = diffused(cells, upper, lower, sides, numbers)

    shape = (rows, width)
    near, far = pl.ds(part * rows, rows), pl.ds((2 + part) * rows, rows)
    lines, lanes = grid_index(shape)
    numbers, is_first, is_last = spread(at, diffusion, part, lanes)
    for out, outside, own, corner, is_west in (
        (outs[2], west, first, 0, True),
        (outs[3], east, last, 2, False),
    ):
        cells, beyond, inside = outside[near, :], outside[far, :], own[near, :]
        place = pl.ds(at.corner_row + corner + part, 1)
        sides = (
            jnp.where(lines == 0, far_north[place, :], pltpu.roll(cells, 1, 0)),
            jnp.where(lines == rows - 1, far_south[place, :], pltpu.roll(cells, rows - 1, 0)),
            beyond if is_west else inside,
            inside if is_west else beyond,
        )
        upper = jnp.where(is_first, cells, pltpu.roll(cells, 1, 1))
        lower = jnp.where(is_last, cells, pltpu.roll(cells, width - 1, 1))
        out[...] = diffused(cells, upper, lower, sides, numbers)


def interleaved(at, west, east):
    width = at.width
    fields_each = width // 2 // at.levels
    columns = jnp.concatenate([east, west], axis=1)
    source, target = grid_index((2 * width, width))
    out = []
    for first in range(0, at.half, fields_each):
        block = jnp.where(source < width, source, source - width) - first * at.levels
        lane = 2 * block + jnp.where(source < width, 0, 1)
        out.append(placed(columns, (lane == target).astype(F32)))
    return out


def field_step(at, field, state, out, north, south, first_line, beside, number):
    levels, rows, width = at.levels, at.rows, at.width
    fields_each = width // 2 // levels
    lines, lanes = grid_index((rows, width))
    for level in range(levels):
        line = first_line + field * levels + level
        start = (field * levels + level) * rows
        cells = state[pl.ds(start, rows), :]
        first_level, last_level = level == 0, level == levels - 1
        upper = cells if first_level else state[pl.ds(start - rows, rows), :]
        lower = cells if last_level else state[pl.ds(start + rows, rows), :]
        lane = 2 * ((field % fields_each) * levels + level) + 1
        edge = pltpu.roll(beside[field // fields_each], width - lane, 1)
        sides = (
            jnp.where(lines == 0, north[pl.ds(line, 1), :], pltpu.roll(cells, 1, 0)),
            jnp.where(
                lines == rows - 1, south[pl.ds(line, 1), :], pltpu.roll(cells, rows - 1, 0)
            ),
            jnp.where(lanes == 0, edge, pltpu.roll(cells, 1, 1)),
            jnp.where(lanes == width - 1, edge, pltpu.roll(cells, width - 1, 1)),
        )
        out[pl.ds(start, rows), :] = diffused(cells, upper, lower, sides, number)


def steps_kernel(
    at,
    state_far,
    north,
    south,
    west,
    east,
    far_north,
    far_south,
    near_first,
    near_last,
    first,
    last,
    diffusion,
    tops,
    sea_before,
    out_far,
    sea_out,
    state,
    middle,
    out,
    *rest,
):
    *rings, arrivals, departures, sea_departures = rest
    rows, levels = at.rows, at.levels
    field_rows = levels * rows

    def coming(field):
        return chunk(state_far, state, field, field_rows, arrivals.at[field])

    def going(field):
        return chunk(out, out_far, field, field_rows, departures.at[field])

    for field in range(at.fields):
        coming(field).start()
    stored = [
        pltpu.make_async_copy(
            tops.at[pl.ds(flux * at.sea_rows, at.sea_rows)],
            sea_out.at[flux, 0],
            sea_departures.at[flux],
        )
        for flux in range(sea_out.shape[0])
    ]
    for copy in stored:
        copy.start()
    halos = (north, south, west, east, far_north, far_south)
    for part in range(2):
        ring = rings[4 * part : 4 * part + 4]
        ring_step(at, part, halos, (near_first, near_last, first, last), diffusion, ring)
    for part in range(2):
        ring = rings[4 * part : 4 * part + 4]
        held = pl.ds(part * rows, rows)
        outer = interleaved(at, west[held, :], east[held, :])
        inner = interleaved(at, ring[2][...], ring[3][...])
        cells = pl.ds(part * at.part * rows, at.part * rows)
        parts = [array.at[cells] for array in (state, middle, out)]
        for field in range(at.half):
            whole = part * at.half + field
            number = diffusion[whole]
            coming(whole).wait()
            field_step(
                at, field, parts[0], parts[1], north, south, part * at.part, outer, number
            )
            field_step(at, field, parts[1], parts[2], ring[0], ring[1], 0, inner, number)
            going(whole).start()
    for copy in stored:
        copy.wait()
    for field in range(at.fields):
        going(field).wait()


def ocean_kernel(
    at,
    levels,
    ocean_far,
    wet,
    north,
    south,
    west,
    east,
    mixing,
    out_far,
    tops,
    ocean,
    out,
    wests,
    easts,
    arrivals,
    departures,
):
    fields, field_rows = at.sea_blocks // levels, levels * at.sea_rows
    for field in range(fields):
        chunk(ocean_far, ocean, field, field_rows, arrivals.at[field]).start()
    rows, width = at.sea_rows, at.width
    lines, lanes = grid_index((rows, width))
    per_tile = width // rows
    held = pl.ds(at.sea_cols, at.sea_col_rows)
    wests[...] = jnp.transpose(squared(west[held, :]))
    easts[...] = jnp.transpose(squared(east[held, :]))
    wet_cells = wet[...].astype(F32)
    wet_lane = at.sea_tiles
    wet_sides = around(
        wet_cells,
        north[pl.ds(at.wet_row, 1), :],
        south[pl.ds(at.wet_row, 1), :],
        wests[pl.ds(0, rows), :][:, wet_lane : wet_lane + 1],
        easts[pl.ds(0, rows), :][:, wet_lane : wet_lane + 1],
    )

    def field_step(field, carry):
        chunk(ocean_far, ocean, field, field_rows, arrivals.at[field]).wait()
        back = lax.rem(width - field * (levels // per_tile), width)
        west_cols = pltpu.roll(wests[...], back, 1)
        east_cols = pltpu.roll(easts[...], back, 1)
        number = mixing[field] * wet_cells
        for level in range(levels):
            block = field * levels + level
            start = pl.multiple_of(block * rows, rows)
            first_level, last_level = level == 0, level == levels - 1
            cells = ocean[pl.ds(start, rows), :]
            upper = cells if first_level else ocean[pl.ds(start - rows, rows), :]
            lower = cells if last_level else ocean[pl.ds(start + rows, rows), :]
            above = pltpu.roll(cells, 1, 0)
            below = pltpu.roll(cells, rows - 1, 0)
            line = at.atmos_rows + block
            tile, within = level // per_tile, (level % per_tile) * rows
            west_col = pltpu.roll(west_cols[within : within + rows, :], (width - tile) % width, 1)
            east_col = pltpu.roll(east_cols[within : within + rows, :], width - 1 - tile, 1)
            sides = (
                jnp.where(lines == 0, north[pl.ds(line, 1), :], above),
                jnp.where(lines == rows - 1, south[pl.ds(line, 1), :], below),
                jnp.where(lanes == 0, west_col, pltpu.roll(cells, 1, 1)),
                jnp.where(lanes == width - 1, east_col, pltpu.roll(cells, width - 1, 1)),
            )
            total = wet_sides[0] * (sides[0] - cells)
            for side in range(1, 4):
                total = total + wet_sides[side] * (sides[side] - cells)
            tendency = number * total + 0.1 * (upper + lower - 2.0 * cells)
            after = cells + wet_cells * tendency
            out[pl.ds(start, rows), :] = after
            if first_level:
                tops[pl.ds(pl.multiple_of(field * rows, rows), rows), :] = after
        chunk(out, out_far, field, field_rows, departures.at[field]).start()
        return carry

    lax.fori_loop(0, fields, field_step, 0)
    for field in range(fields):
        chunk(out, out_far, field, field_rows, departures.at[field]).wait()


def label_base(rows):
    return 2.0 * rows


def routes_kernel(index, own, diffusion, *rest):
    *outs, labels_out, section, numbers, tally, piece_labels, sea_labels = rest
    lanes = lax.broadcasted_iota(jnp.int32, (1, section.shape[1]), 1)
    section[...] = jnp.full(section.shape, own[0].astype(F32))
    for field in range(diffusion.shape[0]):
        numbers[pl.ds(field, 1), :] = jnp.full(lanes.shape, diffusion[field])

    def clear(at, carry):
        tally[at] = 0
        return carry

    for row, slots, labels in ((0, outs[0], piece_labels), (2, outs[1], sea_labels)):
        slots[...] = jnp.zeros(slots.shape, F32)
        labels[...] = jnp.full(labels.shape, -1.0, F32)
        lax.fori_loop(0, tally.shape[0], clear, 0)
        for tile in range(index.shape[1]):
            owner = index[row, tile]
            rank = tally[owner]
            tally[owner] = rank + 1
            slot = pl.ds(owner * CAPACITY + rank, 1)
            slots[slot, :] = (lanes == tile).astype(F32)
            labels[slot, :] = jnp.full(lanes.shape, index[row + 1, tile].astype(F32))
    base = label_base(index.shape[1])
    labels_out[...] = (piece_labels[...] + 1.0) + base * (sea_labels[...] + 1.0)


def inner_kernel(at, state_far, numbers, out, top, arrival):
    fields, rows, width = at.fields, at.rows, at.width
    copy = pltpu.make_async_copy(state_far.at[:, pl.ds(at.levels - 2, 2)], top, arrival)
    copy.start()
    lines, lanes = grid_index((rows, width))
    copy.wait()
    for field in range(fields):
        cells = top[field, 1]
        sides = (
            jnp.where(lines == 0, 0.0, pltpu.roll(cells, 1, 0)),
            jnp.where(lines == rows - 1, 0.0, pltpu.roll(cells, rows - 1, 0)),
            jnp.where(lanes == 0, 0.0, pltpu.roll(cells, 1, 1)),
            jnp.where(lanes == width - 1, 0.0, pltpu.roll(cells, width - 1, 1)),
        )
        out[pl.ds(field * rows, rows), :] = diffused(
            cells, top[field, 0], cells, sides, numbers[pl.ds(field, 1), :]
        )


def pieces_kernel(
    at, inner, north, south, west, east, weights, numbers, routes, labels, out, surface, products
):
    fields, levels, rows, width = at.fields, at.levels, at.rows, at.width
    slots = routes.shape[0]
    lines, lanes = grid_index((rows, width))
    a = []
    for field in range(fields):
        part = field // at.half
        held = pl.ds(part * rows, rows)
        lane = (field % at.half) * levels + levels - 1
        line = pl.ds(part * at.part + lane, 1)
        outside = (
            jnp.where(lines == 0, north[line, :], 0.0)
            + jnp.where(lines == rows - 1, south[line, :], 0.0)
            + jnp.where(lanes == 0, pltpu.roll(west[held, :], (width - lane) % width, 1), 0.0)
            + jnp.where(lanes == width - 1, pltpu.roll(east[held, :], width - 1 - lane, 1), 0.0)
        )
        a.append(inner[pl.ds(field * rows, rows), :] + numbers[pl.ds(field, 1), :] * outside)
    sums = (a[0] - a[4], a[1], a[2], a[3], a[6] + a[7], a[5] + a[8], a[9])
    for place in range(16):
        surface[pl.ds(place * rows, rows), :] = (
            sums[place] if place < len(sums) else jnp.zeros((rows, width), F32)
        )
    for tile in range(rows):
        products[pl.ds(tile * 16, 16), :] = remapped(
            surface[pl.ds(tile, 16, stride=rows), :], weights[tile]
        )
    count = PIECE_ROWS - 1
    sent = picked(
        routes[...][:, :rows],
        jnp.concatenate(
            [products[pl.ds(place, rows, stride=16), :] for place in range(count)], axis=1
        ),
    )
    for place in range(count):
        out[pl.ds(place, slots, stride=PIECE_ROWS), :] = sent[:, place * width : (place + 1) * width]
    out[pl.ds(count, slots, stride=PIECE_ROWS), :] = labels[...]


def sea_labels_kernel(rows, arrived, sea_labels):
    labels = arrived[pl.ds(PIECE_ROWS - 1, sea_labels.shape[0], stride=PIECE_ROWS), :]
    sea_labels[...] = jnp.floor(labels * (1.0 / label_base(rows))) - 1.0


def flux_kernel(sizes, arrived, remap, routes, out, gather, fluxes, products):
    flux_count, rows, sections = sizes
    width = out.shape[1]
    slots = routes.shape[0]
    count = PIECE_ROWS - 1
    labels = arrived[pl.ds(count, slots, stride=PIECE_ROWS), :]
    upper = jnp.floor(labels * (1.0 / label_base(rows)))
    select = one_hot(labels - label_base(rows) * upper - 1.0)
    gather[...] = select
    values = jnp.concatenate(
        [arrived[pl.ds(place, slots, stride=PIECE_ROWS), :] for place in range(count)], axis=1
    )
    exchange = picked(jnp.transpose(select)[:rows, :], values)
    a04, a1, a2, a3, a67, a58, a9 = (
        exchange[:, place * width : (place + 1) * width] for place in range(count)
    )
    speed = jnp.sqrt(a2 * a2 + a3 * a3 + 0.5)
    fluxes[pl.ds(0, rows), :] = speed * a04 + a67
    fluxes[pl.ds(rows, rows), :] = speed * a1 + a58
    fluxes[pl.ds(2 * rows, rows), :] = speed * a2 * (1.0 + 0.2 * jnp.tanh(a9))
    fluxes[pl.ds(3 * rows, rows), :] = speed * a3
    for tile in range(rows):
        products[pl.ds(tile * flux_count, flux_count), :] = remapped(
            fluxes[pl.ds(tile, flux_count, stride=rows), :], both_halves(remap[tile])
        )
    sent = picked(
        routes[...][:, :rows],
        jnp.concatenate(
            [products[pl.ds(flux, rows, stride=flux_count), :] for flux in range(flux_count)],
            axis=1,
        ),
    )
    for flux in range(flux_count):
        for section in range(sections):
            out[pl.ds(section * slots * flux_count + flux, slots, stride=flux_count), :] = sent[
                :, flux * width : (flux + 1) * width
            ]


def sea_kernel(
    sizes, landed, base_tops, wet, own_labels, other_labels, section, tops, answers
):
    flux_count, sea_rows = sizes
    width = landed.shape[1]
    slots = own_labels.shape[0]
    mine = one_hot(own_labels[...])
    others = one_hot(other_labels[...])
    is_first = section[0:1, :] == 0.0
    select = jnp.concatenate(
        [jnp.where(is_first, mine, others), jnp.where(is_first, others, mine)], axis=0
    )
    values = jnp.concatenate(
        [landed[pl.ds(flux, 2 * slots, stride=flux_count), :] for flux in range(flux_count)], axis=1
    )
    forcing = picked(jnp.transpose(select)[:sea_rows, :], values)
    wet_cells = wet[...].astype(F32)
    for flux in range(flux_count):
        held = pl.ds(flux * sea_rows, sea_rows)
        tops[held, :] = base_tops[held, :] + wet_cells * (
            FORCING_SCALE[flux] * forcing[:, flux * width : (flux + 1) * width]
        )
    all_tops = jnp.concatenate(
        [tops[pl.ds(flux * sea_rows, sea_rows), :] for flux in range(flux_count)], axis=1
    )
    reply = picked(mine[:, :sea_rows], all_tops)
    for flux in range(flux_count):
        answers[pl.ds(flux, slots, stride=flux_count), :] = reply[
            :, flux * width : (flux + 1) * width
        ]


def tops_of_tiles(returned, routes, flux_count, scratch):
    slots, width = routes.shape
    rows = scratch.shape[0] // flux_count
    found = picked(
        jnp.transpose(routes[...])[:rows, :],
        jnp.concatenate(
            [returned[pl.ds(flux, slots, stride=flux_count), :] for flux in range(flux_count)],
            axis=1,
        ),
    )
    for flux in range(flux_count):
        scratch[pl.ds(flux, rows, stride=flux_count), :] = found[
            :, flux * width : (flux + 1) * width
        ]


def reply_kernel(flux_count, answered, remap, routes, gather, out, tops, on_exchange):
    slots, width = routes.shape
    rows = remap.shape[0]
    tops_of_tiles(answered, routes, flux_count, tops)
    for tile in range(rows):
        held = pl.ds(tile * flux_count, flux_count)
        on_exchange[held, :] = remapped(
            tops[held, :], both_halves(jnp.transpose(remap[tile]))
        )
    values = jnp.concatenate(
        [on_exchange[pl.ds(flux, rows, stride=flux_count), :] for flux in range(flux_count)], axis=1
    )
    replies = picked(gather[...][:, :rows], values)
    for flux in range(flux_count):
        out[pl.ds(flux, slots, stride=flux_count), :] = replies[
            :, flux * width : (flux + 1) * width
        ]


def surface_kernel(flux_count, returned, weights, routes, out, tops):
    rows = weights.shape[0]
    tops_of_tiles(returned, routes, flux_count, tops)
    for tile in range(rows):
        out[pl.ds(tile, flux_count, stride=rows), :] = remapped(
            tops[pl.ds(tile * flux_count, flux_count), :], weights[tile]
        )


VMEM = pl.BlockSpec(memory_space=pltpu.VMEM)
SMEM = pl.BlockSpec(memory_space=pltpu.SMEM)
ANY = pl.BlockSpec(memory_space=pl.ANY)


def array(*shape):
    return jax.ShapeDtypeStruct(shape, F32)


def call(kernel, name, outs, in_specs, scratch=(), after=(), limit=VMEM_LIMIT, work=1_000_000, **more):
    def body(*refs):
        kernel(*refs[: len(in_specs)], *refs[len(in_specs) + len(after) :])

    run = pl.pallas_call(
        body,
        name=name,
        out_shape=outs,
        in_specs=list(in_specs) + [ANY] * len(after),
        scratch_shapes=list(scratch),
        compiler_params=pltpu.CompilerParams(vmem_limit_bytes=limit),
        cost_estimate=pl.CostEstimate(flops=0, bytes_accessed=work, transcendentals=0),
        **more,
    )
    return lambda *arguments: run(*arguments, *after)


def gated(values, before):
    return lax.optimization_barrier((values, before))[0]


def on_device(
    atmos_state,
    atmos_diffusion,
    remap_atmos,
    exchange_owner,
    exchange_slot,
    remap_ocean,
    ocean_owner,
    ocean_slot,
    ocean_state,
    ocean_mixing,
    wet_mask,
):
    targets = lax.axis_size(SECTION)
    sections = lax.axis_size("comp")
    devices = targets * sections
    fields, levels, rows, width = atmos_state.shape
    sea_fields, sea_levels, sea_rows, _ = ocean_state.shape
    blocks = fields * levels
    sea_blocks = sea_fields * sea_levels
    at = Edges(fields, levels, rows, sea_blocks, sea_rows, width)
    slots = targets * CAPACITY
    ring = ("comp", "gx")

    index = jnp.stack([exchange_owner[:, 0], exchange_slot, ocean_owner[:, 0], ocean_slot])
    section = lax.axis_index("comp").astype(jnp.int32).reshape(1)
    state = atmos_state.reshape(blocks * rows, width)
    ocean = ocean_state.reshape(sea_blocks * sea_rows, width)

    state_copy = pltpu.VMEM((blocks * rows, width), F32)
    ocean_copy = pltpu.VMEM((sea_blocks * sea_rows, width), F32)
    ocean_flags = pltpu.SemaphoreType.DMA((sea_fields,))
    near_first, near_last, far_first, far_last, first_cols, last_cols = call(
        functools.partial(edges_kernel, at),
        "edges",
        (array(at.near_rows, width),) * 2
        + (array(at.far_rows, width),) * 2
        + (array(at.col_rows, width),) * 2,
        [ANY],
        [state_copy, pltpu.SemaphoreType.DMA((fields,))],
        limit=EDGES_LIMIT,
    )(state)
    near_first, near_last, first_cols, last_cols = call(
        functools.partial(sea_edges_kernel, at),
        "sea_edges",
        (array(at.near_rows, width),) * 2 + (array(at.col_rows, width),) * 2,
        [VMEM] * 6,
    )(ocean, wet_mask, near_first, near_last, first_cols, last_cols)
    north = shifted(near_last, ring, 1)
    south = shifted(near_first, ring, -1)
    west = shifted(last_cols, "gy", 1)
    east = shifted(first_cols, "gy", -1)

    def weights_of(remap, transposed, name, before):
        return call(
            functools.partial(weights_kernel, transposed),
            name,
            jax.ShapeDtypeStruct((rows, 2 * width, width), BF16),
            [VMEM],
        )(gated(remap, before))

    tile_slots, sea_slots, labels, here, numbers = call(
        routes_kernel,
        "routes",
        (array(slots, width),) * 3 + (array(8, width), array(-(-fields // 8) * 8, width)),
        [SMEM] * 3,
        [pltpu.SMEM((targets,), jnp.int32)] + [pltpu.VMEM((slots, width), F32)] * 2,
    )(gated(index, first_cols), section, atmos_diffusion)
    inner = call(
        functools.partial(inner_kernel, at),
        "inner",
        array(fields * rows, width),
        [ANY, VMEM],
        [pltpu.VMEM((fields, 2, rows, width), F32), pltpu.SemaphoreType.DMA],
    )(gated(atmos_state, first_cols), numbers)
    pieces = call(
        functools.partial(pieces_kernel, at),
        "pieces",
        array(slots * PIECE_ROWS, width),
        [VMEM] * 9,
        [pltpu.VMEM((16 * rows, width), F32)] * 2,
    )(
        inner,
        north,
        south,
        west,
        east,
        weights_of(remap_atmos, False, "piece_weights", first_cols),
        numbers,
        tile_slots,
        labels,
    )
    arrived = lax.all_to_all(
        pieces.reshape(targets, CAPACITY * PIECE_ROWS, width), SECTION, 0, 0, tiled=True
    )
    to_north, to_south = call(
        functools.partial(corners_kernel, at),
        "corners",
        (array(at.far_rows, width),) * 2,
        [VMEM] * 4,
        after=(pieces,),
    )(far_first, far_last, west, east)
    far_north = shifted(to_south, ring, 1)
    far_south = shifted(to_north, ring, -1)

    sea_base, base_tops = call(
        functools.partial(ocean_kernel, at, sea_levels),
        "sea_base",
        (array(sea_blocks * sea_rows, width), array(sea_fields * sea_rows, width)),
        [ANY] + [VMEM] * 5 + [SMEM],
        [ocean_copy] * 2 + [pltpu.VMEM((width, width), F32)] * 2 + [ocean_flags] * 2,
        after=(pieces,),
        limit=SEA_LIMIT,
        work=1_000_000_000,
        out_specs=(ANY, VMEM),
    )(ocean, wet_mask, north, south, west, east, ocean_mixing)

    arrived, sea_base, far_north, far_south = lax.optimization_barrier(
        (arrived, sea_base, far_north, far_south)
    )
    arrived = arrived.reshape(slots * PIECE_ROWS, width)
    own_labels = call(
        functools.partial(sea_labels_kernel, rows), "sea_labels", array(slots, width), [VMEM]
    )(arrived)
    other_labels = shifted(own_labels, "comp", 1)
    outgoing, gather = call(
        functools.partial(flux_kernel, (sea_fields, rows, sections)),
        "fluxes",
        (array(sections * slots * sea_fields, width), array(slots, width)),
        [VMEM] * 3,
        [pltpu.VMEM((sea_fields * rows, width), F32)] * 2,
    )(arrived, remap_ocean, sea_slots)
    outgoing, other_labels = lax.optimization_barrier((outgoing, other_labels))
    landed = lax.all_to_all(
        outgoing.reshape(devices, CAPACITY * sea_fields, width), EVERY, 0, 0, tiled=True
    )
    tops, answers = call(
        functools.partial(sea_kernel, (sea_fields, sea_rows)),
        "sea_top",
        (array(sea_fields * sea_rows, width), array(slots * sea_fields, width)),
        [VMEM] * 6,
    )(
        landed.reshape(devices * CAPACITY * sea_fields, width),
        base_tops,
        wet_mask,
        own_labels,
        other_labels,
        here,
    )
    answered = lax.all_to_all(
        answers.reshape(targets, CAPACITY * sea_fields, width), SECTION, 0, 0, tiled=True
    )
    replies = call(
        functools.partial(reply_kernel, sea_fields),
        "replies",
        array(slots * sea_fields, width),
        [VMEM] * 4,
        [pltpu.VMEM((sea_fields * rows, width), F32)] * 2,
    )(answered.reshape(slots * sea_fields, width), remap_ocean, sea_slots, gather)
    returned = lax.all_to_all(
        replies.reshape(targets, CAPACITY * sea_fields, width), SECTION, 0, 0, tiled=True
    )
    atmos_next, ocean_next = call(
        functools.partial(steps_kernel, at),
        "steps",
        (array(blocks * rows, width), array(sea_fields, sea_levels, sea_rows, width)),
        [ANY] + [VMEM] * 10 + [SMEM, ANY, ANY],
        [state_copy] * 3
        + (
            [pltpu.VMEM((at.ring_rows, width), F32)] * 2 + [pltpu.VMEM((rows, width), F32)] * 2
        )
        * 2
        + [pltpu.SemaphoreType.DMA((fields,))] * 2
        + [ocean_flags],
        after=(replies,),
        limit=STEPS_LIMIT,
        work=1_000_000_000,
        out_specs=(ANY, ANY),
        input_output_aliases={13: 1},
    )(
        state,
        north,
        south,
        west,
        east,
        far_north,
        far_south,
        near_first,
        near_last,
        first_cols,
        last_cols,
        atmos_diffusion,
        tops,
        sea_base.reshape(sea_fields, sea_levels, sea_rows, width),
    )
    ocean_surface = call(
        functools.partial(surface_kernel, sea_fields),
        "surface",
        array(sea_fields * rows, width),
        [VMEM] * 3,
        [pltpu.VMEM((sea_fields * rows, width), F32)],
    )(
        returned.reshape(slots * sea_fields, width),
        weights_of(remap_atmos, True, "surface_weights", replies),
        tile_slots,
    )
    return (
        atmos_next.reshape(atmos_state.shape),
        ocean_next,
        ocean_surface.reshape(sea_fields, rows, width),
    )


def solution(mesh):
    in_specs = (
        P(None, None, ("comp", "gx"), "gy"),
        P(),
        P(("comp", "gx", "gy"), None, None),
        P(("comp", "gx", "gy"), None),
        P(("comp", "gx", "gy")),
        P(("comp", "gx", "gy"), None, None),
        P(("comp", "gx", "gy"), None),
        P(("comp", "gx", "gy")),
        P(None, None, "gx", "gy"),
        P(),
        P("gx", "gy"),
    )
    out_specs = (
        P(None, None, ("comp", "gx"), "gy"),
        P(None, None, "gx", "gy"),
        P(None, ("comp", "gx"), "gy"),
    )
    return jax.shard_map(
        on_device, mesh=mesh, in_specs=in_specs, out_specs=out_specs, check_vma=False
    )
```
